32 devices in a mesh: section: 4 (over x, core), expert: 8 (over z, y).
Axes of the slice: x: 2, y: 2, z: 4, core: 2. Of those that a mesh axis runs over, the one named last changes fastest.
Arguments:
- hidden_in: bfloat16 [4, 32, 4096], P('section', 'expert'), may hold values from -4 to 4
- attn_gain: bfloat16 [4, 4096], P('section'), may hold values from 0.5 to 2
- w_query: bfloat16 [4, 4096, 4096], P('section', None, 'expert'), may hold values from -0.09375 to 0.09375
- w_out: bfloat16 [4, 4096, 4096], P('section', None, 'expert'), may hold values from -0.09375 to 0.09375
- key_cache: bfloat16 [4, 3, 32, 64, 4, 128], P('section', None, 'expert'), may hold values from -2 to 2
- value_cache: bfloat16 [4, 3, 32, 64, 4, 128], P('section', None, 'expert'), may hold values from -6 to 6
- lengths: int32 [4, 3, 32], P('section', None, 'expert'), may hold values from 1 to 64, 1024 in all within a row
- ffn_gain: bfloat16 [4, 4096], P('section'), may hold values from 0.5 to 2
- w_gate: bfloat16 [4, 8, 4096, 384], P('section', 'expert'), may hold values from -0.09375 to 0.09375
- w_up: bfloat16 [4, 8, 4096, 384], P('section', 'expert'), may hold values from -0.09375 to 0.09375
- w_down: bfloat16 [4, 8, 384, 4096], P('section', 'expert'), may hold values from -0.21875 to 0.21875
- routes: int32 [4, 3, 32, 2], P('section', None, 'expert'), may hold values from 0 to 3, all different within a row; in each aligned block of 4 rows (0 to 3, 4 to 7, ..., all dimensions but the last counted through in order) at most 4 rows name the same one
- gates: float32 [4, 3, 32, 2], P('section', None, 'expert'), may hold values from 0.1 to 1
Outputs:
- out: bfloat16 [4, 32, 4096], P('section', 'expert')
The draws below stay inside these ranges and needn't reach their ends.
Inputs may be any that keep to these rules, and one draw needn't show every extreme that they name: `routes`: each row names 2 different experts of the 4; among the 4 rows that one index of the expert axis holds at one section and step, an expert is named by at most 4 rows.
All inputs are finite; a program needn't handle non-finite values. No bound on the sum of `lengths` on one device may be relied on, other than what follows from the above.
Results may differ from the reference program's by a relative error of at most 0.04.
Values may be sent and summed in bfloat16 or wider, within the bound.
No kernel may reach another device: no remote copies, remote signals or barrier semaphores. Data moves between devices by JAX's collectives and lax.ppermute only.
A program may use at most 64 MiB of HBM per device.

```python
import math
import jax
import jax.numpy as jnp
import numpy as np
from jax import lax

D = 4096
HD = 128
HQ = 32
KVH = 4
FFE = 768
FFD = 384
ROWS_DEV = 4
CACHE = 64
STEPS = 3
SECTIONS = 4
EXPERTS = 4
TOPK = 2
ROWS = 32


def draw_hidden_in(key, part):
    base_key, row_key, col_key = jax.random.split(key, 3)
    full_shape = (SECTIONS, ROWS, D)
    base_values = jnp.clip(jax.random.normal(base_key, full_shape, jnp.float32), -4.0, 4.0)
    log_low = math.log(0.1)
    row_scale = jnp.exp(jax.random.uniform(row_key, (SECTIONS, ROWS, 1), jnp.float32, log_low, 0.0))
    col_scale = jnp.exp(jax.random.uniform(col_key, (1, 1, D), jnp.float32, log_low, 0.0))
    return (base_values * row_scale * col_scale).astype(jnp.bfloat16)


def levels(key, shape, pieces, low, high):
    factor_of = 1.0
    for dim, blocks in pieces:
        steps = jax.random.uniform(jax.random.fold_in(jax.random.fold_in(key, 6), dim), (blocks,), jnp.float32, low / len(pieces), high / len(pieces))
        factor_of = factor_of * jnp.repeat(jnp.exp(steps), shape[dim] // blocks).reshape((-1,) + (1,) * (len(shape) - 1 - dim))
    return factor_of


def profile(number_of, total, bound, skew):
    portions = [(1 << 20) // math.isqrt(standing ** skew) + 1 for standing in range(2, number_of + 1)]
    rest, holding = total - bound - (number_of - 1), [1] * (number_of - 1)
    while rest > 0:
        free = [i for i in range(number_of - 1) if holding[i] < bound]
        pool, left = sum([portions[i] for i in free]), rest
        for i in free:
            extra = min(bound - holding[i], max(1, left * portions[i] // pool), rest)
            holding[i] = holding[i] + extra
            rest = rest - extra
    return np.array([bound] + holding)


def ragged(stream_key, amount, total, bound, lean):
    if amount == 2:
        one = jax.random.randint(stream_key, (), max(1, total - bound), min(bound, total - 1) + 1)
        return jnp.stack([one, total - one])
    tallies = jnp.asarray(profile(amount, total, bound, lean), jnp.int32)
    twos = (amount - 1) // 2
    giver, taker = tallies[1:1 + 2 * twos:2], tallies[2:2 + 2 * twos:2]
    slack = jnp.minimum(giver - 1, bound - taker)
    passed = jax.random.randint(jax.random.fold_in(stream_key, 1), (twos,), 0, 1 << 20) % (slack + 1)
    tallies = tallies.at[1:1 + 2 * twos:2].set(giver - passed).at[2:2 + 2 * twos:2].set(taker + passed)
    return tallies[jax.random.permutation(jax.random.fold_in(stream_key, 2), amount)]


def routed_block(rng, own, number, rows, number_of, top, bound, slope):
    sequence = jax.random.permutation(rng, number_of)
    heavy_load, usual = portions_of(number_of, rows * top, bound, slope, True), portions_of(number_of, rows * top, bound, slope, False)
    places = jnp.arange(number_of)

    def named(sizes, offset_by):
        used = int((sizes > 0).sum())
        fixed = max(1, used // 4)
        passed = fixed + (places - fixed + offset_by * (used - fixed)) % max(1, number_of - fixed)
        return jnp.zeros((number_of,), jnp.int32).at[sequence[jnp.where(places < fixed, places, passed)]].set(jnp.asarray(sizes, jnp.int32))

    sizes = jnp.where(number % 4 == 0, named(heavy_load, number // 4), named(usual, number - number // 4 - 1))
    mixed = jax.random.permutation(jax.random.fold_in(own, 3), number_of)
    giver, taker = mixed[0:number_of // 2 * 2:2], mixed[1:number_of // 2 * 2:2]
    slack = jnp.minimum(sizes[giver] - 1, bound - sizes[taker]) // 2
    slack = jnp.where((giver == sequence[0]) | (taker == sequence[0]) | (sizes[taker] == 0), 0, jnp.maximum(slack, 0))
    passed = jax.random.randint(jax.random.fold_in(own, 4), (number_of // 2,), 0, 1 << 20) % (slack + 1)
    sizes = sizes.at[giver].add(-passed).at[taker].add(passed)
    labels = jnp.searchsorted(jnp.cumsum(sizes), jnp.arange(rows * top), side="right").astype(jnp.int32)
    grid = labels.reshape(top, rows).T
    grid = grid[jax.random.permutation(jax.random.fold_in(own, 1), rows)]
    offset_by = jax.random.randint(jax.random.fold_in(own, 2), (rows, 1), 0, top)
    return jnp.take_along_axis(grid, (jnp.arange(top)[None, :] + offset_by) % top, axis=1)


def portions_of(number_of, total, reach, lean, full):
    loads = [(1 << 20) // math.isqrt(grade ** lean) + 1 for grade in range(1, number_of + 1)]
    largest = reach if full else min(reach, max(-(-total // number_of), total * loads[0] // sum(loads)))
    least = 1 if total - largest >= number_of - 1 else 0
    counts, rest = [largest] + [least] * (number_of - 1), total - largest - least * (number_of - 1)
    while rest > 0:
        free = [i for i in range(1, number_of) if counts[i] < largest] or [i for i in range(1, number_of) if counts[i] < reach]
        mass, left = sum([loads[i] for i in free]), rest
        for i in free:
            addition = min(reach - counts[i], max(1, left * loads[i] // mass), rest)
            counts[i] = counts[i] + addition
            rest = rest - addition
    return np.array(counts)


def scatter_about(stream_key, dims, width, bound, cuts=(), kind=jnp.bfloat16):
    entries = jax.random.normal(stream_key, dims, jnp.float32) * width
    if len(cuts) > 0:
        entries = levels(stream_key, dims, cuts, -0.22, 0.18) * entries
    return jnp.clip(entries, min=-bound, max=bound).astype(kind)


def setup_inputs(seed: int = 0) -> dict:
    arg_keys = jax.random.split(jax.random.key(seed), 14)
    hidden_in = draw_hidden_in(jax.random.fold_in(arg_keys[13], 71), 0)
    attn_gain = jnp.clip(jnp.exp(math.log(2.0) - 1.3862944 * jax.random.uniform(arg_keys[1], (SECTIONS, D), jnp.float32) ** levels(arg_keys[1], (SECTIONS, D), ((0, 4),), -0.2, 0.2)), 0.5, 2.0).astype(jnp.bfloat16)
    w_query = scatter_about(arg_keys[2], (SECTIONS, D, HQ * HD), D ** -0.5, 0.09375, ((0, 4), (2, 8)))
    w_out = scatter_about(arg_keys[3], (SECTIONS, HQ * HD, D), (HQ * HD) ** -0.5, 0.09375, ((0, 4), (2, 8)))
    key_cache = jnp.clip(jax.random.uniform(arg_keys[4], (SECTIONS, STEPS, ROWS, CACHE, KVH, HD), jnp.float32, -2.0, 2.0) * levels(arg_keys[4], (SECTIONS, STEPS, ROWS, CACHE, KVH, HD), ((0, 4), (2, 8)), -0.4, 0.0), -2.0, 2.0).astype(jnp.bfloat16)
    value_cache = scatter_about(arg_keys[5], (SECTIONS, STEPS, ROWS, CACHE, KVH, HD), 1.0, 6.0, ((0, 4), (2, 8)))
    lengths = jax.vmap(lambda own: ragged(own, ROWS, ROWS * CACHE // 2, CACHE, 2))(jax.random.split(arg_keys[6], SECTIONS * STEPS)).reshape((SECTIONS, STEPS, ROWS)).astype(jnp.int32)
    ffn_gain = jnp.clip(jnp.exp(math.log(2.0) - 1.3862944 * jax.random.uniform(arg_keys[7], (SECTIONS, D), jnp.float32) ** levels(arg_keys[7], (SECTIONS, D), ((0, 4),), -0.2, 0.2)), 0.5, 2.0).astype(jnp.bfloat16)
    w_gate = scatter_about(arg_keys[8], (SECTIONS, 2 * EXPERTS, D, FFD), D ** -0.5, 0.09375, ((0, 4), (1, 8)))
    w_up = scatter_about(arg_keys[9], (SECTIONS, 2 * EXPERTS, D, FFD), D ** -0.5, 0.09375, ((0, 4), (1, 8)))
    w_down = scatter_about(arg_keys[10], (SECTIONS, 2 * EXPERTS, FFD, D), FFE ** -0.5, 0.21875, ((0, 4), (1, 8)))
    routes_keys = jax.random.split(jax.random.fold_in(arg_keys[11], 1), SECTIONS * STEPS * ROWS // ROWS_DEV)
    routes_turns = jax.random.permutation(jax.random.fold_in(arg_keys[11], 3), SECTIONS * STEPS * ROWS // ROWS_DEV)
    routes = jax.vmap(lambda own, number: routed_block(jax.random.fold_in(arg_keys[11], 2), own, number, ROWS_DEV, EXPERTS, TOPK, ROWS_DEV, 2))(routes_keys, routes_turns).reshape((SECTIONS, STEPS, ROWS, TOPK))
    gates = jnp.clip(jnp.exp(math.log(1.0) - 2.3025851 * jax.random.uniform(arg_keys[12], (SECTIONS, STEPS, ROWS, TOPK), jnp.float32) ** levels(arg_keys[12], (SECTIONS, STEPS, ROWS, TOPK), ((0, 4), (2, 8)), -0.2, 0.2)), 0.1, 1.0)
    return {"hidden_in": hidden_in, "attn_gain": attn_gain, "w_query": w_query, "w_out": w_out, "key_cache": key_cache, "value_cache": value_cache, "lengths": lengths, "ffn_gain": ffn_gain, "w_gate": w_gate, "w_up": w_up, "w_down": w_down, "routes": routes, "gates": gates}


def rms_scaled(values):
    return values * lax.rsqrt(lax.optimization_barrier(jnp.mean(values * values, axis=-1, keepdims=True)) + 1e-06)

def one_layer(hidden_state, gain_attn, query_w, out_w, cache_keys, cache_values, row_lengths, gain_ffn, gate_w, up_w, down_w, route_ids, gate_vals):
    state32 = hidden_state.astype(jnp.float32)
    normed = (rms_scaled(state32) * gain_attn.astype(jnp.float32)).astype(jnp.bfloat16)
    queries = jnp.dot(normed, query_w, preferred_element_type=jnp.float32).reshape(ROWS, HQ, HD)
    q_normed = rms_scaled(queries).astype(jnp.bfloat16).reshape(ROWS, KVH, HQ // KVH, HD)
    scores = jnp.einsum('mkgd,mpkd->mkgp', q_normed.astype(jnp.float32), cache_keys.astype(jnp.float32)) * HD ** (-0.5)
    in_cache = jnp.arange(CACHE, dtype=jnp.int32)[None, :] < row_lengths[:, None]
    exp_scores = jnp.where(in_cache[:, None, None, :], jnp.exp(scores), 0.0)
    weights = (exp_scores / lax.optimization_barrier(jnp.sum(exp_scores, axis=-1, keepdims=True))).astype(jnp.bfloat16)
    context = jnp.einsum('mkgp,mpkd->mkgd', weights.astype(jnp.float32), cache_values.astype(jnp.float32))
    context = context.astype(jnp.bfloat16).reshape(ROWS, HQ * HD)
    middle = state32 + jnp.dot(context, out_w, preferred_element_type=jnp.float32)
    ffn_in = (rms_scaled(middle) * gain_ffn.astype(jnp.float32)).astype(jnp.bfloat16)
    shares = gate_vals / lax.optimization_barrier(jnp.sum(gate_vals, axis=-1, keepdims=True))
    chosen = route_ids[:, :, None] == jnp.arange(EXPERTS, dtype=jnp.int32)[None, None, :]
    coeffs = lax.optimization_barrier(jnp.sum(jnp.where(chosen, shares[:, :, None], 0.0), axis=1))

    def half_expert(weights_half):
        gate_half, up_half, down_half = weights_half
        gate_val = jnp.dot(ffn_in, gate_half, preferred_element_type=jnp.float32)
        up_val = jnp.dot(ffn_in, up_half, preferred_element_type=jnp.float32)
        active = (jax.nn.silu(gate_val) * up_val).astype(jnp.bfloat16)
        return jnp.dot(active, down_half, preferred_element_type=jnp.float32).astype(jnp.bfloat16)
    halves = lax.map(half_expert, (gate_w, up_w, down_w))
    paired = lax.optimization_barrier(jnp.sum(halves.astype(jnp.float32).reshape(EXPERTS, 2, ROWS, D), axis=1)).astype(jnp.bfloat16)
    paired = lax.optimization_barrier(paired).astype(jnp.float32)
    expert_sum = jnp.einsum('me,emd->md', coeffs, paired, precision=lax.Precision.HIGHEST)
    return (middle + expert_sum).astype(jnp.bfloat16)

def reference(hidden_in, attn_gain, w_query, w_out, key_cache, value_cache, lengths, ffn_gain, w_gate, w_up, w_down, routes, gates):
    states = hidden_in

    def apply_section(packed):
        return one_layer(packed[12], packed[0], packed[1], packed[2], packed[7], packed[8], packed[9], packed[3], packed[4], packed[5], packed[6], packed[10], packed[11])
    for layer_step in range(STEPS):
        results = lax.map(apply_section, (attn_gain, w_query, w_out, ffn_gain, w_gate, w_up, w_down, key_cache[:, layer_step], value_cache[:, layer_step], lengths[:, layer_step], routes[:, layer_step], gates[:, layer_step], states))
        if layer_step + 1 < STEPS:
            states = jnp.roll(results, 1, axis=0)
        else:
            states = results
    return states
```

```python
import jax
import jax.numpy as jnp
from jax import lax
from jax.sharding import PartitionSpec as P

STEPS = 3


def passed_along(array, axis, by):
    length = lax.axis_size(axis)
    return lax.ppermute(array, axis, [(i, (i + by) % length) for i in range(length)])


def everyones(array):
    devices = lax.axis_size("expert")
    copies = jnp.broadcast_to(array[None], (devices,) + array.shape)
    return lax.all_to_all(copies, "expert", split_axis=0, concat_axis=0, tiled=True)


def rms_scaled(values):
    return values * lax.rsqrt(jnp.mean(values * values, axis=-1, keepdims=True) + 1e-06)


def coefficients(route_ids, gate_vals, experts):
    shares = gate_vals / jnp.sum(gate_vals, axis=-1, keepdims=True)
    chosen = route_ids[:, :, None] == jnp.arange(experts, dtype=jnp.int32)[None, None, :]
    return jnp.sum(jnp.where(chosen, shares[:, :, None], 0.0), axis=1)


def body(
    hidden_in,
    attn_gain,
    w_query,
    w_out,
    key_cache,
    value_cache,
    lengths,
    ffn_gain,
    w_gate,
    w_up,
    w_down,
    routes,
    gates,
):
    devices = lax.axis_size("expert")
    me = lax.axis_index("expert")
    experts = devices // 2
    row_count = hidden_in.shape[1]
    all_rows = row_count * devices
    model_width = hidden_in.shape[2]
    head_dim = key_cache.shape[-1]
    kv_heads = key_cache.shape[-2]
    cache_len = key_cache.shape[-3]
    query_w = w_query[0]
    out_w = w_out[0]
    local_heads = query_w.shape[1] // head_dim
    all_heads = local_heads * devices
    group_size = all_heads // kv_heads
    gate_w = w_gate[0, 0]
    up_w = w_up[0, 0]
    down_w = w_down[0, 0]
    gain_attn = attn_gain[0].astype(jnp.float32)
    gain_ffn = ffn_gain[0].astype(jnp.float32)
    hidden_state = hidden_in[0]
    for layer_step in range(STEPS):
        states = everyones(hidden_state).reshape(all_rows, model_width)
        states32 = states.astype(jnp.float32)
        normed = (rms_scaled(states32) * gain_attn).astype(jnp.bfloat16)
        raw_query = lax.optimization_barrier(
            jnp.dot(normed, query_w, preferred_element_type=jnp.float32)
        )
        heads_view = raw_query.reshape(all_rows, local_heads, head_dim)
        own_q = rms_scaled(heads_view).astype(jnp.bfloat16).reshape(all_rows, local_heads * head_dim)
        queries = lax.all_to_all(own_q, "expert", split_axis=0, concat_axis=1, tiled=True)
        queries = queries.reshape(row_count, kv_heads, group_size, head_dim)
        scores = jnp.einsum(
            "rkgd,rpkd->rkgp", queries, key_cache[0, layer_step], preferred_element_type=jnp.float32
        ) * head_dim ** (-0.5)
        in_cache = jnp.arange(cache_len, dtype=jnp.int32)[None, :] < lengths[0, layer_step][:, None]
        exp_scores = jnp.where(in_cache[:, None, None, :], jnp.exp(scores), 0.0)
        weights = (exp_scores / jnp.sum(exp_scores, axis=-1, keepdims=True)).astype(jnp.bfloat16)
        context = jnp.einsum(
            "rkgp,rpkd->rkgd",
            weights,
            value_cache[0, layer_step],
            preferred_element_type=jnp.float32,
        )
        context = context.astype(jnp.bfloat16).reshape(row_count, all_heads * head_dim)
        out_cols = jnp.dot(
            everyones(context).reshape(all_rows, all_heads * head_dim),
            out_w,
            preferred_element_type=jnp.float32,
        ).astype(jnp.bfloat16)
        attended = everyones(out_cols).transpose(1, 0, 2).reshape(all_rows, model_width)
        middle = states32 + attended.astype(jnp.float32)
        ffn_in = (rms_scaled(middle) * gain_ffn).astype(jnp.bfloat16)
        gate_val = jnp.dot(ffn_in, gate_w, preferred_element_type=jnp.float32)
        up_val = jnp.dot(ffn_in, up_w, preferred_element_type=jnp.float32)
        active = (jax.nn.silu(gate_val) * up_val).astype(jnp.bfloat16)
        half_out = jnp.dot(active, down_w, preferred_element_type=jnp.float32).astype(jnp.bfloat16)
        returned = lax.all_to_all(half_out, "expert", split_axis=0, concat_axis=0, tiled=True)
        paired_out = jnp.sum(
            returned.astype(jnp.float32).reshape(experts, 2, row_count, model_width), axis=1
        ).astype(jnp.bfloat16)
        coeffs = coefficients(routes[0, layer_step], gates[0, layer_step], experts)
        combined = lax.optimization_barrier(paired_out).astype(jnp.float32)
        expert_sum = jnp.sum(coeffs.T[:, :, None] * combined, axis=0)
        own_middle = lax.dynamic_slice_in_dim(middle, me * row_count, row_count, 0)
        result = (own_middle + expert_sum).astype(jnp.bfloat16)
        if layer_step + 1 < STEPS:
            hidden_state = passed_along(result, "section", 1)
    return result[None]


def solution(mesh):
    return jax.shard_map(
        body,
        mesh=mesh,
        in_specs=(
            P("section", "expert", None),
            P("section", None),
            P("section", None, "expert"),
            P("section", None, "expert"),
            P("section", None, "expert", None, None, None),
            P("section", None, "expert", None, None, None),
            P("section", None, "expert"),
            P("section", None),
            P("section", "expert", None, None),
            P("section", "expert", None, None),
            P("section", "expert", None, None),
            P("section", None, "expert", None),
            P("section", None, "expert", None),
        ),
        out_specs=P("section", "expert", None),
        check_vma=False,
    )
```

```python
import functools

import jax
import jax.numpy as jnp
from jax import lax
from jax.experimental import pallas as pl
from jax.experimental.pallas import tpu as pltpu
from jax.sharding import PartitionSpec as P

STEPS = 3
EPS = 1e-06
LIMIT = 32 * 1024 * 1024
F32 = jnp.float32
BF16 = jnp.bfloat16


def passed_along(array, axis, by):
    length = lax.axis_size(axis)
    return lax.ppermute(array, axis, [(i, (i + by) % length) for i in range(length)])


def swapped(blocks):
    return lax.all_to_all(blocks, "expert", split_axis=0, concat_axis=0, tiled=True)


def everyones(array):
    devices = lax.axis_size("expert")
    return swapped(jnp.broadcast_to(array[None], (devices,) + array.shape))


def coefficients(route_ids, gate_vals, experts):
    shares = gate_vals / jnp.sum(gate_vals, axis=-1, keepdims=True)
    chosen = route_ids[..., None] == jnp.arange(experts, dtype=jnp.int32)
    return jnp.sum(jnp.where(chosen, shares[..., None], 0.0), axis=-2)


def whole(memory_space=pltpu.VMEM):
    return pl.BlockSpec(memory_space=memory_space)


def call(kernel, out, operands, specs, scratch, name, cost):
    single = not isinstance(out, tuple)
    return pl.pallas_call(
        kernel,
        out_shape=out,
        in_specs=specs,
        out_specs=whole() if single else tuple(whole() for _ in out),
        scratch_shapes=scratch,
        compiler_params=pltpu.CompilerParams(vmem_limit_bytes=LIMIT),
        cost_estimate=pl.CostEstimate(flops=cost[0], bytes_accessed=cost[1], transcendentals=0),
        name=name,
    )(*operands)


def normalize(source, gain_ref, target):
    rows, width = source.shape
    block = 16
    gain = gain_ref[...].astype(F32)
    for at in range(0, rows, block):
        values = source[at:at + block, :]
        scale = lax.rsqrt(jnp.mean(values * values, axis=-1, keepdims=True) + EPS)
        target[at:at + block, :] = (source[at:at + block, :] * scale * gain).astype(BF16)


def matmul(left, right, chunk=1024):
    depth = left.shape[1]
    total = None
    for at in range(0, depth, chunk):
        part = jnp.dot(left[:, at:at + chunk], right[at:at + chunk, :], preferred_element_type=F32)
        total = part if total is None else total + part
    return total


def query_kernel(head_dim, x_ref, gain_ref, w_ref, q_ref, states, normed, spread):
    devices, own, _ = x_ref.shape
    rows = devices * own
    heads = w_ref.shape[1] // head_dim
    for i in range(devices):
        states[own * i:own * (i + 1), :] = x_ref[i].astype(F32)
    normalize(states, gain_ref, normed)
    query = matmul(normed, w_ref)
    for h in range(heads):
        one = query[:, head_dim * h:head_dim * (h + 1)]
        scale = lax.rsqrt(jnp.mean(one * one, axis=-1, keepdims=True) + EPS)
        spread[pl.ds(h, rows, stride=heads), :] = one * scale
    q_ref[...] = spread[...].astype(BF16)


def attention_kernel(step, own, local_heads, kv_heads, q_ref, k_ref, v_ref, len_ref, c_ref):
    count, head_dim = q_ref.shape
    places = k_ref.shape[0]
    heads = count // own
    group = heads // kv_heads
    cache = places // (own * kv_heads)
    target = lax.broadcasted_iota(jnp.int32, (count, count), 0)
    source = lax.broadcasted_iota(jnp.int32, (count, count), 1)
    row, head = target // heads, target % heads
    wanted = (head // local_heads) * (own * local_heads) + row * local_heads + head % local_heads
    order = (source == wanted).astype(F32).astype(BF16)
    q = jnp.dot(order, q_ref[...], preferred_element_type=F32).astype(BF16)
    scores = lax.dot_general(
        q, k_ref[...], (((1,), (1,)), ((), ())), preferred_element_type=F32
    ) * head_dim ** (-0.5)
    column = lax.broadcasted_iota(jnp.int32, (1, places), 1)
    of_row = column // (cache * kv_heads)
    position = (column // kv_heads) % cache
    length = jnp.zeros((1, places), jnp.int32)
    for r in range(own):
        length = jnp.where(of_row == r, len_ref[step, r], length)
    key_of = jnp.where(position < length, of_row * kv_heads + column % kv_heads, -1)
    line = lax.broadcasted_iota(jnp.int32, (count, 1), 0)
    key_for = (line // heads) * kv_heads + (line % heads) // group
    exps = jnp.where(key_of == key_for, jnp.exp(scores), 0.0)
    weights = (exps / jnp.sum(exps, axis=-1, keepdims=True)).astype(BF16)
    c_ref[...] = jnp.dot(weights, v_ref[...], preferred_element_type=F32).astype(BF16)


def out_kernel(heads, c_ref, w_ref, o_ref, wide, lines):
    rows = lines.shape[0]
    head_dim = c_ref.shape[1]
    wide[...] = c_ref[...].astype(F32)
    for h in range(heads):
        lines[:, head_dim * h:head_dim * (h + 1)] = wide[pl.ds(h, rows, stride=heads), :].astype(BF16)
    columns = matmul(lines, w_ref).astype(BF16)
    for i in range(o_ref.shape[0]):
        o_ref[i] = columns


def expert_kernel(me_ref, a_ref, x_ref, gain_ref, gate_ref, up_ref, down_ref, h_ref, m_ref, middle, normed):
    devices, own, width = x_ref.shape
    part = a_ref.shape[2]
    for i in range(devices):
        middle[own * i:own * (i + 1), :] = x_ref[i].astype(F32)
    for j in range(devices):
        at = slice(part * j, part * (j + 1))
        middle[:, at] = middle[:, at] + a_ref[j].astype(F32)
    normalize(middle, gain_ref, normed)
    gate = matmul(normed, gate_ref)
    up = matmul(normed, up_ref)
    active = (gate / (1.0 + jnp.exp(-gate)) * up).astype(BF16)
    chunk = 512
    for at in range(0, width, chunk):
        piece = jnp.dot(active, down_ref[:, at:at + chunk], preferred_element_type=F32)
        for i in range(devices):
            h_ref[i, :, at:at + chunk] = piece[own * i:own * (i + 1), :].astype(BF16)
    pairs = 8 // own
    me = me_ref[0]
    block = middle[pl.ds(pl.multiple_of((me // pairs) * 8, 8), 8), :]
    kept = block[0:own, :]
    for p in range(1, pairs):
        kept = jnp.where(me % pairs == p, block[own * p:own * (p + 1), :], kept)
    m_ref[...] = kept


def combine_kernel(r_ref, m_ref, coeff_ref, o_ref):
    total = m_ref[...]
    for e in range(r_ref.shape[0] // 2):
        pair = (r_ref[2 * e].astype(F32) + r_ref[2 * e + 1].astype(F32)).astype(BF16).astype(F32)
        total = total + coeff_ref[:, e:e + 1] * pair
    o_ref[...] = total.astype(BF16)


def body(
    hidden_in,
    attn_gain,
    w_query,
    w_out,
    key_cache,
    value_cache,
    lengths,
    ffn_gain,
    w_gate,
    w_up,
    w_down,
    routes,
    gates,
):
    devices = lax.axis_size("expert")
    me = lax.axis_index("expert").astype(jnp.int32).reshape(1)
    experts = devices // 2
    own, width = hidden_in.shape[1:]
    rows = own * devices
    cache_len, kv_heads, head_dim = key_cache.shape[3:]
    query_w, out_w = w_query[0], w_out[0]
    part = query_w.shape[1]
    local_heads = part // head_dim
    heads = local_heads * devices
    gate_w, up_w, down_w = w_gate[0, 0], w_up[0, 0], w_down[0, 0]
    hidden = gate_w.shape[1]
    places = own * cache_len * kv_heads
    keys = key_cache.reshape(STEPS, places, head_dim)
    values = value_cache.reshape(STEPS, places, head_dim)
    shares = coefficients(routes[0], gates[0], experts)
    state = hidden_in[0]
    smem = whole(pltpu.SMEM)
    for step in range(STEPS):
        states = everyones(state)
        own_q = call(
            functools.partial(query_kernel, head_dim),
            jax.ShapeDtypeStruct((rows * local_heads, head_dim), BF16),
            (states, attn_gain, query_w),
            [whole()] * 3,
            [
                pltpu.VMEM((rows, width), F32),
                pltpu.VMEM((rows, width), BF16),
                pltpu.VMEM((rows * local_heads, head_dim), F32),
            ],
            "query",
            (2 * rows * width * part, 2 * width * part),
        )
        queries = swapped(own_q.reshape(devices, own * local_heads, head_dim))
        of_step = pl.BlockSpec((None, places, head_dim), lambda i, step=step: (step, 0, 0))
        context = pl.pallas_call(
            functools.partial(attention_kernel, step, own, local_heads, kv_heads),
            grid=(1,),
            out_shape=jax.ShapeDtypeStruct((own * heads, head_dim), BF16),
            in_specs=[
                pl.BlockSpec((own * heads, head_dim), lambda i: (0, 0)),
                of_step,
                of_step,
                smem,
            ],
            out_specs=pl.BlockSpec((own * heads, head_dim), lambda i: (0, 0)),
            compiler_params=pltpu.CompilerParams(vmem_limit_bytes=LIMIT),
            cost_estimate=pl.CostEstimate(
                flops=4 * own * heads * places * head_dim,
                bytes_accessed=4 * places * head_dim,
                transcendentals=0,
            ),
            name="attention",
        )(queries.reshape(own * heads, head_dim), keys, values, lengths[0])
        contexts = everyones(context)
        columns = call(
            functools.partial(out_kernel, heads),
            jax.ShapeDtypeStruct((devices, rows, part), BF16),
            (contexts.reshape(rows * heads, head_dim), out_w),
            [whole()] * 2,
            [pltpu.VMEM((rows * heads, head_dim), F32), pltpu.VMEM((rows, heads * head_dim), BF16)],
            "attention_out",
            (2 * rows * width * part, 2 * width * part),
        )
        attended = swapped(columns)
        half_out, middle = call(
            expert_kernel,
            (
                jax.ShapeDtypeStruct((devices, own, width), BF16),
                jax.ShapeDtypeStruct((own, width), F32),
            ),
            (me, attended, states, ffn_gain, gate_w, up_w, down_w),
            [smem] + [whole()] * 6,
            [pltpu.VMEM((rows, width), F32), pltpu.VMEM((rows, width), BF16)],
            "experts",
            (6 * rows * width * hidden, 6 * width * hidden),
        )
        returned = swapped(half_out)
        state = call(
            combine_kernel,
            jax.ShapeDtypeStruct((own, width), BF16),
            (returned, middle, shares[step]),
            [whole()] * 3,
            [],
            "combine",
            (4 * rows * width, 4 * rows * width),
        )
        if step + 1 < STEPS:
            state = passed_along(state, "section", 1)
    return state[None]


def solution(mesh):
    return jax.shard_map(
        body,
        mesh=mesh,
        in_specs=(
            P("section", "expert", None),
            P("section", None),
            P("section", None, "expert"),
            P("section", None, "expert"),
            P("section", None, "expert", None, None, None),
            P("section", None, "expert", None, None, None),
            P("section", None, "expert"),
            P("section", None),
            P("section", "expert", None, None),
            P("section", "expert", None, None),
            P("section", "expert", None, None),
            P("section", None, "expert", None),
            P("section", None, "expert", None),
        ),
        out_specs=P("section", "expert", None),
        check_vma=False,
    )
```

```python
import functools

import jax
import jax.numpy as jnp
from jax import lax
from jax.experimental import pallas as pl
from jax.experimental.pallas import tpu as pltpu
from jax.sharding import PartitionSpec as P

STEPS = 3
EPS = 1e-06
LIMIT = 24 * 1024 * 1024
EXCHANGE = 20 * 1000 * 1000 * 1000
F32 = jnp.float32
BF16 = jnp.bfloat16


def passed_along(array, axis, by):
    length = lax.axis_size(axis)
    return lax.ppermute(array, axis, [(i, (i + by) % length) for i in range(length)])


def swapped(blocks):
    return lax.all_to_all(blocks, "expert", split_axis=0, concat_axis=0, tiled=True)


def everyones(array):
    devices = lax.axis_size("expert")
    return swapped(jnp.broadcast_to(array[None], (devices,) + array.shape))


def whole(memory_space=pltpu.VMEM):
    return pl.BlockSpec(memory_space=memory_space)


def call(kernel, out, operands, specs, scratch, name, cost):
    single = not isinstance(out, tuple)
    return pl.pallas_call(
        kernel,
        out_shape=out,
        in_specs=specs,
        out_specs=whole() if single else tuple(whole() for _ in out),
        scratch_shapes=scratch,
        compiler_params=pltpu.CompilerParams(vmem_limit_bytes=LIMIT),
        cost_estimate=pl.CostEstimate(flops=cost[0] + EXCHANGE, bytes_accessed=cost[1], transcendentals=0),
        name=name,
    )(*operands)


def normalize(source, gain_ref, target):
    rows, width = source.shape
    block = 16
    gain = gain_ref[...].astype(F32)
    for at in range(0, rows, block):
        values = source[at:at + block, :]
        scale = lax.rsqrt(jnp.mean(values * values, axis=-1, keepdims=True) + EPS)
        target[at:at + block, :] = (source[at:at + block, :] * scale * gain).astype(BF16)


def matmul(left, right, chunk=1024):
    depth = left.shape[1]
    total = None
    for at in range(0, depth, chunk):
        part = jnp.dot(left[:, at:at + chunk], right[at:at + chunk, :], preferred_element_type=F32)
        total = part if total is None else total + part
    return total


def spread_kernel(x_ref, o_ref):
    for i in range(o_ref.shape[0]):
        o_ref[i] = x_ref[...]


def query_kernel(head_dim, x_ref, gain_ref, w_ref, q_ref, states, normed, spread):
    devices, own, _ = x_ref.shape
    rows = devices * own
    heads = w_ref.shape[1] // head_dim
    for i in range(devices):
        states[own * i:own * (i + 1), :] = x_ref[i].astype(F32)
    normalize(states, gain_ref, normed)
    query = matmul(normed, w_ref)
    for h in range(heads):
        one = query[:, head_dim * h:head_dim * (h + 1)]
        scale = lax.rsqrt(jnp.mean(one * one, axis=-1, keepdims=True) + EPS)
        spread[pl.ds(h, rows, stride=heads), :] = one * scale
    q_ref[...] = spread[...].astype(BF16)


def attention_kernel(step, own, local_heads, kv_heads, q_ref, k_ref, v_ref, len_ref, c_ref):
    count, head_dim = q_ref.shape
    places = k_ref.shape[0]
    heads = count // own
    group = heads // kv_heads
    cache = places // (own * kv_heads)
    target = lax.broadcasted_iota(jnp.int32, (count, count), 0)
    source = lax.broadcasted_iota(jnp.int32, (count, count), 1)
    row, head = target // heads, target % heads
    wanted = (head // local_heads) * (own * local_heads) + row * local_heads + head % local_heads
    order = (source == wanted).astype(F32).astype(BF16)
    q = jnp.dot(order, q_ref[...], preferred_element_type=F32).astype(BF16)
    scores = lax.dot_general(
        q, k_ref[...], (((1,), (1,)), ((), ())), preferred_element_type=F32
    ) * head_dim ** (-0.5)
    column = lax.broadcasted_iota(jnp.int32, (1, places), 1)
    of_row = column // (cache * kv_heads)
    position = (column // kv_heads) % cache
    length = jnp.zeros((1, places), jnp.int32)
    for r in range(own):
        length = jnp.where(of_row == r, len_ref[step, 0, r], length)
    key_of = jnp.where(position < length, of_row * kv_heads + column % kv_heads, -1)
    line = lax.broadcasted_iota(jnp.int32, (count, 1), 0)
    key_for = (line // heads) * kv_heads + (line % heads) // group
    exps = jnp.where(key_of == key_for, jnp.exp(scores), 0.0)
    weights = (exps / jnp.sum(exps, axis=-1, keepdims=True)).astype(BF16)
    c_ref[...] = jnp.dot(weights, v_ref[...], preferred_element_type=F32).astype(BF16)


def out_kernel(heads, c_ref, w_ref, o_ref, wide, lines):
    rows = lines.shape[0]
    head_dim = c_ref.shape[1]
    wide[...] = c_ref[...].astype(F32)
    for h in range(heads):
        lines[:, head_dim * h:head_dim * (h + 1)] = wide[pl.ds(h, rows, stride=heads), :].astype(BF16)
    columns = matmul(lines, w_ref).astype(BF16)
    for i in range(o_ref.shape[0]):
        o_ref[i] = columns


def expert_kernel(me_ref, a_ref, x_ref, gain_ref, gate_ref, up_ref, down_ref, h_ref, m_ref, middle, normed):
    devices, own, width = x_ref.shape
    part = a_ref.shape[2]
    for i in range(devices):
        middle[own * i:own * (i + 1), :] = x_ref[i].astype(F32)
    for j in range(devices):
        at = slice(part * j, part * (j + 1))
        middle[:, at] = middle[:, at] + a_ref[j].astype(F32)
    normalize(middle, gain_ref, normed)
    gate = matmul(normed, gate_ref)
    up = matmul(normed, up_ref)
    active = (gate / (1.0 + jnp.exp(-gate)) * up).astype(BF16)
    chunk = 512
    for at in range(0, width, chunk):
        piece = jnp.dot(active, down_ref[:, at:at + chunk], preferred_element_type=F32)
        for i in range(devices):
            h_ref[i, :, at:at + chunk] = piece[own * i:own * (i + 1), :].astype(BF16)
    pairs = 8 // own
    me = me_ref[0]
    block = middle[pl.ds(pl.multiple_of((me // pairs) * 8, 8), 8), :]
    kept = block[0:own, :]
    for p in range(1, pairs):
        kept = jnp.where(me % pairs == p, block[own * p:own * (p + 1), :], kept)
    m_ref[...] = kept


def combine_kernel(step, r_ref, m_ref, routes_ref, gates_ref, o_ref):
    own = m_ref.shape[0]
    routes, gates = routes_ref[step], gates_ref[step]
    shares = gates / jnp.sum(gates, axis=0, keepdims=True)
    line = lax.broadcasted_iota(jnp.int32, (own, own), 0)
    column = lax.broadcasted_iota(jnp.int32, (own, own), 1)
    total = m_ref[...]
    for e in range(r_ref.shape[0] // 2):
        pair = (r_ref[2 * e].astype(F32) + r_ref[2 * e + 1].astype(F32)).astype(BF16).astype(F32)
        coeff = jnp.sum(jnp.where(routes == e, shares, 0.0), axis=0, keepdims=True)
        coeff = jnp.sum(jnp.where(line == column, coeff, 0.0), axis=1, keepdims=True)
        total = total + coeff * pair
    o_ref[...] = total.astype(BF16)


def body(
    hidden_in,
    attn_gain,
    w_query,
    w_out,
    key_cache,
    value_cache,
    lengths,
    ffn_gain,
    w_gate,
    w_up,
    w_down,
    routes,
    gates,
):
    devices = lax.axis_size("expert")
    me = lax.axis_index("expert").astype(jnp.int32).reshape(1)
    own, width = hidden_in.shape[1:]
    rows = own * devices
    cache_len, kv_heads, head_dim = key_cache.shape[3:]
    query_w, out_w = w_query[0], w_out[0]
    part = query_w.shape[1]
    local_heads = part // head_dim
    heads = local_heads * devices
    gate_w, up_w, down_w = w_gate[0, 0], w_up[0, 0], w_down[0, 0]
    hidden = gate_w.shape[1]
    places = own * cache_len * kv_heads
    keys = key_cache.reshape(STEPS, places, head_dim)
    values = value_cache.reshape(STEPS, places, head_dim)
    routes, gates = routes[0].transpose(0, 2, 1), gates[0].transpose(0, 2, 1)
    lengths = lengths.reshape(STEPS, 1, own)
    copies = call(
        spread_kernel,
        jax.ShapeDtypeStruct((devices, own, width), BF16),
        (hidden_in[0],),
        [whole()],
        [],
        "spread",
        (0, 2 * rows * width),
    )
    me, copies = lax.optimization_barrier((me, copies))
    smem = whole(pltpu.SMEM)
    for step in range(STEPS):
        if step:
            copies = jnp.broadcast_to(state[None], (devices, own, width))
        states = swapped(copies)
        own_q = call(
            functools.partial(query_kernel, head_dim),
            jax.ShapeDtypeStruct((rows * local_heads, head_dim), BF16),
            (states, attn_gain, query_w),
            [whole()] * 3,
            [
                pltpu.VMEM((rows, width), F32),
                pltpu.VMEM((rows, width), BF16),
                pltpu.VMEM((rows * local_heads, head_dim), F32),
            ],
            "query",
            (2 * rows * width * part, 2 * width * part),
        )
        queries = swapped(own_q.reshape(devices, own * local_heads, head_dim))
        of_step = pl.BlockSpec((None, places, head_dim), lambda i, step=step: (step, 0, 0))
        context = pl.pallas_call(
            functools.partial(attention_kernel, step, own, local_heads, kv_heads),
            grid=(1,),
            out_shape=jax.ShapeDtypeStruct((own * heads, head_dim), BF16),
            in_specs=[
                pl.BlockSpec((own * heads, head_dim), lambda i: (0, 0)),
                of_step,
                of_step,
                smem,
            ],
            out_specs=pl.BlockSpec((own * heads, head_dim), lambda i: (0, 0)),
            compiler_params=pltpu.CompilerParams(vmem_limit_bytes=LIMIT),
            cost_estimate=pl.CostEstimate(
                flops=4 * own * heads * places * head_dim + EXCHANGE,
                bytes_accessed=4 * places * head_dim,
                transcendentals=0,
            ),
            name="attention",
        )(queries.reshape(own * heads, head_dim), keys, values, lengths)
        contexts = everyones(context)
        columns = call(
            functools.partial(out_kernel, heads),
            jax.ShapeDtypeStruct((devices, rows, part), BF16),
            (contexts.reshape(rows * heads, head_dim), out_w),
            [whole()] * 2,
            [pltpu.VMEM((rows * heads, head_dim), F32), pltpu.VMEM((rows, heads * head_dim), BF16)],
            "attention_out",
            (2 * rows * width * part, 2 * width * part),
        )
        attended = swapped(columns)
        half_out, middle = call(
            expert_kernel,
            (
                jax.ShapeDtypeStruct((devices, own, width), BF16),
                jax.ShapeDtypeStruct((own, width), F32),
            ),
            (me, attended, states, ffn_gain, gate_w, up_w, down_w),
            [smem] + [whole()] * 6,
            [pltpu.VMEM((rows, width), F32), pltpu.VMEM((rows, width), BF16)],
            "experts",
            (6 * rows * width * hidden, 6 * width * hidden),
        )
        returned = swapped(half_out)
        state = call(
            functools.partial(combine_kernel, step),
            jax.ShapeDtypeStruct((own, width), BF16),
            (returned, middle, routes, gates),
            [whole()] * 4,
            [],
            "combine",
            (4 * rows * width, 4 * rows * width),
        )
        if step + 1 < STEPS:
            state = passed_along(state, "section", 1)
    return state[None]


def solution(mesh):
    return jax.shard_map(
        body,
        mesh=mesh,
        in_specs=(
            P("section", "expert", None),
            P("section", None),
            P("section", None, "expert"),
            P("section", None, "expert"),
            P("section", None, "expert", None, None, None),
            P("section", None, "expert", None, None, None),
            P("section", None, "expert"),
            P("section", None),
            P("section", "expert", None, None),
            P("section", "expert", None, None),
            P("section", "expert", None, None),
            P("section", None, "expert", None),
            P("section", None, "expert", None),
        ),
        out_specs=P("section", "expert", None),
        check_vma=False,
    )
```

```python
import functools

import jax
import jax.numpy as jnp
from jax import lax
from jax.experimental import pallas as pl
from jax.experimental.pallas import tpu as pltpu
from jax.sharding import PartitionSpec as P

STEPS = 3
EPS = 1e-06
LIMIT = 24 * 1024 * 1024
EXCHANGE = 20 * 1000 * 1000 * 1000
F32 = jnp.float32
BF16 = jnp.bfloat16


def shifted(array, mask, sections=0):
    stages, devices = lax.axis_size("section"), lax.axis_size("expert")
    pairs = [
        (s * devices + e, (s + sections) % stages * devices + (e ^ mask))
        for s in range(stages)
        for e in range(devices)
    ]
    return lax.ppermute(array, ("section", "expert"), pairs)


def from_last_section(state):
    devices = lax.axis_size("expert")
    pieces = 1
    while pieces * pieces < devices:
        pieces *= 2
    first = jnp.stack([shifted(state, h * pieces, 1) for h in range(devices // pieces)])
    return [first] + [shifted(first, l) for l in range(1, pieces)]


def swapped(blocks):
    return lax.all_to_all(blocks, "expert", split_axis=0, concat_axis=0, tiled=True)


def everyones(array):
    devices = lax.axis_size("expert")
    return swapped(jnp.broadcast_to(array[None], (devices,) + array.shape))


def whole(memory_space=pltpu.VMEM):
    return pl.BlockSpec(memory_space=memory_space)


def call(kernel, out, operands, specs, scratch, name, cost):
    single = not isinstance(out, tuple)
    return pl.pallas_call(
        kernel,
        out_shape=out,
        in_specs=specs,
        out_specs=whole() if single else tuple(whole() for _ in out),
        scratch_shapes=scratch,
        compiler_params=pltpu.CompilerParams(vmem_limit_bytes=LIMIT),
        cost_estimate=pl.CostEstimate(flops=cost[0] + EXCHANGE, bytes_accessed=cost[1], transcendentals=0),
        name=name,
    )(*operands)


def normalize(source, gain_ref, target):
    rows, width = source.shape
    block = 16
    gain = gain_ref[...].astype(F32)
    for at in range(0, rows, block):
        values = source[at:at + block, :]
        scale = lax.rsqrt(jnp.mean(values * values, axis=-1, keepdims=True) + EPS)
        target[at:at + block, :] = (source[at:at + block, :] * scale * gain).astype(BF16)


def matmul(left, right, chunk=1024):
    depth = left.shape[1]
    total = None
    for at in range(0, depth, chunk):
        part = jnp.dot(left[:, at:at + chunk], right[at:at + chunk, :], preferred_element_type=F32)
        total = part if total is None else total + part
    return total


def spread_kernel(x_ref, o_ref):
    for i in range(o_ref.shape[0]):
        o_ref[i] = x_ref[...]


def order_kernel(head_dim, count, me_ref, *refs):
    pieces, (gain_ref, w_ref, q_ref, x_ref, *scratch) = refs[:count], refs[count:]
    me = me_ref[0]
    for l, piece in enumerate(pieces):
        for h in range(piece.shape[0]):
            x_ref[me ^ (l + h * count)] = piece[h]
    query_kernel(head_dim, x_ref, gain_ref, w_ref, q_ref, *scratch)


def query_kernel(head_dim, x_ref, gain_ref, w_ref, q_ref, states, normed, spread):
    devices, own, _ = x_ref.shape
    rows = devices * own
    heads = w_ref.shape[1] // head_dim
    for i in range(devices):
        states[own * i:own * (i + 1), :] = x_ref[i].astype(F32)
    normalize(states, gain_ref, normed)
    query = matmul(normed, w_ref)
    for h in range(heads):
        one = query[:, head_dim * h:head_dim * (h + 1)]
        scale = lax.rsqrt(jnp.mean(one * one, axis=-1, keepdims=True) + EPS)
        spread[pl.ds(h, rows, stride=heads), :] = one * scale
    q_ref[...] = spread[...].astype(BF16)


def attention_kernel(step, own, local_heads, kv_heads, q_ref, k_ref, v_ref, len_ref, c_ref):
    count, head_dim = q_ref.shape
    places = k_ref.shape[1]
    heads = count // own
    group = heads // kv_heads
    cache = places // (own * kv_heads)
    target = lax.broadcasted_iota(jnp.int32, (count, count), 0)
    source = lax.broadcasted_iota(jnp.int32, (count, count), 1)
    row, head = target // heads, target % heads
    wanted = (head // local_heads) * (own * local_heads) + row * local_heads + head % local_heads
    order = (source == wanted).astype(F32).astype(BF16)
    q = jnp.dot(order, q_ref[...], preferred_element_type=F32).astype(BF16)
    scores = lax.dot_general(
        q, k_ref[step], (((1,), (1,)), ((), ())), preferred_element_type=F32
    ) * head_dim ** (-0.5)
    column = lax.broadcasted_iota(jnp.int32, (1, places), 1)
    of_row = column // (cache * kv_heads)
    position = (column // kv_heads) % cache
    length = jnp.zeros((1, places), jnp.int32)
    for r in range(own):
        length = jnp.where(of_row == r, len_ref[step, 0, r], length)
    key_of = jnp.where(position < length, of_row * kv_heads + column % kv_heads, -1)
    line = lax.broadcasted_iota(jnp.int32, (count, 1), 0)
    key_for = (line // heads) * kv_heads + (line % heads) // group
    exps = jnp.where(key_of == key_for, jnp.exp(scores), 0.0)
    weights = (exps / jnp.sum(exps, axis=-1, keepdims=True)).astype(BF16)
    c_ref[...] = jnp.dot(weights, v_ref[step], preferred_element_type=F32).astype(BF16)


def out_kernel(heads, c_ref, w_ref, o_ref, wide, lines):
    rows = lines.shape[0]
    head_dim = c_ref.shape[1]
    wide[...] = c_ref[...].astype(F32)
    for h in range(heads):
        lines[:, head_dim * h:head_dim * (h + 1)] = wide[pl.ds(h, rows, stride=heads), :].astype(BF16)
    columns = matmul(lines, w_ref).astype(BF16)
    for i in range(o_ref.shape[0]):
        o_ref[i] = columns


def expert_kernel(me_ref, a_ref, x_ref, gain_ref, gate_ref, up_ref, down_ref, h_ref, m_ref, middle, normed):
    devices, own, width = x_ref.shape
    part = a_ref.shape[2]
    for i in range(devices):
        middle[own * i:own * (i + 1), :] = x_ref[i].astype(F32)
    for j in range(devices):
        at = slice(part * j, part * (j + 1))
        middle[:, at] = middle[:, at] + a_ref[j].astype(F32)
    normalize(middle, gain_ref, normed)
    gate = matmul(normed, gate_ref)
    up = matmul(normed, up_ref)
    active = (gate / (1.0 + jnp.exp(-gate)) * up).astype(BF16)
    chunk = 512
    for at in range(0, width, chunk):
        piece = jnp.dot(active, down_ref[:, at:at + chunk], preferred_element_type=F32)
        for i in range(devices):
            h_ref[i, :, at:at + chunk] = piece[own * i:own * (i + 1), :].astype(BF16)
    pairs = 8 // own
    me = me_ref[0]
    block = middle[pl.ds(pl.multiple_of((me // pairs) * 8, 8), 8), :]
    kept = block[0:own, :]
    for p in range(1, pairs):
        kept = jnp.where(me % pairs == p, block[own * p:own * (p + 1), :], kept)
    m_ref[...] = kept


def combine_kernel(step, r_ref, m_ref, routes_ref, gates_ref, o_ref):
    own = m_ref.shape[0]
    routes, gates = routes_ref[step], gates_ref[step]
    shares = gates / jnp.sum(gates, axis=0, keepdims=True)
    line = lax.broadcasted_iota(jnp.int32, (own, own), 0)
    column = lax.broadcasted_iota(jnp.int32, (own, own), 1)
    total = m_ref[...]
    for e in range(r_ref.shape[0] // 2):
        pair = (r_ref[2 * e].astype(F32) + r_ref[2 * e + 1].astype(F32)).astype(BF16).astype(F32)
        coeff = jnp.sum(jnp.where(routes == e, shares, 0.0), axis=0, keepdims=True)
        coeff = jnp.sum(jnp.where(line == column, coeff, 0.0), axis=1, keepdims=True)
        total = total + coeff * pair
    o_ref[...] = total.astype(BF16)


def body(
    hidden_in,
    attn_gain,
    w_query,
    w_out,
    key_cache,
    value_cache,
    lengths,
    ffn_gain,
    w_gate,
    w_up,
    w_down,
    routes,
    gates,
):
    devices = lax.axis_size("expert")
    me = lax.axis_index("expert").astype(jnp.int32).reshape(1)
    own, width = hidden_in.shape[1:]
    rows = own * devices
    cache_len, kv_heads, head_dim = key_cache.shape[3:]
    query_w, out_w = w_query[0], w_out[0]
    part = query_w.shape[1]
    local_heads = part // head_dim
    heads = local_heads * devices
    gate_w, up_w, down_w = w_gate[0, 0], w_up[0, 0], w_down[0, 0]
    hidden = gate_w.shape[1]
    places = own * cache_len * kv_heads
    keys = key_cache.reshape(STEPS, places, head_dim)
    values = value_cache.reshape(STEPS, places, head_dim)
    routes, gates = routes[0].transpose(0, 2, 1), gates[0].transpose(0, 2, 1)
    lengths = lengths.reshape(STEPS, 1, own)
    copies = call(
        spread_kernel,
        jax.ShapeDtypeStruct((devices, own, width), BF16),
        (hidden_in[0],),
        [whole()],
        [],
        "spread",
        (0, 2 * rows * width),
    )
    me, copies = lax.optimization_barrier((me, copies))
    smem = whole(pltpu.SMEM)
    for step in range(STEPS):
        scratch = [
            pltpu.VMEM((rows, width), F32),
            pltpu.VMEM((rows, width), BF16),
            pltpu.VMEM((rows * local_heads, head_dim), F32),
        ]
        q_shape = jax.ShapeDtypeStruct((rows * local_heads, head_dim), BF16)
        x_shape = jax.ShapeDtypeStruct((devices, own, width), BF16)
        cost = (2 * rows * width * part, 2 * width * part)
        if step == 0:
            states = swapped(copies)
            own_q = call(
                functools.partial(query_kernel, head_dim),
                q_shape,
                (states, attn_gain, query_w),
                [whole()] * 3,
                scratch,
                "query",
                cost,
            )
        else:
            pieces = from_last_section(state)
            count = len(pieces)
            own_q, states = call(
                functools.partial(order_kernel, head_dim, count),
                (q_shape, x_shape),
                (me, *pieces, attn_gain, query_w),
                [smem] + [whole()] * (count + 2),
                scratch,
                "order_query",
                cost,
            )
        queries = swapped(own_q.reshape(devices, own * local_heads, head_dim))
        context = call(
            functools.partial(attention_kernel, step, own, local_heads, kv_heads),
            jax.ShapeDtypeStruct((own * heads, head_dim), BF16),
            (queries.reshape(own * heads, head_dim), keys, values, lengths),
            [whole()] * 3 + [smem],
            [],
            "attention",
            (4 * own * heads * places * head_dim, 4 * places * head_dim),
        )
        contexts = everyones(context)
        columns = call(
            functools.partial(out_kernel, heads),
            jax.ShapeDtypeStruct((devices, rows, part), BF16),
            (contexts.reshape(rows * heads, head_dim), out_w),
            [whole()] * 2,
            [pltpu.VMEM((rows * heads, head_dim), F32), pltpu.VMEM((rows, heads * head_dim), BF16)],
            "attention_out",
            (2 * rows * width * part, 2 * width * part),
        )
        attended = swapped(columns)
        half_out, middle = call(
            expert_kernel,
            (
                jax.ShapeDtypeStruct((devices, own, width), BF16),
                jax.ShapeDtypeStruct((own, width), F32),
            ),
            (me, attended, states, ffn_gain, gate_w, up_w, down_w),
            [smem] + [whole()] * 6,
            [pltpu.VMEM((rows, width), F32), pltpu.VMEM((rows, width), BF16)],
            "experts",
            (6 * rows * width * hidden, 6 * width * hidden),
        )
        returned = swapped(half_out)
        state = call(
            functools.partial(combine_kernel, step),
            jax.ShapeDtypeStruct((own, width), BF16),
            (returned, middle, routes, gates),
            [whole()] * 4,
            [],
            "combine",
            (4 * rows * width, 4 * rows * width),
        )
    return state[None]


def solution(mesh):
    return jax.shard_map(
        body,
        mesh=mesh,
        in_specs=(
            P("section", "expert", None),
            P("section", None),
            P("section", None, "expert"),
            P("section", None, "expert"),
            P("section", None, "expert", None, None, None),
            P("section", None, "expert", None, None, None),
            P("section", None, "expert"),
            P("section", None),
            P("section", "expert", None, None),
            P("section", "expert", None, None),
            P("section", "expert", None, None),
            P("section", None, "expert", None),
            P("section", None, "expert", None),
        ),
        out_specs=P("section", "expert", None),
        check_vma=False,
    )
```

```python
import functools
import math

import jax
import jax.numpy as jnp
import numpy as np
from jax import lax
from jax.experimental import pallas as pl
from jax.experimental.pallas import tpu as pltpu
from jax.sharding import PartitionSpec as P

STEPS = 3
EPS = 1e-06
LIMIT = 24 * 1024 * 1024
EXCHANGE = 20 * 1000 * 1000 * 1000
LANES = 128
EXTRA = 16
LOG2E = math.log2(math.e)
F32 = jnp.float32
BF16 = jnp.bfloat16


def shifted(array, mask, sections=0):
    stages, devices = lax.axis_size("section"), lax.axis_size("expert")
    pairs = [
        (s * devices + e, (s + sections) % stages * devices + (e ^ mask))
        for s in range(stages)
        for e in range(devices)
    ]
    return lax.ppermute(array, ("section", "expert"), pairs)


def split(devices):
    low = 1
    while low * low < devices:
        low *= 2
    return low, devices // low


def swapped(blocks):
    return lax.all_to_all(blocks, "expert", split_axis=0, concat_axis=0, tiled=True)


def everyones(array):
    devices = lax.axis_size("expert")
    return swapped(jnp.broadcast_to(array[None], (devices,) + array.shape))


def whole(memory_space=pltpu.VMEM):
    return pl.BlockSpec(memory_space=memory_space)


def call(kernel, out, operands, specs, scratch, name, cost):
    single = not isinstance(out, tuple)
    return pl.pallas_call(
        kernel,
        out_shape=out,
        in_specs=specs,
        out_specs=whole() if single else tuple(whole() for _ in out),
        scratch_shapes=scratch,
        compiler_params=pltpu.CompilerParams(vmem_limit_bytes=LIMIT),
        cost_estimate=pl.CostEstimate(flops=cost[0] + EXCHANGE, bytes_accessed=cost[1], transcendentals=0),
        name=name,
    )(*operands)


def normalize(source, gain_ref, target):
    rows, width = source.shape
    block = 16
    gain = gain_ref[...].astype(F32)
    for at in range(0, rows, block):
        values = source[at:at + block, :]
        scale = lax.rsqrt(jnp.mean(values * values, axis=-1, keepdims=True) + EPS)
        target[at:at + block, :] = (source[at:at + block, :] * scale * gain).astype(BF16)


def matmul(left, right, chunk=1024):
    depth = left.shape[1]
    total = None
    for at in range(0, depth, chunk):
        part = jnp.dot(left[:, at:at + chunk], right[at:at + chunk, :], preferred_element_type=F32)
        total = part if total is None else total + part
    return total


def spread_kernel(x_ref, o_ref):
    for i in range(o_ref.shape[0]):
        o_ref[i] = x_ref[...]


def coded_shares(routes_ref, gates_ref, experts):
    own = routes_ref.shape[2]
    lane = lax.broadcasted_iota(jnp.int32, (EXTRA, LANES), 1)
    row = lax.broadcasted_iota(jnp.int32, (EXTRA, LANES), 0)
    line = lax.broadcasted_iota(jnp.int32, (EXTRA, own), 0)
    column = lax.broadcasted_iota(jnp.int32, (EXTRA, own), 1)
    here = (line == column) | (line == column + own) | (line == column + 2 * own)
    shares = jnp.zeros((EXTRA, LANES), F32)
    for step in range(STEPS):
        routes, gates = routes_ref[step], gates_ref[step]
        parts = gates / jnp.sum(gates, axis=0, keepdims=True)
        for e in range(experts):
            share = jnp.sum(jnp.where(routes == e, parts, 0.0), axis=0, keepdims=True)
            share = jnp.sum(jnp.where(here, share, 0.0), axis=1, keepdims=True)
            shares = jnp.where(lane == step * experts + e, share, shares)
    first = shares.astype(BF16).astype(F32)
    second = (shares - first).astype(BF16).astype(F32)
    return jnp.where(row < own, first, jnp.where(row < 2 * own, second, shares - first - second)).astype(BF16)


def first_kernel(head_dim, x_ref, gain_ref, w_ref, routes_ref, gates_ref, q_ref, states, normed, spread):
    query_kernel(head_dim, x_ref, gain_ref, w_ref, None, states, normed, spread)
    devices = q_ref.shape[0]
    count = spread.shape[0] // devices
    coded = coded_shares(routes_ref, gates_ref, devices // 2)
    for i in range(devices):
        q_ref[i, :EXTRA, :] = coded
        q_ref[i, EXTRA:, :] = spread[count * i:count * (i + 1), :].astype(BF16)


def order_kernel(head_dim, low, me_ref, *refs):
    pieces, (gain_ref, w_ref, q_ref, x_ref, *scratch) = refs[:low], refs[low:]
    me = me_ref[0]
    for l, piece in enumerate(pieces):
        for h in range(piece.shape[0]):
            x_ref[me ^ (l + h * low)] = piece[h]
    query_kernel(head_dim, x_ref, gain_ref, w_ref, q_ref, *scratch)


def query_kernel(head_dim, x_ref, gain_ref, w_ref, q_ref, states, normed, spread):
    devices, own, _ = x_ref.shape
    width = w_ref.shape[0]
    rows = devices * own
    heads = w_ref.shape[1] // head_dim
    for i in range(devices):
        states[own * i:own * (i + 1), :] = x_ref[i, :, :width].astype(F32)
    normalize(states, gain_ref, normed)
    query = matmul(normed, w_ref)
    for h in range(heads):
        one = query[:, head_dim * h:head_dim * (h + 1)]
        scale = lax.rsqrt(jnp.mean(one * one, axis=-1, keepdims=True) + EPS)
        spread[pl.ds(h, rows, stride=heads), :] = one * scale
    if q_ref is not None:
        q_ref[...] = spread[...].astype(BF16)


def first_attention_kernel(own, pick_ref, q_ref, *refs):
    *rest, share_ref = refs
    share_ref[...] = jnp.dot(pick_ref[...], q_ref[...], preferred_element_type=F32)
    attention_kernel(0, own, q_ref, *rest)


def attention_kernel(step, own, q_ref, k_ref, v_ref, len_ref, order_ref, line_ref, column_ref, c_ref):
    head_dim = q_ref.shape[1]
    q = jnp.dot(order_ref[...], q_ref[...], preferred_element_type=F32).astype(BF16)
    scores = lax.dot_general(q, k_ref[step], (((1,), (1,)), ((), ())), preferred_element_type=F32)
    key_of, position, of_row = column_ref[0:1, :], column_ref[1:2, :], column_ref[2:3, :]
    length = jnp.zeros(of_row.shape, jnp.int32)
    for r in range(own):
        length = jnp.where(of_row == r, len_ref[step, 0, r], length)
    key_of = jnp.where(position < length, key_of, -1)
    exps = jnp.where(key_of == line_ref[...], jnp.exp2(scores * (head_dim ** (-0.5) * LOG2E)), 0.0)
    scale = 1.0 / jnp.sum(exps, axis=-1, keepdims=True)
    context = jnp.dot(exps.astype(BF16), v_ref[step], preferred_element_type=F32)
    c_ref[...] = (context * scale).astype(BF16)


def attention_tables(own, heads, local_heads, kv_heads, cache_len):
    group = heads // kv_heads
    row, head = np.divmod(np.arange(own * heads), heads)
    sender, place = head // local_heads, row * local_heads + head % local_heads
    devices, count = heads // local_heads, own * local_heads
    order = np.zeros((own * heads, own * heads), np.float32)
    order[np.arange(own * heads), sender * count + place] = 1.0
    first_order = np.zeros((own * heads, devices * (EXTRA + count)), np.float32)
    first_order[np.arange(own * heads), sender * (EXTRA + count) + EXTRA + place] = 1.0
    pick = np.zeros((devices * own, devices * (EXTRA + count)), np.float32)
    for part in range(3):
        for r in range(own):
            pick[np.arange(devices) * own + r, np.arange(devices) * (EXTRA + count) + part * own + r] = 1.0
    line = (row * kv_heads + head // group).astype(np.int32)[:, None]
    place = np.arange(own * cache_len * kv_heads)
    of_row, position, kv = place // (cache_len * kv_heads), place // kv_heads % cache_len, place % kv_heads
    column = np.zeros((8, place.size), np.int32)
    column[:3] = of_row * kv_heads + kv, position, of_row
    asis = jnp.asarray(line), jnp.asarray(column)
    return (jnp.asarray(order, BF16), *asis), (jnp.asarray(first_order, BF16), *asis), jnp.asarray(pick, BF16)


def out_kernel(heads, c_ref, w_ref, o_ref, wide, lines):
    rows = lines.shape[0]
    head_dim = c_ref.shape[1]
    wide[...] = c_ref[...].astype(F32)
    for h in range(heads):
        lines[:, head_dim * h:head_dim * (h + 1)] = wide[pl.ds(h, rows, stride=heads), :].astype(BF16)
    columns = matmul(lines, w_ref).astype(BF16)
    for i in range(o_ref.shape[0]):
        o_ref[i] = columns


def expert_kernel(step, me_ref, a_ref, x_ref, gain_ref, gate_ref, up_ref, down_ref, share_ref, h_ref, m_ref, middle, normed):
    devices, own, _ = x_ref.shape
    part = a_ref.shape[2]
    width = part * devices
    me = me_ref[0]
    for i in range(devices):
        middle[own * i:own * (i + 1), :] = x_ref[i, :, :width].astype(F32)
    for j in range(devices):
        at = slice(part * j, part * (j + 1))
        middle[:, at] = middle[:, at] + a_ref[j].astype(F32)
    normalize(middle, gain_ref, normed)
    gate = matmul(normed, gate_ref)
    up = matmul(normed, up_ref)
    lane = lax.broadcasted_iota(jnp.int32, share_ref.shape, 1)
    mine = lane == step * (devices // 2) + me // 2
    share = jnp.sum(jnp.where(mine, share_ref[...], 0.0), axis=1, keepdims=True)
    active = (gate / (1.0 + jnp.exp(-gate)) * up * share).astype(BF16)
    chunk = 512
    for at in range(0, width, chunk):
        piece = jnp.dot(active, down_ref[:, at:at + chunk], preferred_element_type=F32)
        for i in range(devices):
            h_ref[i, :, at:at + chunk] = piece[own * i:own * (i + 1), :].astype(BF16)
    pairs = 8 // own
    block = middle[pl.ds(pl.multiple_of((me // pairs) * 8, 8), 8), :]
    kept = block[0:own, :]
    for p in range(1, pairs):
        kept = jnp.where(me % pairs == p, block[own * p:own * (p + 1), :], kept)
    m_ref[...] = kept


def sending_kernel(step, low, me_ref, *refs):
    pieces, (m_ref, middle, normed, rows) = refs[7:7 + low], refs[7 + low:]
    expert_kernel(step, me_ref, *refs[:7], rows, m_ref, middle, normed)
    me = me_ref[0]
    for l, piece in enumerate(pieces):
        for h in range(piece.shape[0]):
            piece[h] = rows[me ^ (l + h * low)]


def partial_kernel(m_ref, *refs):
    pieces, t_ref = refs[:-1], refs[-1]
    for h in range(t_ref.shape[0]):
        total = m_ref[...] if h == 0 else jnp.zeros(m_ref.shape, F32)
        for piece in pieces:
            total = total + piece[h].astype(F32)
        t_ref[h] = total.astype(BF16)


def join_kernel(*refs):
    parts, x_ref = refs[:-1], refs[-1]
    for g in range(len(parts)):
        total = parts[0][g].astype(F32)
        for h in range(1, len(parts)):
            total = total + parts[h][h ^ g].astype(F32)
        x_ref[g] = total.astype(BF16)


def combine_kernel(r_ref, m_ref, o_ref):
    total = m_ref[...]
    for i in range(r_ref.shape[0]):
        total = total + r_ref[i].astype(F32)
    o_ref[...] = total.astype(BF16)


def body(
    hidden_in,
    attn_gain,
    w_query,
    w_out,
    key_cache,
    value_cache,
    lengths,
    ffn_gain,
    w_gate,
    w_up,
    w_down,
    routes,
    gates,
):
    devices = lax.axis_size("expert")
    me = lax.axis_index("expert").astype(jnp.int32).reshape(1)
    own, width = hidden_in.shape[1:]
    rows = own * devices
    cache_len, kv_heads, head_dim = key_cache.shape[3:]
    query_w, out_w = w_query[0], w_out[0]
    part = query_w.shape[1]
    local_heads = part // head_dim
    heads = local_heads * devices
    gate_w, up_w, down_w = w_gate[0, 0], w_up[0, 0], w_down[0, 0]
    hidden = gate_w.shape[1]
    places = own * cache_len * kv_heads
    keys = key_cache.reshape(STEPS, places, head_dim)
    values = value_cache.reshape(STEPS, places, head_dim)
    routes, gates = routes[0].transpose(0, 2, 1), gates[0].transpose(0, 2, 1)
    lengths = lengths.reshape(STEPS, 1, own)
    tables, first_tables, pick = attention_tables(own, heads, local_heads, kv_heads, cache_len)
    low, high = split(devices)
    smem = whole(pltpu.SMEM)
    q_shape = jax.ShapeDtypeStruct((rows * local_heads, head_dim), BF16)
    x_shape = jax.ShapeDtypeStruct((devices, own, width), BF16)
    m_shape = jax.ShapeDtypeStruct((own, width), F32)
    slots = jax.ShapeDtypeStruct((high, own, width), BF16)
    copies = call(
        spread_kernel,
        x_shape,
        (hidden_in[0],),
        [whole()],
        [],
        "spread",
        (0, 2 * rows * width),
    )
    me, copies = lax.optimization_barrier((me, copies))
    for step in range(STEPS):
        scratch = [
            pltpu.VMEM((rows, width), F32),
            pltpu.VMEM((rows, width), BF16),
            pltpu.VMEM((rows * local_heads, head_dim), F32),
        ]
        cost = (2 * rows * width * part, 2 * width * part)
        if step == 0:
            states = swapped(copies)
            own_q = call(
                functools.partial(first_kernel, head_dim),
                jax.ShapeDtypeStruct((devices, EXTRA + own * local_heads, head_dim), BF16),
                (states, attn_gain, query_w, routes, gates),
                [whole()] * 5,
                scratch,
                "first_query",
                cost,
            )
        else:
            pieces = [state] + [shifted(state, l) for l in range(1, low)]
            own_q, states = call(
                functools.partial(order_kernel, head_dim, low),
                (q_shape, x_shape),
                (me, *pieces, attn_gain, query_w),
                [smem] + [whole()] * (low + 2),
                scratch,
                "order_query",
                cost,
            )
        c_shape = jax.ShapeDtypeStruct((own * heads, head_dim), BF16)
        cost = (4 * own * heads * places * head_dim, 4 * places * head_dim)
        queries = swapped(own_q.reshape(devices, -1, head_dim)).reshape(-1, head_dim)
        if step == 0:
            context, shares = call(
                functools.partial(first_attention_kernel, own),
                (c_shape, jax.ShapeDtypeStruct((rows, LANES), F32)),
                (pick, queries, keys, values, lengths, *first_tables),
                [whole()] * 4 + [smem] + [whole()] * 3,
                [],
                "first_attention",
                cost,
            )
        else:
            context = call(
                functools.partial(attention_kernel, step, own),
                c_shape,
                (queries, keys, values, lengths, *tables),
                [whole()] * 3 + [smem] + [whole()] * 3,
                [],
                "attention",
                cost,
            )
        contexts = everyones(context)
        columns = call(
            functools.partial(out_kernel, heads),
            jax.ShapeDtypeStruct((devices, rows, part), BF16),
            (contexts.reshape(rows * heads, head_dim), out_w),
            [whole()] * 2,
            [pltpu.VMEM((rows * heads, head_dim), F32), pltpu.VMEM((rows, heads * head_dim), BF16)],
            "attention_out",
            (2 * rows * width * part, 2 * width * part),
        )
        attended = swapped(columns)
        operands = (me, attended, states, ffn_gain, gate_w, up_w, down_w, shares)
        specs = [smem] + [whole()] * 7
        scratch = [pltpu.VMEM((rows, width), F32), pltpu.VMEM((rows, width), BF16)]
        cost = (6 * rows * width * hidden, 6 * width * hidden)
        if step + 1 == STEPS:
            half_out, middle = call(
                functools.partial(expert_kernel, step), (x_shape, m_shape), operands, specs, scratch, "experts", cost
            )
            state = call(
                combine_kernel,
                jax.ShapeDtypeStruct((own, width), BF16),
                (swapped(half_out), middle),
                [whole()] * 2,
                [],
                "combine",
                (rows * width, 4 * rows * width),
            )
        else:
            *pieces, middle = call(
                functools.partial(sending_kernel, step, low),
                (slots,) * low + (m_shape,),
                operands,
                specs,
                scratch + [pltpu.VMEM((devices, own, width), BF16)],
                "experts_sending",
                cost,
            )
            pieces = [pieces[0]] + [shifted(pieces[l], l) for l in range(1, low)]
            part_sums = call(
                partial_kernel, slots, (middle, *pieces), [whole()] * (low + 1), [], "partial",
                (rows * width, 4 * rows * width),
            )
            parts = [shifted(part_sums, h * low, 1) for h in range(high)]
            state = call(
                join_kernel, slots, tuple(parts), [whole()] * high, [], "join", (rows * width, 4 * rows * width)
            )
    return state[None]


def solution(mesh):
    return jax.shard_map(
        body,
        mesh=mesh,
        in_specs=(
            P("section", "expert", None),
            P("section", None),
            P("section", None, "expert"),
            P("section", None, "expert"),
            P("section", None, "expert", None, None, None),
            P("section", None, "expert", None, None, None),
            P("section", None, "expert"),
            P("section", None),
            P("section", "expert", None, None),
            P("section", "expert", None, None),
            P("section", "expert", None, None),
            P("section", None, "expert", None),
            P("section", None, "expert", None),
        ),
        out_specs=P("section", "expert", None),
        check_vma=False,
    )
```

```python
import functools
import math

import jax
import jax.numpy as jnp
import numpy as np
from jax import lax
from jax.experimental import pallas as pl
from jax.experimental.pallas import tpu as pltpu
from jax.sharding import PartitionSpec as P

STEPS = 3
EPS = 1e-06
LIMIT = 24 * 1024 * 1024
EXCHANGE = 20 * 1000 * 1000 * 1000
LANES = 128
EXTRA = 16
LOG2E = math.log2(math.e)
F32 = jnp.float32
BF16 = jnp.bfloat16


def shifted(array, mask, sections=0):
    stages, devices = lax.axis_size("section"), lax.axis_size("expert")
    pairs = [
        (s * devices + e, (s + sections) % stages * devices + (e ^ mask))
        for s in range(stages)
        for e in range(devices)
    ]
    return lax.ppermute(array, ("section", "expert"), pairs)


def split(devices):
    low = 1
    while low * low < devices:
        low *= 2
    return low, devices // low


def swapped(blocks):
    return lax.all_to_all(blocks, "expert", split_axis=0, concat_axis=0, tiled=True)


def everyones(array):
    devices = lax.axis_size("expert")
    return swapped(jnp.broadcast_to(array[None], (devices,) + array.shape))


def whole(memory_space=pltpu.VMEM):
    return pl.BlockSpec(memory_space=memory_space)


def call(kernel, out, operands, specs, scratch, name, cost):
    single = not isinstance(out, tuple)
    return pl.pallas_call(
        kernel,
        out_shape=out,
        in_specs=specs,
        out_specs=whole() if single else tuple(whole() for _ in out),
        scratch_shapes=scratch,
        compiler_params=pltpu.CompilerParams(vmem_limit_bytes=LIMIT),
        cost_estimate=pl.CostEstimate(flops=cost[0] + EXCHANGE, bytes_accessed=cost[1], transcendentals=0),
        name=name,
    )(*operands)


def add_tiles(totals, left, right, depth, tile=128):
    for at in range(0, right.shape[1], tile):
        part = jnp.dot(left, right[depth, at:at + tile], preferred_element_type=F32)
        totals[at] = totals[at] + part if at in totals else part


def add_squares(totals, values):
    for at in range(0, values.shape[1], 128):
        totals = totals + values[:, at:at + 128] * values[:, at:at + 128]
    return totals


def spread_kernel(x_ref, o_ref):
    for i in range(o_ref.shape[0]):
        o_ref[i] = x_ref[...]


def coded_shares(routes_ref, gates_ref, experts):
    own = routes_ref.shape[2]
    lane = lax.broadcasted_iota(jnp.int32, (EXTRA, LANES), 1)
    row = lax.broadcasted_iota(jnp.int32, (EXTRA, LANES), 0)
    line = lax.broadcasted_iota(jnp.int32, (EXTRA, own), 0)
    column = lax.broadcasted_iota(jnp.int32, (EXTRA, own), 1)
    here = (line == column) | (line == column + own) | (line == column + 2 * own)
    shares = jnp.zeros((EXTRA, LANES), F32)
    for step in range(STEPS):
        routes, gates = routes_ref[step], gates_ref[step]
        parts = gates / jnp.sum(gates, axis=0, keepdims=True)
        for e in range(experts):
            share = jnp.sum(jnp.where(routes == e, parts, 0.0), axis=0, keepdims=True)
            share = jnp.sum(jnp.where(here, share, 0.0), axis=1, keepdims=True)
            shares = jnp.where(lane == step * experts + e, share, shares)
    first = shares.astype(BF16).astype(F32)
    second = (shares - first).astype(BF16).astype(F32)
    return jnp.where(row < own, first, jnp.where(row < 2 * own, second, shares - first - second)).astype(BF16)


def first_kernel(head_dim, x_ref, gain_ref, w_ref, routes_ref, gates_ref, q_ref, states, spread):
    query_kernel(head_dim, x_ref, gain_ref, w_ref, None, states, spread)
    devices = q_ref.shape[0]
    count = spread.shape[0] // devices
    coded = coded_shares(routes_ref, gates_ref, devices // 2)
    for i in range(devices):
        q_ref[i, :EXTRA, :] = coded
        q_ref[i, EXTRA:, :] = spread[count * i:count * (i + 1), :].astype(BF16)


def order_kernel(head_dim, low, me_ref, *refs):
    pieces, (gain_ref, w_ref, q_ref, x_ref, *scratch) = refs[:low], refs[low:]
    me = me_ref[0]
    for l, piece in enumerate(pieces):
        for h in range(piece.shape[0]):
            x_ref[me ^ (l + h * low)] = piece[h]
    query_kernel(head_dim, x_ref, gain_ref, w_ref, q_ref, *scratch)


def query_kernel(head_dim, x_ref, gain_ref, w_ref, q_ref, states, spread):
    devices, own, _ = x_ref.shape
    rows, (width, columns) = devices * own, w_ref.shape
    heads = columns // head_dim
    chunk = 512
    totals, squares = {}, jnp.zeros((rows, 128), F32)
    for start in range(0, width, chunk):
        at = slice(start, start + chunk)
        for i in range(devices):
            states[own * i:own * (i + 1), at] = x_ref[i, :, at].astype(F32)
        values = states[:, at]
        squares = add_squares(squares, values)
        add_tiles(totals, (values * gain_ref[:, at].astype(F32)).astype(BF16), w_ref, at, head_dim)
    scale = lax.rsqrt(jnp.sum(squares, axis=-1, keepdims=True) / width + EPS)
    for h in range(heads):
        one = totals[head_dim * h] * scale
        norm = lax.rsqrt(jnp.mean(one * one, axis=-1, keepdims=True) + EPS)
        spread[pl.ds(h, rows, stride=heads), :] = one * norm
    if q_ref is not None:
        q_ref[...] = spread[...].astype(BF16)


def first_attention_kernel(own, pick_ref, q_ref, *refs):
    *rest, share_ref = refs
    share_ref[...] = jnp.dot(pick_ref[...], q_ref[...], preferred_element_type=F32)
    attention_kernel(0, own, q_ref, *rest)


def attention_kernel(step, own, q_ref, k_ref, v_ref, len_ref, order_ref, line_ref, column_ref, c_ref):
    head_dim = q_ref.shape[1]
    q = jnp.dot(order_ref[...], q_ref[...], preferred_element_type=F32).astype(BF16)
    scores = lax.dot_general(q, k_ref[step], (((1,), (1,)), ((), ())), preferred_element_type=F32)
    key_of, position, of_row = column_ref[0:1, :], column_ref[1:2, :], column_ref[2:3, :]
    length = jnp.zeros(of_row.shape, jnp.int32)
    for r in range(own):
        length = jnp.where(of_row == r, len_ref[step, 0, r], length)
    key_of = jnp.where(position < length, key_of, -1)
    exps = jnp.where(key_of == line_ref[...], jnp.exp2(scores * (head_dim ** (-0.5) * LOG2E)), 0.0)
    scale = 1.0 / jnp.sum(exps, axis=-1, keepdims=True)
    context = jnp.dot(exps.astype(BF16), v_ref[step], preferred_element_type=F32)
    c_ref[...] = (context * scale).astype(BF16)


def attention_tables(own, heads, local_heads, kv_heads, cache_len):
    group = heads // kv_heads
    row, head = np.divmod(np.arange(own * heads), heads)
    sender, place = head // local_heads, row * local_heads + head % local_heads
    devices, count = heads // local_heads, own * local_heads
    order = np.zeros((own * heads, own * heads), np.float32)
    order[np.arange(own * heads), sender * count + place] = 1.0
    first_order = np.zeros((own * heads, devices * (EXTRA + count)), np.float32)
    first_order[np.arange(own * heads), sender * (EXTRA + count) + EXTRA + place] = 1.0
    pick = np.zeros((devices * own, devices * (EXTRA + count)), np.float32)
    for part in range(3):
        for r in range(own):
            pick[np.arange(devices) * own + r, np.arange(devices) * (EXTRA + count) + part * own + r] = 1.0
    line = (row * kv_heads + head // group).astype(np.int32)[:, None]
    place = np.arange(own * cache_len * kv_heads)
    of_row, position, kv = place // (cache_len * kv_heads), place // kv_heads % cache_len, place % kv_heads
    column = np.zeros((8, place.size), np.int32)
    column[:3] = of_row * kv_heads + kv, position, of_row
    asis = jnp.asarray(line), jnp.asarray(column)
    return (jnp.asarray(order, BF16), *asis), (jnp.asarray(first_order, BF16), *asis), jnp.asarray(pick, BF16)


def out_kernel(heads, c_ref, w_ref, o_ref, wide, lines):
    rows = lines.shape[0]
    head_dim = c_ref.shape[1]
    wide[...] = c_ref[...].astype(F32)
    for h in range(heads):
        lines[:, head_dim * h:head_dim * (h + 1)] = wide[pl.ds(h, rows, stride=heads), :].astype(BF16)
    chunk, total = 1024, None
    for start in range(0, lines.shape[1], chunk):
        at = slice(start, start + chunk)
        part = jnp.dot(lines[:, at], w_ref[at, :], preferred_element_type=F32)
        total = part if total is None else total + part
    columns = total.astype(BF16)
    for i in range(o_ref.shape[0]):
        o_ref[i] = columns


def expert_kernel(step, me_ref, a_ref, x_ref, gain_ref, gate_ref, up_ref, down_ref, share_ref, h_ref, m_ref, middle):
    devices, own, _ = x_ref.shape
    part = a_ref.shape[2]
    width = part * devices
    me = me_ref[0]
    gates, ups, squares = {}, {}, jnp.zeros((devices * own, 128), F32)
    for j in range(devices):
        at = slice(part * j, part * (j + 1))
        for i in range(devices):
            middle[own * i:own * (i + 1), at] = x_ref[i, :, at].astype(F32)
        values = middle[:, at] + a_ref[j].astype(F32)
        middle[:, at] = values
        squares = add_squares(squares, values)
        left = (values * gain_ref[:, at].astype(F32)).astype(BF16)
        add_tiles(gates, left, gate_ref, at)
        add_tiles(ups, left, up_ref, at)
    scale = lax.rsqrt(jnp.sum(squares, axis=-1, keepdims=True) / width + EPS)
    lane = lax.broadcasted_iota(jnp.int32, share_ref.shape, 1)
    mine = lane == step * (devices // 2) + me // 2
    share = jnp.sum(jnp.where(mine, share_ref[...], 0.0), axis=1, keepdims=True)
    active = {}
    for at in gates:
        gate, up = gates[at] * scale, ups[at] * scale
        active[at] = (gate / (1.0 + jnp.exp(-gate)) * up * share).astype(BF16)
    chunk = 512
    for start in range(0, width, chunk):
        piece = None
        for at, left in active.items():
            term = jnp.dot(
                left, down_ref[at:at + left.shape[1], start:start + chunk], preferred_element_type=F32
            )
            piece = term if piece is None else piece + term
        for i in range(devices):
            h_ref[i, :, start:start + chunk] = piece[own * i:own * (i + 1), :].astype(BF16)
    pairs = 8 // own
    block = middle[pl.ds(pl.multiple_of((me // pairs) * 8, 8), 8), :]
    kept = block[0:own, :]
    for p in range(1, pairs):
        kept = jnp.where(me % pairs == p, block[own * p:own * (p + 1), :], kept)
    m_ref[...] = kept


def sending_kernel(step, low, me_ref, *refs):
    pieces, (m_ref, middle, rows) = refs[7:7 + low], refs[7 + low:]
    expert_kernel(step, me_ref, *refs[:7], rows, m_ref, middle)
    me = me_ref[0]
    for l, piece in enumerate(pieces):
        for h in range(piece.shape[0]):
            piece[h] = rows[me ^ (l + h * low)]


def partial_kernel(m_ref, *refs):
    pieces, t_ref = refs[:-1], refs[-1]
    for h in range(t_ref.shape[0]):
        total = m_ref[...] if h == 0 else jnp.zeros(m_ref.shape, F32)
        for piece in pieces:
            total = total + piece[h].astype(F32)
        t_ref[h] = total.astype(BF16)


def join_kernel(*refs):
    parts, x_ref = refs[:-1], refs[-1]
    for g in range(len(parts)):
        total = parts[0][g].astype(F32)
        for h in range(1, len(parts)):
            total = total + parts[h][h ^ g].astype(F32)
        x_ref[g] = total.astype(BF16)


def combine_kernel(r_ref, m_ref, o_ref):
    total = m_ref[...]
    for i in range(r_ref.shape[0]):
        total = total + r_ref[i].astype(F32)
    o_ref[...] = total.astype(BF16)


def body(
    hidden_in,
    attn_gain,
    w_query,
    w_out,
    key_cache,
    value_cache,
    lengths,
    ffn_gain,
    w_gate,
    w_up,
    w_down,
    routes,
    gates,
):
    devices = lax.axis_size("expert")
    me = lax.axis_index("expert").astype(jnp.int32).reshape(1)
    own, width = hidden_in.shape[1:]
    rows = own * devices
    cache_len, kv_heads, head_dim = key_cache.shape[3:]
    query_w, out_w = w_query[0], w_out[0]
    part = query_w.shape[1]
    local_heads = part // head_dim
    heads = local_heads * devices
    gate_w, up_w, down_w = w_gate[0, 0], w_up[0, 0], w_down[0, 0]
    hidden = gate_w.shape[1]
    places = own * cache_len * kv_heads
    keys = key_cache.reshape(STEPS, places, head_dim)
    values = value_cache.reshape(STEPS, places, head_dim)
    routes, gates = routes[0].transpose(0, 2, 1), gates[0].transpose(0, 2, 1)
    lengths = lengths.reshape(STEPS, 1, own)
    tables, first_tables, pick = attention_tables(own, heads, local_heads, kv_heads, cache_len)
    low, high = split(devices)
    smem = whole(pltpu.SMEM)
    q_shape = jax.ShapeDtypeStruct((rows * local_heads, head_dim), BF16)
    x_shape = jax.ShapeDtypeStruct((devices, own, width), BF16)
    m_shape = jax.ShapeDtypeStruct((own, width), F32)
    slots = jax.ShapeDtypeStruct((high, own, width), BF16)
    copies = call(
        spread_kernel,
        x_shape,
        (hidden_in[0],),
        [whole()],
        [],
        "spread",
        (0, 2 * rows * width),
    )
    me, copies = lax.optimization_barrier((me, copies))
    for step in range(STEPS):
        scratch = [
            pltpu.VMEM((rows, width), F32),
            pltpu.VMEM((rows * local_heads, head_dim), F32),
        ]
        cost = (2 * rows * width * part, 2 * width * part)
        if step == 0:
            states = swapped(copies)
            own_q = call(
                functools.partial(first_kernel, head_dim),
                jax.ShapeDtypeStruct((devices, EXTRA + own * local_heads, head_dim), BF16),
                (states, attn_gain, query_w, routes, gates),
                [whole()] * 5,
                scratch,
                "first_query",
                cost,
            )
        else:
            pieces = [state] + [shifted(state, l) for l in range(1, low)]
            own_q, states = call(
                functools.partial(order_kernel, head_dim, low),
                (q_shape, x_shape),
                (me, *pieces, attn_gain, query_w),
                [smem] + [whole()] * (low + 2),
                scratch,
                "order_query",
                cost,
            )
        c_shape = jax.ShapeDtypeStruct((own * heads, head_dim), BF16)
        cost = (4 * own * heads * places * head_dim, 4 * places * head_dim)
        queries = swapped(own_q.reshape(devices, -1, head_dim)).reshape(-1, head_dim)
        if step == 0:
            context, shares = call(
                functools.partial(first_attention_kernel, own),
                (c_shape, jax.ShapeDtypeStruct((rows, LANES), F32)),
                (pick, queries, keys, values, lengths, *first_tables),
                [whole()] * 4 + [smem] + [whole()] * 3,
                [],
                "first_attention",
                cost,
            )
        else:
            context = call(
                functools.partial(attention_kernel, step, own),
                c_shape,
                (queries, keys, values, lengths, *tables),
                [whole()] * 3 + [smem] + [whole()] * 3,
                [],
                "attention",
                cost,
            )
        contexts = everyones(context)
        columns = call(
            functools.partial(out_kernel, heads),
            jax.ShapeDtypeStruct((devices, rows, part), BF16),
            (contexts.reshape(rows * heads, head_dim), out_w),
            [whole()] * 2,
            [pltpu.VMEM((rows * heads, head_dim), F32), pltpu.VMEM((rows, heads * head_dim), BF16)],
            "attention_out",
            (2 * rows * width * part, 2 * width * part),
        )
        attended = swapped(columns)
        operands = (me, attended, states, ffn_gain, gate_w, up_w, down_w, shares)
        specs = [smem] + [whole()] * 7
        scratch = [pltpu.VMEM((rows, width), F32)]
        cost = (6 * rows * width * hidden, 6 * width * hidden)
        if step + 1 == STEPS:
            half_out, middle = call(
                functools.partial(expert_kernel, step), (x_shape, m_shape), operands, specs, scratch, "experts", cost
            )
            state = call(
                combine_kernel,
                jax.ShapeDtypeStruct((own, width), BF16),
                (swapped(half_out), middle),
                [whole()] * 2,
                [],
                "combine",
                (rows * width, 4 * rows * width),
            )
        else:
            *pieces, middle = call(
                functools.partial(sending_kernel, step, low),
                (slots,) * low + (m_shape,),
                operands,
                specs,
                scratch + [pltpu.VMEM((devices, own, width), BF16)],
                "experts_sending",
                cost,
            )
            pieces = [pieces[0]] + [shifted(pieces[l], l) for l in range(low - 1, 0, -1)]
            part_sums = call(
                partial_kernel, slots, (middle, *pieces), [whole()] * (low + 1), [], "partial",
                (rows * width, 4 * rows * width),
            )
            parts = [shifted(part_sums, h * low, 1) for h in range(high)]
            state = call(
                join_kernel, slots, tuple(parts), [whole()] * high, [], "join", (rows * width, 4 * rows * width)
            )
    return state[None]


def solution(mesh):
    return jax.shard_map(
        body,
        mesh=mesh,
        in_specs=(
            P("section", "expert", None),
            P("section", None),
            P("section", None, "expert"),
            P("section", None, "expert"),
            P("section", None, "expert", None, None, None),
            P("section", None, "expert", None, None, None),
            P("section", None, "expert"),
            P("section", None),
            P("section", "expert", None, None),
            P("section", "expert", None, None),
            P("section", "expert", None, None),
            P("section", None, "expert", None),
            P("section", None, "expert", None),
        ),
        out_specs=P("section", "expert", None),
        check_vma=False,
    )
```

```python
import functools
import math

import jax
import jax.numpy as jnp
import numpy as np
from jax import lax
from jax.experimental import pallas as pl
from jax.experimental.pallas import tpu as pltpu
from jax.sharding import PartitionSpec as P

STEPS = 3
EPS = 1e-06
LIMIT = 24 * 1024 * 1024
EXCHANGE = 20 * 1000 * 1000 * 1000
LANES = 128
EXTRA = 16
LOG2E = math.log2(math.e)
F32 = jnp.float32
BF16 = jnp.bfloat16


def shifted(array, mask, sections=0):
    stages, devices = lax.axis_size("section"), lax.axis_size("expert")
    pairs = [
        (s * devices + e, (s + sections) % stages * devices + (e ^ mask))
        for s in range(stages)
        for e in range(devices)
    ]
    return lax.ppermute(array, ("section", "expert"), pairs)


def split(devices):
    low = 1
    while low * low < devices:
        low *= 2
    return low, devices // low


def swapped(blocks):
    return lax.all_to_all(blocks, "expert", split_axis=0, concat_axis=0, tiled=True)


def everyones(array):
    devices = lax.axis_size("expert")
    return swapped(jnp.broadcast_to(array[None], (devices,) + array.shape))


def whole(memory_space=pltpu.VMEM):
    return pl.BlockSpec(memory_space=memory_space)


def call(kernel, out, operands, specs, scratch, name, cost):
    single = not isinstance(out, tuple)
    return pl.pallas_call(
        kernel,
        out_shape=out,
        in_specs=specs,
        out_specs=whole() if single else tuple(whole() for _ in out),
        scratch_shapes=scratch,
        compiler_params=pltpu.CompilerParams(vmem_limit_bytes=LIMIT),
        cost_estimate=pl.CostEstimate(flops=cost[0] + EXCHANGE, bytes_accessed=cost[1], transcendentals=0),
        name=name,
    )(*operands)


def add_tiles(totals, left, right, depth, tile=128):
    for at in range(0, right.shape[1], tile):
        part = jnp.dot(left, right[depth, at:at + tile], preferred_element_type=F32)
        totals[at] = totals[at] + part if at in totals else part


def add_squares(totals, values):
    for at in range(0, values.shape[1], 128):
        totals = totals + values[:, at:at + 128] * values[:, at:at + 128]
    return totals


def spread_kernel(x_ref, o_ref):
    for i in range(o_ref.shape[0]):
        o_ref[i] = x_ref[...]


def coded_shares(routes_ref, gates_ref, experts):
    own = routes_ref.shape[2]
    lane = lax.broadcasted_iota(jnp.int32, (EXTRA, LANES), 1)
    row = lax.broadcasted_iota(jnp.int32, (EXTRA, LANES), 0)
    line = lax.broadcasted_iota(jnp.int32, (EXTRA, own), 0)
    column = lax.broadcasted_iota(jnp.int32, (EXTRA, own), 1)
    here = (line == column) | (line == column + own) | (line == column + 2 * own)
    shares = jnp.zeros((EXTRA, LANES), F32)
    for step in range(STEPS):
        routes, gates = routes_ref[step], gates_ref[step]
        parts = gates / jnp.sum(gates, axis=0, keepdims=True)
        for e in range(experts):
            share = jnp.sum(jnp.where(routes == e, parts, 0.0), axis=0, keepdims=True)
            share = jnp.sum(jnp.where(here, share, 0.0), axis=1, keepdims=True)
            shares = jnp.where(lane == step * experts + e, share, shares)
    first = shares.astype(BF16).astype(F32)
    second = (shares - first).astype(BF16).astype(F32)
    return jnp.where(row < own, first, jnp.where(row < 2 * own, second, shares - first - second)).astype(BF16)


def first_kernel(head_dim, x_ref, gain_ref, w_ref, routes_ref, gates_ref, q_ref, states, spread):
    query_kernel(head_dim, x_ref, gain_ref, w_ref, None, states, spread)
    devices = q_ref.shape[0]
    count = spread.shape[0] // devices
    coded = coded_shares(routes_ref, gates_ref, devices // 2)
    for i in range(devices):
        q_ref[i, :EXTRA, :] = coded
        q_ref[i, EXTRA:, :] = spread[count * i:count * (i + 1), :].astype(BF16)


def order_kernel(head_dim, low, me_ref, *refs):
    pieces, (gain_ref, w_ref, q_ref, states, x_ref, spread) = refs[:low], refs[low:]
    me = me_ref[0]
    for l, piece in enumerate(pieces):
        for h in range(piece.shape[0]):
            x_ref[me ^ (l + h * low)] = piece[h]
    query_kernel(head_dim, x_ref, gain_ref, w_ref, q_ref, states, spread)


def query_kernel(head_dim, x_ref, gain_ref, w_ref, q_ref, states, spread):
    devices, own, _ = x_ref.shape
    rows, (width, columns) = devices * own, w_ref.shape
    heads = columns // head_dim
    chunk = 512
    totals, squares = {}, jnp.zeros((rows, 128), F32)
    for start in range(0, width, chunk):
        at = slice(start, start + chunk)
        for i in range(devices):
            states[own * i:own * (i + 1), at] = x_ref[i, :, at].astype(F32)
        values = states[:, at]
        squares = add_squares(squares, values)
        add_tiles(totals, (values * gain_ref[:, at].astype(F32)).astype(BF16), w_ref, at, head_dim)
    scale = lax.rsqrt(jnp.sum(squares, axis=-1, keepdims=True) / width + EPS)
    for h in range(heads):
        one = totals[head_dim * h] * scale
        norm = lax.rsqrt(jnp.mean(one * one, axis=-1, keepdims=True) + EPS)
        spread[pl.ds(h, rows, stride=heads), :] = one * norm
    if q_ref is not None:
        q_ref[...] = spread[...].astype(BF16)


def first_attention_kernel(own, pick_ref, q_ref, *refs):
    *rest, c_ref, share_ref, lines = refs
    share_ref[...] = jnp.dot(pick_ref[...], q_ref[...], preferred_element_type=F32)
    attention_kernel(0, own, q_ref, *rest, c_ref, lines)


def attention_kernel(step, own, q_ref, k_ref, v_ref, len_ref, order_ref, line_ref, column_ref, c_ref, lines):
    head_dim = q_ref.shape[1]
    heads = line_ref.shape[0]
    span = column_ref.shape[1]
    q = jnp.dot(order_ref[...], q_ref[...], preferred_element_type=F32).astype(BF16)
    group_of, position = column_ref[0:1, :], column_ref[1:2, :]
    same = group_of == line_ref[...]
    ours = [slice(heads * r, heads * (r + 1)) for r in range(own)]
    keys = [slice(span * r, span * (r + 1)) for r in range(own)]
    scores = [
        lax.dot_general(
            q[ours[r], :], k_ref[step, keys[r], :], (((1,), (1,)), ((), ())), preferred_element_type=F32
        )
        for r in range(own)
    ]
    exps = [
        jnp.where(
            same & (position < len_ref[step, :, r:r + 1]), jnp.exp2(scores[r] * (head_dim ** (-0.5) * LOG2E)), 0.0
        )
        for r in range(own)
    ]
    contexts = [
        jnp.dot(exps[r].astype(BF16), v_ref[step, keys[r], :], preferred_element_type=F32) for r in range(own)
    ]
    for r in range(own):
        lines[ours[r], :] = contexts[r] * (1.0 / jnp.sum(exps[r], axis=-1, keepdims=True))
    for h in range(heads):
        c_ref[:, head_dim * h:head_dim * (h + 1)] = lines[pl.ds(h, own, stride=heads), :].astype(BF16)


def attention_tables(own, heads, local_heads, kv_heads, cache_len):
    group = heads // kv_heads
    row, head = np.divmod(np.arange(own * heads), heads)
    sender, place = head // local_heads, row * local_heads + head % local_heads
    devices, count = heads // local_heads, own * local_heads
    order = np.zeros((own * heads, own * heads), np.float32)
    order[np.arange(own * heads), sender * count + place] = 1.0
    first_order = np.zeros((own * heads, devices * (EXTRA + count)), np.float32)
    first_order[np.arange(own * heads), sender * (EXTRA + count) + EXTRA + place] = 1.0
    pick = np.zeros((devices * own, devices * (EXTRA + count)), np.float32)
    for part in range(3):
        for r in range(own):
            pick[np.arange(devices) * own + r, np.arange(devices) * (EXTRA + count) + part * own + r] = 1.0
    line = (np.arange(heads) // group).astype(np.int32)[:, None]
    position, kv = np.divmod(np.arange(cache_len * kv_heads), kv_heads)
    column = np.zeros((8, cache_len * kv_heads), np.int32)
    column[:2] = kv, position
    asis = jnp.asarray(line), jnp.asarray(column)
    return (jnp.asarray(order, BF16), *asis), (jnp.asarray(first_order, BF16), *asis), jnp.asarray(pick, BF16)


def out_kernel(c_ref, w_ref, o_ref, lines):
    devices, own, width = c_ref.shape
    chunk, total = 512, None
    for start in range(0, width, chunk):
        at = slice(start, start + chunk)
        for i in range(devices):
            lines[own * i:own * (i + 1), at] = c_ref[i, :, at].astype(F32)
        part = jnp.dot(lines[:, at].astype(BF16), w_ref[at, :], preferred_element_type=F32)
        total = part if total is None else total + part
    columns = total.astype(BF16)
    for i in range(devices):
        o_ref[i] = columns


def expert_kernel(step, me_ref, a_ref, x_ref, gain_ref, gate_ref, up_ref, down_ref, share_ref, h_ref, m_ref, middle):
    devices, own, _ = h_ref.shape
    part = a_ref.shape[2]
    width = part * devices
    me = me_ref[0]
    gates, ups, squares = {}, {}, jnp.zeros((devices * own, 128), F32)
    for j in range(devices):
        at = slice(part * j, part * (j + 1))
        values = x_ref[:, at] + a_ref[j].astype(F32)
        middle[:, at] = values
        squares = add_squares(squares, values)
        left = (values * gain_ref[:, at].astype(F32)).astype(BF16)
        add_tiles(gates, left, gate_ref, at)
        add_tiles(ups, left, up_ref, at)
    scale = lax.rsqrt(jnp.sum(squares, axis=-1, keepdims=True) / width + EPS)
    lane = lax.broadcasted_iota(jnp.int32, share_ref.shape, 1)
    mine = lane == step * (devices // 2) + me // 2
    share = jnp.sum(jnp.where(mine, share_ref[...], 0.0), axis=1, keepdims=True)
    active = {}
    for at in gates:
        gate, up = gates[at] * scale, ups[at] * scale
        active[at] = (gate / (1.0 + jnp.exp(-gate)) * up * share).astype(BF16)
    chunk = 512
    for start in range(0, width, chunk):
        piece = None
        for at, left in active.items():
            term = jnp.dot(
                left, down_ref[at:at + left.shape[1], start:start + chunk], preferred_element_type=F32
            )
            piece = term if piece is None else piece + term
        for i in range(devices):
            h_ref[i, :, start:start + chunk] = piece[own * i:own * (i + 1), :].astype(BF16)
    pairs = 8 // own
    block = middle[pl.ds(pl.multiple_of((me // pairs) * 8, 8), 8), :]
    kept = block[0:own, :]
    for p in range(1, pairs):
        kept = jnp.where(me % pairs == p, block[own * p:own * (p + 1), :], kept)
    m_ref[...] = kept


def sending_kernel(step, low, me_ref, *refs):
    pieces, (m_ref, middle, rows) = refs[7:7 + low], refs[7 + low:]
    expert_kernel(step, me_ref, *refs[:7], rows, m_ref, middle)
    me = me_ref[0]
    for l, piece in enumerate(pieces):
        for h in range(piece.shape[0]):
            piece[h] = rows[me ^ (l + h * low)]


def partial_kernel(m_ref, *refs):
    pieces, t_ref = refs[:-1], refs[-1]
    for h in range(t_ref.shape[0]):
        total = m_ref[...] if h == 0 else jnp.zeros(m_ref.shape, F32)
        for piece in pieces:
            total = total + piece[h].astype(F32)
        t_ref[h] = total.astype(BF16)


def join_kernel(*refs):
    parts, x_ref = refs[:-1], refs[-1]
    for g in range(len(parts)):
        total = parts[0][g].astype(F32)
        for h in range(1, len(parts)):
            total = total + parts[h][h ^ g].astype(F32)
        x_ref[g] = total.astype(BF16)


def combine_kernel(r_ref, m_ref, o_ref):
    total = m_ref[...]
    for i in range(r_ref.shape[0]):
        total = total + r_ref[i].astype(F32)
    o_ref[...] = total.astype(BF16)


def body(
    hidden_in,
    attn_gain,
    w_query,
    w_out,
    key_cache,
    value_cache,
    lengths,
    ffn_gain,
    w_gate,
    w_up,
    w_down,
    routes,
    gates,
):
    devices = lax.axis_size("expert")
    me = lax.axis_index("expert").astype(jnp.int32).reshape(1)
    own, width = hidden_in.shape[1:]
    rows = own * devices
    cache_len, kv_heads, head_dim = key_cache.shape[3:]
    query_w, out_w = w_query[0], w_out[0]
    part = query_w.shape[1]
    local_heads = part // head_dim
    heads = local_heads * devices
    gate_w, up_w, down_w = w_gate[0, 0], w_up[0, 0], w_down[0, 0]
    hidden = gate_w.shape[1]
    places = own * cache_len * kv_heads
    keys = key_cache.reshape(STEPS, places, head_dim)
    values = value_cache.reshape(STEPS, places, head_dim)
    routes, gates = routes[0].transpose(0, 2, 1), gates[0].transpose(0, 2, 1)
    lengths = lengths.reshape(STEPS, 1, own)
    tables, first_tables, pick = attention_tables(own, heads, local_heads, kv_heads, cache_len)
    low, high = split(devices)
    smem = whole(pltpu.SMEM)
    q_shape = jax.ShapeDtypeStruct((rows * local_heads, head_dim), BF16)
    x_shape = jax.ShapeDtypeStruct((devices, own, width), BF16)
    states_shape = jax.ShapeDtypeStruct((rows, width), F32)
    m_shape = jax.ShapeDtypeStruct((own, width), F32)
    slots = jax.ShapeDtypeStruct((high, own, width), BF16)
    copies = call(
        spread_kernel,
        x_shape,
        (hidden_in[0],),
        [whole()],
        [],
        "spread",
        (0, 2 * rows * width),
    )
    me, copies = lax.optimization_barrier((me, copies))
    for step in range(STEPS):
        spread = pltpu.VMEM((rows * local_heads, head_dim), F32)
        cost = (2 * rows * width * part, 2 * width * part)
        if step == 0:
            own_q, states = call(
                functools.partial(first_kernel, head_dim),
                (jax.ShapeDtypeStruct((devices, EXTRA + own * local_heads, head_dim), BF16), states_shape),
                (swapped(copies), attn_gain, query_w, routes, gates),
                [whole()] * 5,
                [spread],
                "first_query",
                cost,
            )
        else:
            pieces = [state] + [shifted(state, l) for l in range(1, low)]
            own_q, states = call(
                functools.partial(order_kernel, head_dim, low),
                (q_shape, states_shape),
                (me, *pieces, attn_gain, query_w),
                [smem] + [whole()] * (low + 2),
                [pltpu.VMEM((devices, own, width), BF16), spread],
                "order_query",
                cost,
            )
        c_shape = jax.ShapeDtypeStruct((own, heads * head_dim), BF16)
        by_row = [pltpu.VMEM((own * heads, head_dim), F32)]
        cost = (4 * own * heads * places * head_dim, 4 * places * head_dim)
        queries = swapped(own_q.reshape(devices, -1, head_dim)).reshape(-1, head_dim)
        if step == 0:
            context, shares = call(
                functools.partial(first_attention_kernel, own),
                (c_shape, jax.ShapeDtypeStruct((rows, LANES), F32)),
                (pick, queries, keys, values, lengths, *first_tables),
                [whole()] * 8,
                by_row,
                "first_attention",
                cost,
            )
        else:
            context = call(
                functools.partial(attention_kernel, step, own),
                c_shape,
                (queries, keys, values, lengths, *tables),
                [whole()] * 7,
                by_row,
                "attention",
                cost,
            )
        contexts = everyones(context)
        columns = call(
            out_kernel,
            jax.ShapeDtypeStruct((devices, rows, part), BF16),
            (contexts, out_w),
            [whole()] * 2,
            [pltpu.VMEM((rows, heads * head_dim), F32)],
            "attention_out",
            (2 * rows * width * part, 2 * width * part),
        )
        attended = swapped(columns)
        operands = (me, attended, states, ffn_gain, gate_w, up_w, down_w, shares)
        specs = [smem] + [whole()] * 7
        scratch = [pltpu.VMEM((rows, width), F32)]
        cost = (6 * rows * width * hidden, 6 * width * hidden)
        if step + 1 == STEPS:
            half_out, middle = call(
                functools.partial(expert_kernel, step), (x_shape, m_shape), operands, specs, scratch, "experts", cost
            )
            state = call(
                combine_kernel,
                jax.ShapeDtypeStruct((own, width), BF16),
                (swapped(half_out), middle),
                [whole()] * 2,
                [],
                "combine",
                (rows * width, 4 * rows * width),
            )
        else:
            *pieces, middle = call(
                functools.partial(sending_kernel, step, low),
                (slots,) * low + (m_shape,),
                operands,
                specs,
                scratch + [pltpu.VMEM((devices, own, width), BF16)],
                "experts_sending",
                cost,
            )
            pieces = [pieces[0]] + [shifted(pieces[l], l) for l in range(low - 1, 0, -1)]
            part_sums = call(
                partial_kernel, slots, (middle, *pieces), [whole()] * (low + 1), [], "partial",
                (rows * width, 4 * rows * width),
            )
            parts = [shifted(part_sums, h * low, 1) for h in range(high)]
            state = call(
                join_kernel, slots, tuple(parts), [whole()] * high, [], "join", (rows * width, 4 * rows * width)
            )
    return state[None]


def solution(mesh):
    return jax.shard_map(
        body,
        mesh=mesh,
        in_specs=(
            P("section", "expert", None),
            P("section", None),
            P("section", None, "expert"),
            P("section", None, "expert"),
            P("section", None, "expert", None, None, None),
            P("section", None, "expert", None, None, None),
            P("section", None, "expert"),
            P("section", None),
            P("section", "expert", None, None),
            P("section", "expert", None, None),
            P("section", "expert", None, None),
            P("section", None, "expert", None),
            P("section", None, "expert", None),
        ),
        out_specs=P("section", "expert", None),
        check_vma=False,
    )
```

```python
import functools
import math

import jax
import jax.numpy as jnp
import numpy as np
from jax import lax
from jax.experimental import pallas as pl
from jax.experimental.pallas import tpu as pltpu
from jax.sharding import PartitionSpec as P

STEPS = 3
EPS = 1e-06
LIMIT = 24 * 1024 * 1024
EXCHANGE = 20 * 1000 * 1000 * 1000
LANES = 128
EXTRA = 16
LOG2E = math.log2(math.e)
F32 = jnp.float32
BF16 = jnp.bfloat16


def shifted(array, mask, sections=0):
    stages, devices = lax.axis_size("section"), lax.axis_size("expert")
    pairs = [
        (s * devices + e, (s + sections) % stages * devices + (e ^ mask))
        for s in range(stages)
        for e in range(devices)
    ]
    return lax.ppermute(array, ("section", "expert"), pairs)


def split(devices):
    low = 1
    while low * low < devices:
        low *= 2
    return low, devices // low


def swapped(blocks):
    return lax.all_to_all(blocks, "expert", split_axis=0, concat_axis=0, tiled=True)


def everyones(array):
    devices = lax.axis_size("expert")
    return swapped(jnp.broadcast_to(array[None], (devices,) + array.shape))


def whole(memory_space=pltpu.VMEM):
    return pl.BlockSpec(memory_space=memory_space)


def call(kernel, out, operands, specs, scratch, name, cost):
    single = not isinstance(out, tuple)
    return pl.pallas_call(
        kernel,
        out_shape=out,
        in_specs=specs,
        out_specs=whole() if single else tuple(whole() for _ in out),
        scratch_shapes=scratch,
        compiler_params=pltpu.CompilerParams(vmem_limit_bytes=LIMIT),
        cost_estimate=pl.CostEstimate(flops=cost[0] + EXCHANGE, bytes_accessed=cost[1], transcendentals=0),
        name=name,
    )(*operands)


def add_tiles(totals, left, right, depth, tile=128):
    for at in range(0, right.shape[1], tile):
        part = jnp.dot(left, right[depth, at:at + tile], preferred_element_type=F32)
        totals[at] = totals[at] + part if at in totals else part


def add_squares(totals, values):
    for at in range(0, values.shape[1], 128):
        totals = totals + values[:, at:at + 128] * values[:, at:at + 128]
    return totals


def spread_kernel(x_ref, o_ref):
    for i in range(o_ref.shape[0]):
        o_ref[i] = x_ref[...]


def coded_shares(routes_ref, gates_ref, experts):
    own = routes_ref.shape[2]
    lane = lax.broadcasted_iota(jnp.int32, (EXTRA, LANES), 1)
    row = lax.broadcasted_iota(jnp.int32, (EXTRA, LANES), 0)
    line = lax.broadcasted_iota(jnp.int32, (EXTRA, own), 0)
    column = lax.broadcasted_iota(jnp.int32, (EXTRA, own), 1)
    here = (line == column) | (line == column + own) | (line == column + 2 * own)
    shares = jnp.zeros((EXTRA, LANES), F32)
    for step in range(STEPS):
        routes, gates = routes_ref[step], gates_ref[step]
        parts = gates / jnp.sum(gates, axis=0, keepdims=True)
        for e in range(experts):
            share = jnp.sum(jnp.where(routes == e, parts, 0.0), axis=0, keepdims=True)
            share = jnp.sum(jnp.where(here, share, 0.0), axis=1, keepdims=True)
            shares = jnp.where(lane == step * experts + e, share, shares)
    first = shares.astype(BF16).astype(F32)
    second = (shares - first).astype(BF16).astype(F32)
    return jnp.where(row < own, first, jnp.where(row < 2 * own, second, shares - first - second)).astype(BF16)


def first_kernel(head_dim, x_ref, gain_ref, w_ref, routes_ref, gates_ref, q_ref, states, spread):
    query_kernel(head_dim, x_ref, gain_ref, w_ref, None, states, spread)
    devices = q_ref.shape[0]
    count = spread.shape[0] // devices
    coded = coded_shares(routes_ref, gates_ref, devices // 2)
    for i in range(devices):
        q_ref[i, :EXTRA, :] = coded
        q_ref[i, EXTRA:, :] = spread[count * i:count * (i + 1), :].astype(BF16)


def order_kernel(head_dim, low, me_ref, *refs):
    pieces, (gain_ref, w_ref, q_ref, states, x_ref, spread) = refs[:low], refs[low:]
    me = me_ref[0]
    for l, piece in enumerate(pieces):
        for h in range(piece.shape[0]):
            x_ref[me ^ (l + h * low)] = piece[h]
    query_kernel(head_dim, x_ref, gain_ref, w_ref, q_ref, states, spread)


def query_kernel(head_dim, x_ref, gain_ref, w_ref, q_ref, states, spread):
    devices, own, _ = x_ref.shape
    rows, (width, columns) = devices * own, w_ref.shape
    heads = columns // head_dim
    chunk = 512
    totals, squares = {}, jnp.zeros((rows, 128), F32)
    for start in range(0, width, chunk):
        at = slice(start, start + chunk)
        for i in range(devices):
            states[own * i:own * (i + 1), at] = x_ref[i, :, at].astype(F32)
        values = states[:, at]
        squares = add_squares(squares, values)
        add_tiles(totals, (values * gain_ref[:, at].astype(F32)).astype(BF16), w_ref, at, head_dim)
    scale = lax.rsqrt(jnp.sum(squares, axis=-1, keepdims=True) / width + EPS)
    for h in range(heads):
        one = totals[head_dim * h] * scale
        norm = lax.rsqrt(jnp.mean(one * one, axis=-1, keepdims=True) + EPS)
        spread[pl.ds(h, rows, stride=heads), :] = one * norm
    if q_ref is not None:
        q_ref[...] = spread[...].astype(BF16)


def first_attention_kernel(own, pick_ref, q_ref, *refs):
    *rest, c_ref, share_ref, lines = refs
    share_ref[...] = jnp.dot(pick_ref[...], q_ref[...], preferred_element_type=F32)
    attention_kernel(0, own, q_ref, *rest, c_ref, lines)


def attention_kernel(step, own, q_ref, k_ref, v_ref, len_ref, order_ref, line_ref, column_ref, c_ref, lines):
    head_dim = q_ref.shape[1]
    heads = line_ref.shape[0]
    span = column_ref.shape[1]
    q = jnp.dot(order_ref[...], q_ref[...], preferred_element_type=F32).astype(BF16)
    group_of, position = column_ref[0:1, :], column_ref[1:2, :]
    same = group_of == line_ref[...]
    ours = [slice(heads * r, heads * (r + 1)) for r in range(own)]
    keys = [slice(span * r, span * (r + 1)) for r in range(own)]
    scores = [
        lax.dot_general(
            q[ours[r], :], k_ref[step, keys[r], :], (((1,), (1,)), ((), ())), preferred_element_type=F32
        )
        for r in range(own)
    ]
    exps = [
        jnp.where(
            same & (position < len_ref[step, :, r:r + 1]), jnp.exp2(scores[r] * (head_dim ** (-0.5) * LOG2E)), 0.0
        )
        for r in range(own)
    ]
    contexts = [
        jnp.dot(exps[r].astype(BF16), v_ref[step, keys[r], :], preferred_element_type=F32) for r in range(own)
    ]
    for r in range(own):
        lines[ours[r], :] = contexts[r] * (1.0 / jnp.sum(exps[r], axis=-1, keepdims=True))
    for h in range(heads):
        c_ref[:, head_dim * h:head_dim * (h + 1)] = lines[pl.ds(h, own, stride=heads), :].astype(BF16)


def attention_tables(own, heads, local_heads, kv_heads, cache_len):
    group = heads // kv_heads
    row, head = np.divmod(np.arange(own * heads), heads)
    sender, place = head // local_heads, row * local_heads + head % local_heads
    devices, count = heads // local_heads, own * local_heads
    order = np.zeros((own * heads, own * heads), np.float32)
    order[np.arange(own * heads), sender * count + place] = 1.0
    first_order = np.zeros((own * heads, devices * (EXTRA + count)), np.float32)
    first_order[np.arange(own * heads), sender * (EXTRA + count) + EXTRA + place] = 1.0
    pick = np.zeros((devices * own, devices * (EXTRA + count)), np.float32)
    for part in range(3):
        for r in range(own):
            pick[np.arange(devices) * own + r, np.arange(devices) * (EXTRA + count) + part * own + r] = 1.0
    line = (np.arange(heads) // group).astype(np.int32)[:, None]
    position, kv = np.divmod(np.arange(cache_len * kv_heads), kv_heads)
    column = np.zeros((8, cache_len * kv_heads), np.int32)
    column[:2] = kv, position
    asis = jnp.asarray(line), jnp.asarray(column)
    return (jnp.asarray(order, BF16), *asis), (jnp.asarray(first_order, BF16), *asis), jnp.asarray(pick, BF16)


def out_kernel(c_ref, w_ref, o_ref, lines):
    devices, own, width = c_ref.shape
    chunk, totals = 512, {}
    for start in range(0, width, chunk):
        at = slice(start, start + chunk)
        for i in range(devices):
            lines[own * i:own * (i + 1), at] = c_ref[i, :, at].astype(F32)
        add_tiles(totals, lines[:, at].astype(BF16), w_ref, at)
    for at, total in totals.items():
        columns = total.astype(BF16)
        for i in range(devices):
            o_ref[i, :, at:at + columns.shape[1]] = columns


def expert_kernel(step, me_ref, a_ref, x_ref, gain_ref, gate_ref, up_ref, down_ref, share_ref, h_ref, m_ref, middle):
    devices, own, _ = h_ref.shape
    part = a_ref.shape[2]
    width = part * devices
    me = me_ref[0]
    gates, ups, squares = {}, {}, jnp.zeros((devices * own, 128), F32)
    for j in range(devices):
        at = slice(part * j, part * (j + 1))
        values = x_ref[:, at] + a_ref[j].astype(F32)
        middle[:, at] = values
        squares = add_squares(squares, values)
        left = (values * gain_ref[:, at].astype(F32)).astype(BF16)
        add_tiles(gates, left, gate_ref, at)
        add_tiles(ups, left, up_ref, at)
    scale = lax.rsqrt(jnp.sum(squares, axis=-1, keepdims=True) / width + EPS)
    lane = lax.broadcasted_iota(jnp.int32, share_ref.shape, 1)
    mine = lane == step * (devices // 2) + me // 2
    share = jnp.sum(jnp.where(mine, share_ref[...], 0.0), axis=1, keepdims=True)
    active = {}
    for at in gates:
        gate, up = gates[at] * scale, ups[at] * scale
        active[at] = (gate / (1.0 + jnp.exp(-gate)) * up * share).astype(BF16)
    chunk = 512
    for start in range(0, width, chunk):
        piece = None
        for at, left in active.items():
            term = jnp.dot(
                left, down_ref[at:at + left.shape[1], start:start + chunk], preferred_element_type=F32
            )
            piece = term if piece is None else piece + term
        for i in range(devices):
            h_ref[i, :, start:start + chunk] = piece[own * i:own * (i + 1), :].astype(BF16)
    pairs = 8 // own
    block = middle[pl.ds(pl.multiple_of((me // pairs) * 8, 8), 8), :]
    kept = block[0:own, :]
    for p in range(1, pairs):
        kept = jnp.where(me % pairs == p, block[own * p:own * (p + 1), :], kept)
    m_ref[...] = kept


def sending_kernel(step, low, me_ref, *refs):
    pieces, (m_ref, middle, rows) = refs[7:7 + low], refs[7 + low:]
    expert_kernel(step, me_ref, *refs[:7], rows, m_ref, middle)
    me = me_ref[0]
    for l, piece in enumerate(pieces):
        for h in range(piece.shape[0]):
            piece[h] = rows[me ^ (l + h * low)]


def partial_kernel(m_ref, *refs):
    pieces, t_ref = refs[:-1], refs[-1]
    for h in range(t_ref.shape[0]):
        total = m_ref[...] if h == 0 else jnp.zeros(m_ref.shape, F32)
        for piece in pieces:
            total = total + piece[h].astype(F32)
        t_ref[h] = total.astype(BF16)


def join_kernel(*refs):
    parts, x_ref = refs[:-1], refs[-1]
    for g in range(len(parts)):
        total = parts[0][g].astype(F32)
        for h in range(1, len(parts)):
            total = total + parts[h][h ^ g].astype(F32)
        x_ref[g] = total.astype(BF16)


def combine_kernel(r_ref, m_ref, o_ref):
    total = m_ref[...]
    for i in range(r_ref.shape[0]):
        total = total + r_ref[i].astype(F32)
    o_ref[...] = total.astype(BF16)


def body(
    hidden_in,
    attn_gain,
    w_query,
    w_out,
    key_cache,
    value_cache,
    lengths,
    ffn_gain,
    w_gate,
    w_up,
    w_down,
    routes,
    gates,
):
    devices = lax.axis_size("expert")
    me = lax.axis_index("expert").astype(jnp.int32).reshape(1)
    own, width = hidden_in.shape[1:]
    rows = own * devices
    cache_len, kv_heads, head_dim = key_cache.shape[3:]
    query_w, out_w = w_query[0], w_out[0]
    part = query_w.shape[1]
    local_heads = part // head_dim
    heads = local_heads * devices
    gate_w, up_w, down_w = w_gate[0, 0], w_up[0, 0], w_down[0, 0]
    hidden = gate_w.shape[1]
    places = own * cache_len * kv_heads
    keys = key_cache.reshape(STEPS, places, head_dim)
    values = value_cache.reshape(STEPS, places, head_dim)
    routes, gates = routes[0].transpose(0, 2, 1), gates[0].transpose(0, 2, 1)
    lengths = lengths.reshape(STEPS, 1, own)
    tables, first_tables, pick = attention_tables(own, heads, local_heads, kv_heads, cache_len)
    low, high = split(devices)
    smem = whole(pltpu.SMEM)
    q_shape = jax.ShapeDtypeStruct((rows * local_heads, head_dim), BF16)
    x_shape = jax.ShapeDtypeStruct((devices, own, width), BF16)
    states_shape = jax.ShapeDtypeStruct((rows, width), F32)
    m_shape = jax.ShapeDtypeStruct((own, width), F32)
    slots = jax.ShapeDtypeStruct((high, own, width), BF16)
    copies = call(
        spread_kernel,
        x_shape,
        (hidden_in[0],),
        [whole()],
        [],
        "spread",
        (0, 2 * rows * width),
    )
    me, copies = lax.optimization_barrier((me, copies))
    for step in range(STEPS):
        spread = pltpu.VMEM((rows * local_heads, head_dim), F32)
        cost = (2 * rows * width * part, 2 * width * part)
        if step == 0:
            own_q, states = call(
                functools.partial(first_kernel, head_dim),
                (jax.ShapeDtypeStruct((devices, EXTRA + own * local_heads, head_dim), BF16), states_shape),
                (swapped(copies), attn_gain, query_w, routes, gates),
                [whole()] * 5,
                [spread],
                "first_query",
                cost,
            )
        else:
            pieces = [state] + [shifted(state, l) for l in range(1, low)]
            own_q, states = call(
                functools.partial(order_kernel, head_dim, low),
                (q_shape, states_shape),
                (me, *pieces, attn_gain, query_w),
                [smem] + [whole()] * (low + 2),
                [pltpu.VMEM((devices, own, width), BF16), spread],
                "order_query",
                cost,
            )
        c_shape = jax.ShapeDtypeStruct((own, heads * head_dim), BF16)
        by_row = [pltpu.VMEM((own * heads, head_dim), F32)]
        cost = (4 * own * heads * places * head_dim, 4 * places * head_dim)
        queries = swapped(own_q.reshape(devices, -1, head_dim)).reshape(-1, head_dim)
        if step == 0:
            context, shares = call(
                functools.partial(first_attention_kernel, own),
                (c_shape, jax.ShapeDtypeStruct((rows, LANES), F32)),
                (pick, queries, keys, values, lengths, *first_tables),
                [whole()] * 8,
                by_row,
                "first_attention",
                cost,
            )
        else:
            context = call(
                functools.partial(attention_kernel, step, own),
                c_shape,
                (queries, keys, values, lengths, *tables),
                [whole()] * 7,
                by_row,
                "attention",
                cost,
            )
        contexts = everyones(context)
        columns = call(
            out_kernel,
            jax.ShapeDtypeStruct((devices, rows, part), BF16),
            (contexts, out_w),
            [whole()] * 2,
            [pltpu.VMEM((rows, heads * head_dim), F32)],
            "attention_out",
            (2 * rows * width * part, 2 * width * part),
        )
        attended = swapped(columns)
        operands = (me, attended, states, ffn_gain, gate_w, up_w, down_w, shares)
        specs = [smem] + [whole()] * 7
        scratch = [pltpu.VMEM((rows, width), F32)]
        cost = (6 * rows * width * hidden, 6 * width * hidden)
        if step + 1 == STEPS:
            half_out, middle = call(
                functools.partial(expert_kernel, step), (x_shape, m_shape), operands, specs, scratch, "experts", cost
            )
            state = call(
                combine_kernel,
                jax.ShapeDtypeStruct((own, width), BF16),
                (swapped(half_out), middle),
                [whole()] * 2,
                [],
                "combine",
                (rows * width, 4 * rows * width),
            )
        else:
            *pieces, middle = call(
                functools.partial(sending_kernel, step, low),
                (slots,) * low + (m_shape,),
                operands,
                specs,
                scratch + [pltpu.VMEM((devices, own, width), BF16)],
                "experts_sending",
                cost,
            )
            pieces = [pieces[0]] + [shifted(pieces[l], l) for l in range(low - 1, 0, -1)]
            part_sums = call(
                partial_kernel, slots, (middle, *pieces), [whole()] * (low + 1), [], "partial",
                (rows * width, 4 * rows * width),
            )
            parts = [shifted(part_sums, h * low, 1) for h in range(high)]
            state = call(
                join_kernel, slots, tuple(parts), [whole()] * high, [], "join", (rows * width, 4 * rows * width)
            )
    return state[None]


def solution(mesh):
    return jax.shard_map(
        body,
        mesh=mesh,
        in_specs=(
            P("section", "expert", None),
            P("section", None),
            P("section", None, "expert"),
            P("section", None, "expert"),
            P("section", None, "expert", None, None, None),
            P("section", None, "expert", None, None, None),
            P("section", None, "expert"),
            P("section", None),
            P("section", "expert", None, None),
            P("section", "expert", None, None),
            P("section", "expert", None, None),
            P("section", None, "expert", None),
            P("section", None, "expert", None),
        ),
        out_specs=P("section", "expert", None),
        check_vma=False,
    )
```

```python
import functools
import math

import jax
import jax.numpy as jnp
import numpy as np
from jax import lax
from jax.experimental import pallas as pl
from jax.experimental.pallas import tpu as pltpu
from jax.sharding import PartitionSpec as P

STEPS = 3
EPS = 1e-06
LIMIT = 24 * 1024 * 1024
EXCHANGE = 20 * 1000 * 1000 * 1000
LANES = 128
EXTRA = 16
LOG2E = math.log2(math.e)
F32 = jnp.float32
BF16 = jnp.bfloat16


def shifted(array, mask, sections=0):
    stages, devices = lax.axis_size("section"), lax.axis_size("expert")
    pairs = [
        (s * devices + e, (s + sections) % stages * devices + (e ^ mask))
        for s in range(stages)
        for e in range(devices)
    ]
    return lax.ppermute(array, ("section", "expert"), pairs)


def split(devices):
    low = 1
    while low * low < devices:
        low *= 2
    return low, devices // low


def swapped(blocks):
    return lax.all_to_all(blocks, "expert", split_axis=0, concat_axis=0, tiled=True)


def everyones(array):
    devices = lax.axis_size("expert")
    return swapped(jnp.broadcast_to(array[None], (devices,) + array.shape))


def whole(memory_space=pltpu.VMEM):
    return pl.BlockSpec(memory_space=memory_space)


def call(kernel, out, operands, specs, scratch, name, cost, exchange=EXCHANGE):
    single = not isinstance(out, tuple)
    return pl.pallas_call(
        kernel,
        out_shape=out,
        in_specs=specs,
        out_specs=whole() if single else tuple(whole() for _ in out),
        scratch_shapes=scratch,
        compiler_params=pltpu.CompilerParams(vmem_limit_bytes=LIMIT),
        cost_estimate=pl.CostEstimate(flops=cost[0] + exchange, bytes_accessed=cost[1], transcendentals=0),
        name=name,
    )(*operands)


def add_tiles(totals, left, right, depth, tile=128):
    for at in range(0, right.shape[1], tile):
        part = jnp.dot(left, right[depth, at:at + tile], preferred_element_type=F32)
        totals[at] = totals[at] + part if at in totals else part


def add_squares(totals, values):
    for at in range(0, values.shape[1], 128):
        totals = totals + values[:, at:at + 128] * values[:, at:at + 128]
    return totals


def spread_kernel(x_ref, o_ref):
    for i in range(o_ref.shape[0]):
        o_ref[i] = x_ref[...]


def coded_shares(routes_ref, gates_ref, experts):
    own = routes_ref.shape[2]
    lane = lax.broadcasted_iota(jnp.int32, (EXTRA, LANES), 1)
    row = lax.broadcasted_iota(jnp.int32, (EXTRA, LANES), 0)
    line = lax.broadcasted_iota(jnp.int32, (EXTRA, own), 0)
    column = lax.broadcasted_iota(jnp.int32, (EXTRA, own), 1)
    here = (line == column) | (line == column + own) | (line == column + 2 * own)
    shares = jnp.zeros((EXTRA, LANES), F32)
    for step in range(STEPS):
        routes, gates = routes_ref[step], gates_ref[step]
        parts = gates / jnp.sum(gates, axis=0, keepdims=True)
        for e in range(experts):
            share = jnp.sum(jnp.where(routes == e, parts, 0.0), axis=0, keepdims=True)
            share = jnp.sum(jnp.where(here, share, 0.0), axis=1, keepdims=True)
            shares = jnp.where(lane == step * experts + e, share, shares)
    first = shares.astype(BF16).astype(F32)
    second = (shares - first).astype(BF16).astype(F32)
    return jnp.where(row < own, first, jnp.where(row < 2 * own, second, shares - first - second)).astype(BF16)


def first_kernel(head_dim, x_ref, gain_ref, w_ref, routes_ref, gates_ref, q_ref, states, spread):
    query_kernel(head_dim, x_ref, gain_ref, w_ref, None, states, spread)
    devices = q_ref.shape[0]
    count = spread.shape[0] // devices
    coded = coded_shares(routes_ref, gates_ref, devices // 2)
    for i in range(devices):
        q_ref[i, :EXTRA, :] = coded
        q_ref[i, EXTRA:, :] = spread[count * i:count * (i + 1), :].astype(BF16)


def order_kernel(head_dim, low, me_ref, *refs):
    pieces, (gain_ref, w_ref, q_ref, states, x_ref, spread) = refs[:low], refs[low:]
    me = me_ref[0]
    for l, piece in enumerate(pieces):
        for h in range(piece.shape[0]):
            x_ref[me ^ (l + h * low)] = piece[h]
    query_kernel(head_dim, x_ref, gain_ref, w_ref, q_ref, states, spread)


def head_queries(head_dim, x_ref, gain_ref, w_ref, states):
    devices, own, _ = x_ref.shape
    rows, (width, columns) = devices * own, w_ref.shape
    chunk = 512
    totals, squares = {}, jnp.zeros((rows, 128), F32)
    for start in range(0, width, chunk):
        at = slice(start, start + chunk)
        for i in range(devices):
            states[own * i:own * (i + 1), at] = x_ref[i, :, at].astype(F32)
        values = states[:, at]
        squares = add_squares(squares, values)
        add_tiles(totals, (values * gain_ref[:, at].astype(F32)).astype(BF16), w_ref, at, head_dim)
    scale = lax.rsqrt(jnp.sum(squares, axis=-1, keepdims=True) / width + EPS)
    queries = []
    for h in range(columns // head_dim):
        one = totals[head_dim * h] * scale
        queries.append(one * lax.rsqrt(jnp.mean(one * one, axis=-1, keepdims=True) + EPS))
    return queries


def query_kernel(head_dim, x_ref, gain_ref, w_ref, q_ref, states, spread):
    queries = head_queries(head_dim, x_ref, gain_ref, w_ref, states)
    for h, one in enumerate(queries):
        spread[pl.ds(h, one.shape[0], stride=len(queries)), :] = one
    if q_ref is not None:
        q_ref[...] = spread[...].astype(BF16)


def halves_kernel(head_dim, low, me_ref, *refs):
    pieces, refs = refs[:low], refs[low:]
    (gain_ref, w_ref), outs, (states, x_ref, spread) = refs[:2], refs[2:2 + low], refs[2 + low:]
    me = me_ref[0]
    for l, piece in enumerate(pieces):
        for h in range(piece.shape[0]):
            x_ref[me ^ (l + h * low)] = piece[h]
    devices, own, _ = x_ref.shape
    for h, one in enumerate(head_queries(head_dim, x_ref, gain_ref, w_ref, states)):
        for i in range(devices):
            spread[i, own * h:own * (h + 1), :] = one[own * i:own * (i + 1), :]
    for l, out in enumerate(outs):
        for g in range(out.shape[0]):
            out[g] = spread[(me % low ^ l) + g * low].astype(BF16)


def cache_kernel(own, kv_heads, me_ref, len_ref, k_ref, v_ref, *refs):
    *blocks, wide = refs
    half = kv_heads // 2
    first = jnp.where(me_ref[0] >= kv_heads, 0, half)
    span = k_ref.shape[1] // kv_heads
    cache = span // own
    line = lax.broadcasted_iota(jnp.int32, (EXTRA, LANES), 0)
    place = lax.broadcasted_iota(jnp.int32, (EXTRA, LANES), 1) + line * LANES
    for step, block in enumerate(blocks, 1):
        at = 0
        for ref in (k_ref, v_ref):
            wide[...] = ref[step].astype(F32)
            for j in range(half):
                block[at:at + span, :] = wide[pl.ds(first + j, span, stride=kv_heads), :].astype(BF16)
                at += span
        valid = jnp.zeros((EXTRA, LANES), F32)
        for r in range(own):
            inside = (place >= r * cache) & (place < r * cache + len_ref[step, :, r:r + 1])
            valid = jnp.where(inside, 1.0, valid)
        block[at:, :] = valid.astype(BF16)


def softmax_times(scores, valid, head_dim, values):
    exps = jnp.where(valid, jnp.exp2(scores * (head_dim ** (-0.5) * LOG2E)), 0.0)
    context = jnp.dot(exps.astype(BF16), values, preferred_element_type=F32)
    return context * (1.0 / jnp.sum(exps, axis=-1, keepdims=True))


def products(queries, keys):
    return lax.dot_general(queries, keys, (((1,), (1,)), ((), ())), preferred_element_type=F32)


def half_attention_kernel(step, own, kv_heads, me_ref, *refs):
    low = len(refs) - 6
    pieces, (k_ref, v_ref, len_ref, pair_ref, c_ref, q_ref) = refs[:low], refs[low:]
    me = me_ref[0]
    mine = jnp.where(me >= low, 1, 0)
    half = kv_heads // 2
    count, head_dim = pieces[0].shape[1:]
    for l, piece in enumerate(pieces):
        for g in range(2):
            q_ref[g, me % low ^ l] = piece[g]
    rows = low * count
    span = k_ref.shape[1] // kv_heads
    cache = span // own
    q = q_ref[mine].reshape(rows, head_dim)
    line = lax.broadcasted_iota(jnp.int32, (rows, 1), 0)
    place = lax.broadcasted_iota(jnp.int32, (1, span * kv_heads), 1)
    of_row = place // (cache * kv_heads)
    length = jnp.zeros(place.shape, jnp.int32)
    for r in range(own):
        length = jnp.where(of_row == r, len_ref[step, :, r:r + 1], length)
    key_of = jnp.where(place // kv_heads % cache < length, of_row * kv_heads + place % kv_heads, -1)
    key_for = line % own * kv_heads + line // (rows // half) + half * mine
    scores = products(q, k_ref[step])
    other = q_ref[1 - mine].reshape(rows, head_dim)
    part = rows // half
    ends = pair_ref[2 * half * span:, :].astype(F32)
    valid = jnp.concatenate([ends[g:g + 1, :] for g in range(span // LANES)], axis=1) > 0.0
    line = lax.broadcasted_iota(jnp.int32, (part, 1), 0)
    place = lax.broadcasted_iota(jnp.int32, (1, span), 1)
    theirs = (line % own == place // cache) & valid
    others = [products(other[part * j:part * (j + 1), :], pair_ref[span * j:span * (j + 1), :]) for j in range(half)]
    own_context = softmax_times(scores, key_of == key_for, head_dim, v_ref[step])
    contexts = [
        softmax_times(others[j], theirs, head_dim, pair_ref[span * (half + j):span * (half + j + 1), :])
        for j in range(half)
    ]
    heads = part // own
    for h in range(rows // own):
        at = slice(head_dim * h, head_dim * (h + 1))
        c_ref[mine, :, at] = own_context[own * h:own * (h + 1), :].astype(BF16)
        j, inside = h // heads, h % heads
        c_ref[1 - mine, :, at] = contexts[j][own * inside:own * (inside + 1), :].astype(BF16)


def first_attention_kernel(own, pick_ref, q_ref, *refs):
    *rest, c_ref, share_ref, lines = refs
    share_ref[...] = jnp.dot(pick_ref[...], q_ref[...], preferred_element_type=F32)
    attention_kernel(0, own, q_ref, *rest, c_ref, lines)


def attention_kernel(step, own, q_ref, k_ref, v_ref, len_ref, order_ref, line_ref, column_ref, c_ref, lines):
    head_dim = q_ref.shape[1]
    heads = line_ref.shape[0]
    span = column_ref.shape[1]
    q = jnp.dot(order_ref[...], q_ref[...], preferred_element_type=F32).astype(BF16)
    group_of, position = column_ref[0:1, :], column_ref[1:2, :]
    same = group_of == line_ref[...]
    ours = [slice(heads * r, heads * (r + 1)) for r in range(own)]
    keys = [slice(span * r, span * (r + 1)) for r in range(own)]
    scores = [
        lax.dot_general(
            q[ours[r], :], k_ref[step, keys[r], :], (((1,), (1,)), ((), ())), preferred_element_type=F32
        )
        for r in range(own)
    ]
    exps = [
        jnp.where(
            same & (position < len_ref[step, :, r:r + 1]), jnp.exp2(scores[r] * (head_dim ** (-0.5) * LOG2E)), 0.0
        )
        for r in range(own)
    ]
    contexts = [
        jnp.dot(exps[r].astype(BF16), v_ref[step, keys[r], :], preferred_element_type=F32) for r in range(own)
    ]
    for r in range(own):
        lines[ours[r], :] = contexts[r] * (1.0 / jnp.sum(exps[r], axis=-1, keepdims=True))
    for h in range(heads):
        c_ref[:, head_dim * h:head_dim * (h + 1)] = lines[pl.ds(h, own, stride=heads), :].astype(BF16)


def attention_tables(own, heads, local_heads, kv_heads, cache_len):
    group = heads // kv_heads
    row, head = np.divmod(np.arange(own * heads), heads)
    sender, place = head // local_heads, row * local_heads + head % local_heads
    devices, count = heads // local_heads, own * local_heads
    order = np.zeros((own * heads, own * heads), np.float32)
    order[np.arange(own * heads), sender * count + place] = 1.0
    first_order = np.zeros((own * heads, devices * (EXTRA + count)), np.float32)
    first_order[np.arange(own * heads), sender * (EXTRA + count) + EXTRA + place] = 1.0
    pick = np.zeros((devices * own, devices * (EXTRA + count)), np.float32)
    for part in range(3):
        for r in range(own):
            pick[np.arange(devices) * own + r, np.arange(devices) * (EXTRA + count) + part * own + r] = 1.0
    line = (np.arange(heads) // group).astype(np.int32)[:, None]
    position, kv = np.divmod(np.arange(cache_len * kv_heads), kv_heads)
    column = np.zeros((8, cache_len * kv_heads), np.int32)
    column[:2] = kv, position
    asis = jnp.asarray(line), jnp.asarray(column)
    return (jnp.asarray(order, BF16), *asis), (jnp.asarray(first_order, BF16), *asis), jnp.asarray(pick, BF16)


def out_kernel(c_ref, w_ref, o_ref, lines):
    devices, own, width = c_ref.shape
    chunk, totals = 512, {}
    for start in range(0, width, chunk):
        at = slice(start, start + chunk)
        for i in range(devices):
            lines[own * i:own * (i + 1), at] = c_ref[i, :, at].astype(F32)
        add_tiles(totals, lines[:, at].astype(BF16), w_ref, at)
    for at, total in totals.items():
        columns = total.astype(BF16)
        for i in range(devices):
            o_ref[i, :, at:at + columns.shape[1]] = columns


def half_out_kernel(c_ref, w_ref, o_ref, lines):
    devices, slots, own, part = c_ref.shape
    low = devices // slots
    chunk, totals = 512, {}
    for start in range(0, slots * part, chunk):
        at = slice(start, start + chunk)
        half, inside = start // part, slice(start % part, start % part + chunk)
        for i in range(devices):
            lines[own * i:own * (i + 1), at] = c_ref[half * low + i % low, i // low, :, inside].astype(F32)
        add_tiles(totals, lines[:, at].astype(BF16), w_ref, at)
    for at, total in totals.items():
        columns = total.astype(BF16)
        for i in range(devices):
            o_ref[i, :, at:at + columns.shape[1]] = columns


def expert_kernel(step, me_ref, a_ref, x_ref, gain_ref, gate_ref, up_ref, down_ref, share_ref, h_ref, m_ref, middle):
    devices, own, _ = h_ref.shape
    part = a_ref.shape[2]
    width = part * devices
    me = me_ref[0]
    gates, ups, squares = {}, {}, jnp.zeros((devices * own, 128), F32)
    for j in range(devices):
        at = slice(part * j, part * (j + 1))
        values = x_ref[:, at] + a_ref[j].astype(F32)
        middle[:, at] = values
        squares = add_squares(squares, values)
        left = (values * gain_ref[:, at].astype(F32)).astype(BF16)
        add_tiles(gates, left, gate_ref, at)
        add_tiles(ups, left, up_ref, at)
    scale = lax.rsqrt(jnp.sum(squares, axis=-1, keepdims=True) / width + EPS)
    lane = lax.broadcasted_iota(jnp.int32, share_ref.shape, 1)
    mine = lane == step * (devices // 2) + me // 2
    share = jnp.sum(jnp.where(mine, share_ref[...], 0.0), axis=1, keepdims=True)
    active = {}
    for at in gates:
        gate, up = gates[at] * scale, ups[at] * scale
        active[at] = (gate / (1.0 + jnp.exp(-gate)) * up * share).astype(BF16)
    chunk = 512
    for start in range(0, width, chunk):
        piece = None
        for at, left in active.items():
            term = jnp.dot(
                left, down_ref[at:at + left.shape[1], start:start + chunk], preferred_element_type=F32
            )
            piece = term if piece is None else piece + term
        for i in range(devices):
            h_ref[i, :, start:start + chunk] = piece[own * i:own * (i + 1), :].astype(BF16)
    pairs = 8 // own
    block = middle[pl.ds(pl.multiple_of((me // pairs) * 8, 8), 8), :]
    kept = block[0:own, :]
    for p in range(1, pairs):
        kept = jnp.where(me % pairs == p, block[own * p:own * (p + 1), :], kept)
    m_ref[...] = kept


def sending_kernel(step, low, me_ref, *refs):
    pieces, (m_ref, middle, rows) = refs[7:7 + low], refs[7 + low:]
    expert_kernel(step, me_ref, *refs[:7], rows, m_ref, middle)
    me = me_ref[0]
    for l, piece in enumerate(pieces):
        for h in range(piece.shape[0]):
            piece[h] = rows[me ^ (l + h * low)]


def partial_kernel(m_ref, *refs):
    pieces, t_ref = refs[:-1], refs[-1]
    for h in range(t_ref.shape[0]):
        total = m_ref[...] if h == 0 else jnp.zeros(m_ref.shape, F32)
        for piece in pieces:
            total = total + piece[h].astype(F32)
        t_ref[h] = total.astype(BF16)


def join_kernel(*refs):
    parts, x_ref = refs[:-1], refs[-1]
    for g in range(len(parts)):
        total = parts[0][g].astype(F32)
        for h in range(1, len(parts)):
            total = total + parts[h][h ^ g].astype(F32)
        x_ref[g] = total.astype(BF16)


def combine_kernel(r_ref, m_ref, o_ref):
    total = m_ref[...]
    for i in range(r_ref.shape[0]):
        total = total + r_ref[i].astype(F32)
    o_ref[...] = total.astype(BF16)


def body(
    hidden_in,
    attn_gain,
    w_query,
    w_out,
    key_cache,
    value_cache,
    lengths,
    ffn_gain,
    w_gate,
    w_up,
    w_down,
    routes,
    gates,
):
    devices = lax.axis_size("expert")
    me = lax.axis_index("expert").astype(jnp.int32).reshape(1)
    own, width = hidden_in.shape[1:]
    rows = own * devices
    cache_len, kv_heads, head_dim = key_cache.shape[3:]
    query_w, out_w = w_query[0], w_out[0]
    part = query_w.shape[1]
    local_heads = part // head_dim
    heads = local_heads * devices
    gate_w, up_w, down_w = w_gate[0, 0], w_up[0, 0], w_down[0, 0]
    hidden = gate_w.shape[1]
    places = own * cache_len * kv_heads
    keys = key_cache.reshape(STEPS, places, head_dim)
    values = value_cache.reshape(STEPS, places, head_dim)
    routes, gates = routes[0].transpose(0, 2, 1), gates[0].transpose(0, 2, 1)
    lengths = lengths.reshape(STEPS, 1, own)
    tables, first_tables, pick = attention_tables(own, heads, local_heads, kv_heads, cache_len)
    low, high = split(devices)
    by_half = high == 2 and devices == 2 * kv_heads
    smem = whole(pltpu.SMEM)
    q_shape = jax.ShapeDtypeStruct((rows * local_heads, head_dim), BF16)
    x_shape = jax.ShapeDtypeStruct((devices, own, width), BF16)
    states_shape = jax.ShapeDtypeStruct((rows, width), F32)
    m_shape = jax.ShapeDtypeStruct((own, width), F32)
    slots = jax.ShapeDtypeStruct((high, own, width), BF16)
    copies = call(
        spread_kernel,
        x_shape,
        (hidden_in[0],),
        [whole()],
        [],
        "spread",
        (0, 2 * rows * width),
    )
    me, copies = lax.optimization_barrier((me, copies))
    if by_half:
        block = jax.ShapeDtypeStruct((2 * places // 2 + EXTRA, head_dim), BF16)
        others = call(
            functools.partial(cache_kernel, own, kv_heads),
            (block,) * (STEPS - 1),
            (me, lengths, keys, values),
            [smem] + [whole()] * 3,
            [pltpu.VMEM((places, head_dim), F32)],
            "caches_of_other_half",
            (places * head_dim, 8 * places * head_dim),
            0,
        )
        others = [shifted(one, low) for one in others]
    for step in range(STEPS):
        spread = pltpu.VMEM((rows * local_heads, head_dim), F32)
        cost = (2 * rows * width * part, 2 * width * part)
        if step == 0:
            own_q, states = call(
                functools.partial(first_kernel, head_dim),
                (jax.ShapeDtypeStruct((devices, EXTRA + own * local_heads, head_dim), BF16), states_shape),
                (swapped(copies), attn_gain, query_w, routes, gates),
                [whole()] * 5,
                [spread],
                "first_query",
                cost,
            )
        else:
            pieces = [state] + [shifted(state, l) for l in range(1, low)]
            if by_half:
                *queries, states = call(
                    functools.partial(halves_kernel, head_dim, low),
                    (jax.ShapeDtypeStruct((2, own * local_heads, head_dim), BF16),) * low + (states_shape,),
                    (me, *pieces, attn_gain, query_w),
                    [smem] + [whole()] * (low + 2),
                    [pltpu.VMEM((devices, own, width), BF16), pltpu.VMEM((devices, own * local_heads, head_dim), F32)],
                    "queries_by_half",
                    cost,
                )
                queries = [queries[0]] + [shifted(queries[l], l) for l in range(1, low)]
            else:
                own_q, states = call(
                    functools.partial(order_kernel, head_dim, low),
                    (q_shape, states_shape),
                    (me, *pieces, attn_gain, query_w),
                    [smem] + [whole()] * (low + 2),
                    [pltpu.VMEM((devices, own, width), BF16), spread],
                    "order_query",
                    cost,
                )
        if step and by_half:
            context = call(
                functools.partial(half_attention_kernel, step, own, kv_heads),
                jax.ShapeDtypeStruct((2, own, heads * head_dim // 2), BF16),
                (me, *queries, keys, values, lengths, others[step - 1]),
                [smem] + [whole()] * (low + 4),
                [pltpu.VMEM((2, low, own * local_heads, head_dim), BF16)],
                "half_attention",
                cost,
            )
        else:
            c_shape = jax.ShapeDtypeStruct((own, heads * head_dim), BF16)
            by_row = [pltpu.VMEM((own * heads, head_dim), F32)]
            cost = (4 * own * heads * places * head_dim, 4 * places * head_dim)
            queries = swapped(own_q.reshape(devices, -1, head_dim)).reshape(-1, head_dim)
            if step == 0:
                context, shares = call(
                    functools.partial(first_attention_kernel, own),
                    (c_shape, jax.ShapeDtypeStruct((rows, LANES), F32)),
                    (pick, queries, keys, values, lengths, *first_tables),
                    [whole()] * 8,
                    by_row,
                    "first_attention",
                    cost,
                )
            else:
                context = call(
                    functools.partial(attention_kernel, step, own),
                    c_shape,
                    (queries, keys, values, lengths, *tables),
                    [whole()] * 7,
                    by_row,
                    "attention",
                    cost,
                )
        contexts = everyones(context)
        columns = call(
            half_out_kernel if step and by_half else out_kernel,
            jax.ShapeDtypeStruct((devices, rows, part), BF16),
            (contexts, out_w),
            [whole()] * 2,
            [pltpu.VMEM((rows, heads * head_dim), F32)],
            "attention_out",
            (2 * rows * width * part, 2 * width * part),
        )
        attended = swapped(columns)
        operands = (me, attended, states, ffn_gain, gate_w, up_w, down_w, shares)
        specs = [smem] + [whole()] * 7
        scratch = [pltpu.VMEM((rows, width), F32)]
        cost = (6 * rows * width * hidden, 6 * width * hidden)
        if step + 1 == STEPS:
            half_out, middle = call(
                functools.partial(expert_kernel, step), (x_shape, m_shape), operands, specs, scratch, "experts", cost
            )
            state = call(
                combine_kernel,
                jax.ShapeDtypeStruct((own, width), BF16),
                (swapped(half_out), middle),
                [whole()] * 2,
                [],
                "combine",
                (rows * width, 4 * rows * width),
            )
        else:
            *pieces, middle = call(
                functools.partial(sending_kernel, step, low),
                (slots,) * low + (m_shape,),
                operands,
                specs,
                scratch + [pltpu.VMEM((devices, own, width), BF16)],
                "experts_sending",
                cost,
            )
            pieces = [pieces[0]] + [shifted(pieces[l], l) for l in range(low - 1, 0, -1)]
            part_sums = call(
                partial_kernel, slots, (middle, *pieces), [whole()] * (low + 1), [], "partial",
                (rows * width, 4 * rows * width),
            )
            parts = [shifted(part_sums, h * low, 1) for h in range(high)]
            if by_half:
                parts[0], others[step] = lax.optimization_barrier((parts[0], others[step]))
            state = call(
                join_kernel, slots, tuple(parts), [whole()] * high, [], "join", (rows * width, 4 * rows * width)
            )
    return state[None]


def solution(mesh):
    return jax.shard_map(
        body,
        mesh=mesh,
        in_specs=(
            P("section", "expert", None),
            P("section", None),
            P("section", None, "expert"),
            P("section", None, "expert"),
            P("section", None, "expert", None, None, None),
            P("section", None, "expert", None, None, None),
            P("section", None, "expert"),
            P("section", None),
            P("section", "expert", None, None),
            P("section", "expert", None, None),
            P("section", "expert", None, None),
            P("section", None, "expert", None),
            P("section", None, "expert", None),
        ),
        out_specs=P("section", "expert", None),
        check_vma=False,
    )
```

```python
import functools
import math

import jax
import jax.numpy as jnp
import numpy as np
from jax import lax
from jax.experimental import pallas as pl
from jax.experimental.pallas import tpu as pltpu
from jax.sharding import PartitionSpec as P

STEPS = 3
EPS = 1e-06
LIMIT = 24 * 1024 * 1024
EXCHANGE = 20 * 1000 * 1000 * 1000
LANES = 128
EXTRA = 16
LOG2E = math.log2(math.e)
F32 = jnp.float32
BF16 = jnp.bfloat16


def shifted(array, mask, sections=0):
    stages, devices = lax.axis_size("section"), lax.axis_size("expert")
    pairs = [
        (s * devices + e, (s + sections) % stages * devices + (e ^ mask))
        for s in range(stages)
        for e in range(devices)
    ]
    return lax.ppermute(array, ("section", "expert"), pairs)


def split(devices):
    low = 1
    while low * low < devices:
        low *= 2
    return low, devices // low


def swapped(blocks):
    return lax.all_to_all(blocks, "expert", split_axis=0, concat_axis=0, tiled=True)


def everyones(array):
    devices = lax.axis_size("expert")
    return swapped(jnp.broadcast_to(array[None], (devices,) + array.shape))


def whole(memory_space=pltpu.VMEM):
    return pl.BlockSpec(memory_space=memory_space)


def call(kernel, out, operands, specs, scratch, name, cost, exchange=EXCHANGE):
    single = not isinstance(out, tuple)
    return pl.pallas_call(
        kernel,
        out_shape=out,
        in_specs=specs,
        out_specs=whole() if single else tuple(whole() for _ in out),
        scratch_shapes=scratch,
        compiler_params=pltpu.CompilerParams(vmem_limit_bytes=LIMIT),
        cost_estimate=pl.CostEstimate(flops=cost[0] + exchange, bytes_accessed=cost[1], transcendentals=0),
        name=name,
    )(*operands)


def add_tiles(totals, left, right, depth, tile=128):
    for at in range(0, right.shape[1], tile):
        part = jnp.dot(left, right[depth, at:at + tile], preferred_element_type=F32)
        totals[at] = totals[at] + part if at in totals else part


def add_squares(totals, values):
    for at in range(0, values.shape[1], 128):
        totals = totals + values[:, at:at + 128] * values[:, at:at + 128]
    return totals


def spread_kernel(x_ref, o_ref):
    for i in range(o_ref.shape[0]):
        o_ref[i] = x_ref[...]


def coded_shares(routes_ref, gates_ref, experts):
    own = routes_ref.shape[2]
    lane = lax.broadcasted_iota(jnp.int32, (EXTRA, LANES), 1)
    row = lax.broadcasted_iota(jnp.int32, (EXTRA, LANES), 0)
    line = lax.broadcasted_iota(jnp.int32, (EXTRA, own), 0)
    column = lax.broadcasted_iota(jnp.int32, (EXTRA, own), 1)
    here = (line == column) | (line == column + own) | (line == column + 2 * own)
    shares = jnp.zeros((EXTRA, LANES), F32)
    for step in range(STEPS):
        routes, gates = routes_ref[step], gates_ref[step]
        parts = gates / jnp.sum(gates, axis=0, keepdims=True)
        for e in range(experts):
            share = jnp.sum(jnp.where(routes == e, parts, 0.0), axis=0, keepdims=True)
            share = jnp.sum(jnp.where(here, share, 0.0), axis=1, keepdims=True)
            shares = jnp.where(lane == step * experts + e, share, shares)
    first = shares.astype(BF16).astype(F32)
    second = (shares - first).astype(BF16).astype(F32)
    return jnp.where(row < own, first, jnp.where(row < 2 * own, second, shares - first - second)).astype(BF16)


def first_kernel(head_dim, x_ref, gain_ref, w_ref, routes_ref, gates_ref, q_ref, states, spread):
    query_kernel(head_dim, x_ref, gain_ref, w_ref, None, states, spread)
    devices = q_ref.shape[0]
    count = spread.shape[0] // devices
    coded = coded_shares(routes_ref, gates_ref, devices // 2)
    for i in range(devices):
        q_ref[i, :EXTRA, :] = coded
        q_ref[i, EXTRA:, :] = spread[count * i:count * (i + 1), :].astype(BF16)


def order_kernel(head_dim, low, me_ref, *refs):
    pieces, (gain_ref, w_ref, q_ref, states, x_ref, spread) = refs[:low], refs[low:]
    me = me_ref[0]
    for l, piece in enumerate(pieces):
        for h in range(piece.shape[0]):
            x_ref[me ^ (l + h * low)] = piece[h]
    query_kernel(head_dim, x_ref, gain_ref, w_ref, q_ref, states, spread)


def head_queries(head_dim, x_ref, gain_ref, w_ref, states):
    devices, own, _ = x_ref.shape
    rows, (width, columns) = devices * own, w_ref.shape
    chunk = 512
    totals, squares = {}, jnp.zeros((rows, 128), F32)
    for start in range(0, width, chunk):
        at = slice(start, start + chunk)
        for i in range(devices):
            states[own * i:own * (i + 1), at] = x_ref[i, :, at].astype(F32)
        values = states[:, at]
        squares = add_squares(squares, values)
        add_tiles(totals, (values * gain_ref[:, at].astype(F32)).astype(BF16), w_ref, at, head_dim)
    scale = lax.rsqrt(jnp.sum(squares, axis=-1, keepdims=True) / width + EPS)
    queries = []
    for h in range(columns // head_dim):
        one = totals[head_dim * h] * scale
        queries.append(one * lax.rsqrt(jnp.mean(one * one, axis=-1, keepdims=True) + EPS))
    return queries


def query_kernel(head_dim, x_ref, gain_ref, w_ref, q_ref, states, spread):
    queries = head_queries(head_dim, x_ref, gain_ref, w_ref, states)
    for h, one in enumerate(queries):
        spread[pl.ds(h, one.shape[0], stride=len(queries)), :] = one
    if q_ref is not None:
        q_ref[...] = spread[...].astype(BF16)


def halves_kernel(head_dim, low, me_ref, *refs):
    pieces, refs = refs[:low], refs[low:]
    (gain_ref, w_ref), outs, (states, x_ref, spread) = refs[:2], refs[2:2 + low], refs[2 + low:]
    me = me_ref[0]
    for l, piece in enumerate(pieces):
        for h in range(piece.shape[0]):
            x_ref[me ^ (l + h * low)] = piece[h]
    devices, own, _ = x_ref.shape
    for h, one in enumerate(head_queries(head_dim, x_ref, gain_ref, w_ref, states)):
        for i in range(devices):
            spread[i, own * h:own * (h + 1), :] = one[own * i:own * (i + 1), :]
    for l, out in enumerate(outs):
        for g in range(out.shape[0]):
            out[g] = spread[(me % low ^ l) + g * low].astype(BF16)


def cache_kernel(own, kv_heads, me_ref, len_ref, k_ref, v_ref, *refs):
    *blocks, wide = refs
    half = kv_heads // 2
    first = jnp.where(me_ref[0] >= kv_heads, 0, half)
    span = k_ref.shape[1] // kv_heads
    cache = span // own
    line = lax.broadcasted_iota(jnp.int32, (EXTRA, LANES), 0)
    place = lax.broadcasted_iota(jnp.int32, (EXTRA, LANES), 1) + line * LANES
    for step, block in enumerate(blocks, 1):
        at = 0
        for ref in (k_ref, v_ref):
            wide[...] = ref[step].astype(F32)
            for j in range(half):
                block[at:at + span, :] = wide[pl.ds(first + j, span, stride=kv_heads), :].astype(BF16)
                at += span
        valid = jnp.zeros((EXTRA, LANES), F32)
        for r in range(own):
            inside = (place >= r * cache) & (place < r * cache + len_ref[step, :, r:r + 1])
            valid = jnp.where(inside, 1.0, valid)
        block[at:, :] = valid.astype(BF16)


def softmax_times(scores, valid, head_dim, values):
    exps = jnp.where(valid, jnp.exp2(scores * (head_dim ** (-0.5) * LOG2E)), 0.0)
    context = jnp.dot(exps.astype(BF16), values, preferred_element_type=F32)
    return context * (1.0 / jnp.sum(exps, axis=-1, keepdims=True))


def products(queries, keys):
    return lax.dot_general(queries, keys, (((1,), (1,)), ((), ())), preferred_element_type=F32)


def half_attention_kernel(step, own, kv_heads, me_ref, *refs):
    low = len(refs) - 6
    pieces, (k_ref, v_ref, len_ref, pair_ref, c_ref, q_ref) = refs[:low], refs[low:]
    me = me_ref[0]
    mine = jnp.where(me >= low, 1, 0)
    half = kv_heads // 2
    count, head_dim = pieces[0].shape[1:]
    for l, piece in enumerate(pieces):
        for g in range(2):
            q_ref[g, me % low ^ (low - l) % low] = piece[g]
    rows = low * count
    span = k_ref.shape[1] // kv_heads
    cache = span // own
    q = q_ref[mine].reshape(rows, head_dim)
    line = lax.broadcasted_iota(jnp.int32, (rows, 1), 0)
    place = lax.broadcasted_iota(jnp.int32, (1, span * kv_heads), 1)
    of_row = place // (cache * kv_heads)
    length = jnp.zeros(place.shape, jnp.int32)
    for r in range(own):
        length = jnp.where(of_row == r, len_ref[step, :, r:r + 1], length)
    key_of = jnp.where(place // kv_heads % cache < length, of_row * kv_heads + place % kv_heads, -1)
    key_for = line % own * kv_heads + line // (rows // half) + half * mine
    scores = products(q, k_ref[step])
    other = q_ref[1 - mine].reshape(rows, head_dim)
    part = rows // half
    ends = pair_ref[2 * half * span:, :].astype(F32)
    valid = jnp.concatenate([ends[g:g + 1, :] for g in range(span // LANES)], axis=1) > 0.0
    line = lax.broadcasted_iota(jnp.int32, (part, 1), 0)
    place = lax.broadcasted_iota(jnp.int32, (1, span), 1)
    theirs = (line % own == place // cache) & valid
    others = [products(other[part * j:part * (j + 1), :], pair_ref[span * j:span * (j + 1), :]) for j in range(half)]
    own_context = softmax_times(scores, key_of == key_for, head_dim, v_ref[step])
    contexts = [
        softmax_times(others[j], theirs, head_dim, pair_ref[span * (half + j):span * (half + j + 1), :])
        for j in range(half)
    ]
    heads = part // own
    for h in range(rows // own):
        at = slice(head_dim * h, head_dim * (h + 1))
        c_ref[mine, :, at] = own_context[own * h:own * (h + 1), :].astype(BF16)
        j, inside = h // heads, h % heads
        c_ref[1 - mine, :, at] = contexts[j][own * inside:own * (inside + 1), :].astype(BF16)


def first_attention_kernel(own, pick_ref, q_ref, *refs):
    *rest, c_ref, share_ref, lines = refs
    share_ref[...] = jnp.dot(pick_ref[...], q_ref[...], preferred_element_type=F32)
    attention_kernel(0, own, q_ref, *rest, c_ref, lines)


def attention_kernel(step, own, q_ref, k_ref, v_ref, len_ref, order_ref, line_ref, column_ref, c_ref, lines):
    head_dim = q_ref.shape[1]
    heads = line_ref.shape[0]
    span = column_ref.shape[1]
    q = jnp.dot(order_ref[...], q_ref[...], preferred_element_type=F32).astype(BF16)
    group_of, position = column_ref[0:1, :], column_ref[1:2, :]
    same = group_of == line_ref[...]
    ours = [slice(heads * r, heads * (r + 1)) for r in range(own)]
    keys = [slice(span * r, span * (r + 1)) for r in range(own)]
    scores = [
        lax.dot_general(
            q[ours[r], :], k_ref[step, keys[r], :], (((1,), (1,)), ((), ())), preferred_element_type=F32
        )
        for r in range(own)
    ]
    exps = [
        jnp.where(
            same & (position < len_ref[step, :, r:r + 1]), jnp.exp2(scores[r] * (head_dim ** (-0.5) * LOG2E)), 0.0
        )
        for r in range(own)
    ]
    contexts = [
        jnp.dot(exps[r].astype(BF16), v_ref[step, keys[r], :], preferred_element_type=F32) for r in range(own)
    ]
    for r in range(own):
        lines[ours[r], :] = contexts[r] * (1.0 / jnp.sum(exps[r], axis=-1, keepdims=True))
    for h in range(heads):
        c_ref[:, head_dim * h:head_dim * (h + 1)] = lines[pl.ds(h, own, stride=heads), :].astype(BF16)


def attention_tables(own, heads, local_heads, kv_heads, cache_len):
    group = heads // kv_heads
    row, head = np.divmod(np.arange(own * heads), heads)
    sender, place = head // local_heads, row * local_heads + head % local_heads
    devices, count = heads // local_heads, own * local_heads
    order = np.zeros((own * heads, own * heads), np.float32)
    order[np.arange(own * heads), sender * count + place] = 1.0
    first_order = np.zeros((own * heads, devices * (EXTRA + count)), np.float32)
    first_order[np.arange(own * heads), sender * (EXTRA + count) + EXTRA + place] = 1.0
    pick = np.zeros((devices * own, devices * (EXTRA + count)), np.float32)
    for part in range(3):
        for r in range(own):
            pick[np.arange(devices) * own + r, np.arange(devices) * (EXTRA + count) + part * own + r] = 1.0
    line = (np.arange(heads) // group).astype(np.int32)[:, None]
    position, kv = np.divmod(np.arange(cache_len * kv_heads), kv_heads)
    column = np.zeros((8, cache_len * kv_heads), np.int32)
    column[:2] = kv, position
    asis = jnp.asarray(line), jnp.asarray(column)
    return (jnp.asarray(order, BF16), *asis), (jnp.asarray(first_order, BF16), *asis), jnp.asarray(pick, BF16)


def out_kernel(c_ref, w_ref, o_ref, lines):
    devices, own, width = c_ref.shape
    chunk, totals = 512, {}
    for start in range(0, width, chunk):
        at = slice(start, start + chunk)
        for i in range(devices):
            lines[own * i:own * (i + 1), at] = c_ref[i, :, at].astype(F32)
        add_tiles(totals, lines[:, at].astype(BF16), w_ref, at)
    for at, total in totals.items():
        columns = total.astype(BF16)
        for i in range(devices):
            o_ref[i, :, at:at + columns.shape[1]] = columns


def half_out_kernel(c_ref, w_ref, o_ref, lines):
    devices, slots, own, part = c_ref.shape
    low = devices // slots
    chunk, totals = 512, {}
    for start in range(0, slots * part, chunk):
        at = slice(start, start + chunk)
        half, inside = start // part, slice(start % part, start % part + chunk)
        for i in range(devices):
            lines[own * i:own * (i + 1), at] = c_ref[half * low + i % low, i // low, :, inside].astype(F32)
        add_tiles(totals, lines[:, at].astype(BF16), w_ref, at)
    for at, total in totals.items():
        columns = total.astype(BF16)
        for i in range(devices):
            o_ref[i, :, at:at + columns.shape[1]] = columns


def expert_kernel(step, me_ref, a_ref, x_ref, gain_ref, gate_ref, up_ref, down_ref, share_ref, h_ref, m_ref, middle):
    devices, own, _ = h_ref.shape
    part = a_ref.shape[2]
    width = part * devices
    me = me_ref[0]
    gates, ups, squares = {}, {}, jnp.zeros((devices * own, 128), F32)
    for j in range(devices):
        at = slice(part * j, part * (j + 1))
        values = x_ref[:, at] + a_ref[j].astype(F32)
        middle[:, at] = values
        squares = add_squares(squares, values)
        left = (values * gain_ref[:, at].astype(F32)).astype(BF16)
        add_tiles(gates, left, gate_ref, at)
        add_tiles(ups, left, up_ref, at)
    scale = lax.rsqrt(jnp.sum(squares, axis=-1, keepdims=True) / width + EPS)
    lane = lax.broadcasted_iota(jnp.int32, share_ref.shape, 1)
    mine = lane == step * (devices // 2) + me // 2
    share = jnp.sum(jnp.where(mine, share_ref[...], 0.0), axis=1, keepdims=True)
    active = {}
    for at in gates:
        gate, up = gates[at] * scale, ups[at] * scale
        active[at] = (gate / (1.0 + jnp.exp(-gate)) * up * share).astype(BF16)
    chunk = 512
    for start in range(0, width, chunk):
        piece = None
        for at, left in active.items():
            term = jnp.dot(
                left, down_ref[at:at + left.shape[1], start:start + chunk], preferred_element_type=F32
            )
            piece = term if piece is None else piece + term
        for i in range(devices):
            h_ref[i, :, start:start + chunk] = piece[own * i:own * (i + 1), :].astype(BF16)
    pairs = 8 // own
    block = middle[pl.ds(pl.multiple_of((me // pairs) * 8, 8), 8), :]
    kept = block[0:own, :]
    for p in range(1, pairs):
        kept = jnp.where(me % pairs == p, block[own * p:own * (p + 1), :], kept)
    m_ref[...] = kept


def sending_kernel(step, low, me_ref, *refs):
    pieces, (m_ref, middle, rows) = refs[7:7 + low], refs[7 + low:]
    expert_kernel(step, me_ref, *refs[:7], rows, m_ref, middle)
    me = me_ref[0]
    for l, piece in enumerate(pieces):
        for h in range(piece.shape[0]):
            piece[h] = rows[me ^ (l + h * low)]


def partial_kernel(m_ref, *refs):
    pieces, t_ref = refs[:-1], refs[-1]
    for h in range(t_ref.shape[0]):
        total = m_ref[...] if h == 0 else jnp.zeros(m_ref.shape, F32)
        for piece in pieces:
            total = total + piece[h].astype(F32)
        t_ref[h] = total.astype(BF16)


def join_kernel(*refs):
    parts, x_ref = refs[:-1], refs[-1]
    for g in range(len(parts)):
        total = parts[0][g].astype(F32)
        for h in range(1, len(parts)):
            total = total + parts[h][h ^ g].astype(F32)
        x_ref[g] = total.astype(BF16)


def combine_kernel(r_ref, m_ref, o_ref):
    total = m_ref[...]
    for i in range(r_ref.shape[0]):
        total = total + r_ref[i].astype(F32)
    o_ref[...] = total.astype(BF16)


def body(
    hidden_in,
    attn_gain,
    w_query,
    w_out,
    key_cache,
    value_cache,
    lengths,
    ffn_gain,
    w_gate,
    w_up,
    w_down,
    routes,
    gates,
):
    devices = lax.axis_size("expert")
    me = lax.axis_index("expert").astype(jnp.int32).reshape(1)
    own, width = hidden_in.shape[1:]
    rows = own * devices
    cache_len, kv_heads, head_dim = key_cache.shape[3:]
    query_w, out_w = w_query[0], w_out[0]
    part = query_w.shape[1]
    local_heads = part // head_dim
    heads = local_heads * devices
    gate_w, up_w, down_w = w_gate[0, 0], w_up[0, 0], w_down[0, 0]
    hidden = gate_w.shape[1]
    places = own * cache_len * kv_heads
    keys = key_cache.reshape(STEPS, places, head_dim)
    values = value_cache.reshape(STEPS, places, head_dim)
    routes, gates = routes[0].transpose(0, 2, 1), gates[0].transpose(0, 2, 1)
    lengths = lengths.reshape(STEPS, 1, own)
    tables, first_tables, pick = attention_tables(own, heads, local_heads, kv_heads, cache_len)
    low, high = split(devices)
    by_half = high == 2 and devices == 2 * kv_heads
    smem = whole(pltpu.SMEM)
    q_shape = jax.ShapeDtypeStruct((rows * local_heads, head_dim), BF16)
    x_shape = jax.ShapeDtypeStruct((devices, own, width), BF16)
    states_shape = jax.ShapeDtypeStruct((rows, width), F32)
    m_shape = jax.ShapeDtypeStruct((own, width), F32)
    slots = jax.ShapeDtypeStruct((high, own, width), BF16)
    copies = call(
        spread_kernel,
        x_shape,
        (hidden_in[0],),
        [whole()],
        [],
        "spread",
        (0, 2 * rows * width),
    )
    me, copies = lax.optimization_barrier((me, copies))
    if by_half:
        block = jax.ShapeDtypeStruct((2 * places // 2 + EXTRA, head_dim), BF16)
        others = call(
            functools.partial(cache_kernel, own, kv_heads),
            (block,) * (STEPS - 1),
            (me, lengths, keys, values),
            [smem] + [whole()] * 3,
            [pltpu.VMEM((places, head_dim), F32)],
            "caches_of_other_half",
            (places * head_dim, 8 * places * head_dim),
            0,
        )
        others = [shifted(one, low) for one in others]
    for step in range(STEPS):
        spread = pltpu.VMEM((rows * local_heads, head_dim), F32)
        cost = (2 * rows * width * part, 2 * width * part)
        if step == 0:
            own_q, states = call(
                functools.partial(first_kernel, head_dim),
                (jax.ShapeDtypeStruct((devices, EXTRA + own * local_heads, head_dim), BF16), states_shape),
                (swapped(copies), attn_gain, query_w, routes, gates),
                [whole()] * 5,
                [spread],
                "first_query",
                cost,
            )
        else:
            pieces = [state] + [shifted(state, l) for l in range(1, low)]
            if by_half:
                *queries, states = call(
                    functools.partial(halves_kernel, head_dim, low),
                    (jax.ShapeDtypeStruct((2, own * local_heads, head_dim), BF16),) * low + (states_shape,),
                    (me, *pieces, attn_gain, query_w),
                    [smem] + [whole()] * (low + 2),
                    [pltpu.VMEM((devices, own, width), BF16), pltpu.VMEM((devices, own * local_heads, head_dim), F32)],
                    "queries_by_half",
                    cost,
                    0,
                )
                queries = [queries[0]] + [shifted(queries[l], l) for l in range(low - 1, 0, -1)]
            else:
                own_q, states = call(
                    functools.partial(order_kernel, head_dim, low),
                    (q_shape, states_shape),
                    (me, *pieces, attn_gain, query_w),
                    [smem] + [whole()] * (low + 2),
                    [pltpu.VMEM((devices, own, width), BF16), spread],
                    "order_query",
                    cost,
                )
        if step and by_half:
            context = call(
                functools.partial(half_attention_kernel, step, own, kv_heads),
                jax.ShapeDtypeStruct((2, own, heads * head_dim // 2), BF16),
                (me, *queries, keys, values, lengths, others[step - 1]),
                [smem] + [whole()] * (low + 4),
                [pltpu.VMEM((2, low, own * local_heads, head_dim), BF16)],
                "half_attention",
                cost,
            )
        else:
            c_shape = jax.ShapeDtypeStruct((own, heads * head_dim), BF16)
            by_row = [pltpu.VMEM((own * heads, head_dim), F32)]
            cost = (4 * own * heads * places * head_dim, 4 * places * head_dim)
            queries = swapped(own_q.reshape(devices, -1, head_dim)).reshape(-1, head_dim)
            if step == 0:
                context, shares = call(
                    functools.partial(first_attention_kernel, own),
                    (c_shape, jax.ShapeDtypeStruct((rows, LANES), F32)),
                    (pick, queries, keys, values, lengths, *first_tables),
                    [whole()] * 8,
                    by_row,
                    "first_attention",
                    cost,
                )
            else:
                context = call(
                    functools.partial(attention_kernel, step, own),
                    c_shape,
                    (queries, keys, values, lengths, *tables),
                    [whole()] * 7,
                    by_row,
                    "attention",
                    cost,
                )
        contexts = everyones(context)
        columns = call(
            half_out_kernel if step and by_half else out_kernel,
            jax.ShapeDtypeStruct((devices, rows, part), BF16),
            (contexts, out_w),
            [whole()] * 2,
            [pltpu.VMEM((rows, heads * head_dim), F32)],
            "attention_out",
            (2 * rows * width * part, 2 * width * part),
        )
        attended = swapped(columns)
        operands = (me, attended, states, ffn_gain, gate_w, up_w, down_w, shares)
        specs = [smem] + [whole()] * 7
        scratch = [pltpu.VMEM((rows, width), F32)]
        cost = (6 * rows * width * hidden, 6 * width * hidden)
        if step + 1 == STEPS:
            half_out, middle = call(
                functools.partial(expert_kernel, step), (x_shape, m_shape), operands, specs, scratch, "experts", cost
            )
            state = call(
                combine_kernel,
                jax.ShapeDtypeStruct((own, width), BF16),
                (swapped(half_out), middle),
                [whole()] * 2,
                [],
                "combine",
                (rows * width, 4 * rows * width),
            )
        else:
            *pieces, middle = call(
                functools.partial(sending_kernel, step, low),
                (slots,) * low + (m_shape,),
                operands,
                specs,
                scratch + [pltpu.VMEM((devices, own, width), BF16)],
                "experts_sending",
                cost,
            )
            pieces = [pieces[0]] + [shifted(pieces[l], l) for l in range(low - 1, 0, -1)]
            part_sums = call(
                partial_kernel, slots, (middle, *pieces), [whole()] * (low + 1), [], "partial",
                (rows * width, 4 * rows * width),
            )
            parts = [shifted(part_sums, h * low, 1) for h in range(high)]
            state = call(
                join_kernel, slots, tuple(parts), [whole()] * high, [], "join", (rows * width, 4 * rows * width), 0
            )
    return state[None]


def solution(mesh):
    return jax.shard_map(
        body,
        mesh=mesh,
        in_specs=(
            P("section", "expert", None),
            P("section", None),
            P("section", None, "expert"),
            P("section", None, "expert"),
            P("section", None, "expert", None, None, None),
            P("section", None, "expert", None, None, None),
            P("section", None, "expert"),
            P("section", None),
            P("section", "expert", None, None),
            P("section", "expert", None, None),
            P("section", "expert", None, None),
            P("section", None, "expert", None),
            P("section", None, "expert", None),
        ),
        out_specs=P("section", "expert", None),
        check_vma=False,
    )
```

```python
import functools
import math

import jax
import jax.numpy as jnp
import numpy as np
from jax import lax
from jax.experimental import pallas as pl
from jax.experimental.pallas import tpu as pltpu
from jax.sharding import PartitionSpec as P

STEPS = 3
EPS = 1e-06
LIMIT = 24 * 1024 * 1024
EXCHANGE = 20 * 1000 * 1000 * 1000
LANES = 128
EXTRA = 16
LOG2E = math.log2(math.e)
F32 = jnp.float32
BF16 = jnp.bfloat16


def shifted(array, mask, sections=0):
    stages, devices = lax.axis_size("section"), lax.axis_size("expert")
    pairs = [
        (s * devices + e, (s + sections) % stages * devices + (e ^ mask))
        for s in range(stages)
        for e in range(devices)
    ]
    return lax.ppermute(array, ("section", "expert"), pairs)


def split(devices):
    low = 1
    while low * low < devices:
        low *= 2
    return low, devices // low


def swapped(blocks):
    return lax.all_to_all(blocks, "expert", split_axis=0, concat_axis=0, tiled=True)


def whole(memory_space=pltpu.VMEM):
    return pl.BlockSpec(memory_space=memory_space)


def call(kernel, out, operands, specs, scratch, name, cost, exchange=EXCHANGE):
    single = not isinstance(out, tuple)
    return pl.pallas_call(
        kernel,
        out_shape=out,
        in_specs=specs,
        out_specs=whole() if single else tuple(whole() for _ in out),
        scratch_shapes=scratch,
        compiler_params=pltpu.CompilerParams(vmem_limit_bytes=LIMIT),
        cost_estimate=pl.CostEstimate(flops=cost[0] + exchange, bytes_accessed=cost[1], transcendentals=0),
        name=name,
    )(*operands)


def add_tiles(totals, left, right, depth, tile=128):
    for at in range(0, right.shape[1], tile):
        part = jnp.dot(left, right[depth, at:at + tile], preferred_element_type=F32)
        totals[at] = totals[at] + part if at in totals else part


def add_squares(totals, values):
    for at in range(0, values.shape[1], 128):
        totals = totals + values[:, at:at + 128] * values[:, at:at + 128]
    return totals


def spread_kernel(x_ref, o_ref):
    for i in range(o_ref.shape[0]):
        o_ref[i] = x_ref[...]


def coded_shares(routes_ref, gates_ref, experts):
    own = routes_ref.shape[2]
    lane = lax.broadcasted_iota(jnp.int32, (EXTRA, LANES), 1)
    row = lax.broadcasted_iota(jnp.int32, (EXTRA, LANES), 0)
    line = lax.broadcasted_iota(jnp.int32, (EXTRA, own), 0)
    column = lax.broadcasted_iota(jnp.int32, (EXTRA, own), 1)
    here = (line == column) | (line == column + own) | (line == column + 2 * own)
    shares = jnp.zeros((EXTRA, LANES), F32)
    for step in range(STEPS):
        routes, gates = routes_ref[step], gates_ref[step]
        parts = gates / jnp.sum(gates, axis=0, keepdims=True)
        for e in range(experts):
            share = jnp.sum(jnp.where(routes == e, parts, 0.0), axis=0, keepdims=True)
            share = jnp.sum(jnp.where(here, share, 0.0), axis=1, keepdims=True)
            shares = jnp.where(lane == step * experts + e, share, shares)
    first = shares.astype(BF16).astype(F32)
    second = (shares - first).astype(BF16).astype(F32)
    return jnp.where(row < own, first, jnp.where(row < 2 * own, second, shares - first - second)).astype(BF16)


def first_kernel(head_dim, x_ref, gain_ref, w_ref, routes_ref, gates_ref, q_ref, states, spread):
    query_kernel(head_dim, x_ref, gain_ref, w_ref, None, states, spread)
    devices = q_ref.shape[0]
    count = spread.shape[0] // devices
    coded = coded_shares(routes_ref, gates_ref, devices // 2)
    for i in range(devices):
        q_ref[i, :EXTRA, :] = coded
        q_ref[i, EXTRA:, :] = spread[count * i:count * (i + 1), :].astype(BF16)


def order_kernel(head_dim, low, me_ref, *refs):
    pieces, (gain_ref, w_ref, q_ref, states, x_ref, spread) = refs[:low], refs[low:]
    me = me_ref[0]
    for l, piece in enumerate(pieces):
        for h in range(piece.shape[0]):
            x_ref[me ^ (l + h * low)] = piece[h]
    query_kernel(head_dim, x_ref, gain_ref, w_ref, q_ref, states, spread)


def head_queries(head_dim, x_ref, gain_ref, w_ref, states):
    devices, own, _ = x_ref.shape
    rows, (width, columns) = devices * own, w_ref.shape
    chunk = 512
    totals, squares = {}, jnp.zeros((rows, 128), F32)
    for start in range(0, width, chunk):
        at = slice(start, start + chunk)
        for i in range(devices):
            states[own * i:own * (i + 1), at] = x_ref[i, :, at].astype(F32)
        values = states[:, at]
        squares = add_squares(squares, values)
        add_tiles(totals, (values * gain_ref[:, at].astype(F32)).astype(BF16), w_ref, at, head_dim)
    scale = lax.rsqrt(jnp.sum(squares, axis=-1, keepdims=True) / width + EPS)
    queries = []
    for h in range(columns // head_dim):
        one = totals[head_dim * h] * scale
        queries.append(one * lax.rsqrt(jnp.mean(one * one, axis=-1, keepdims=True) + EPS))
    return queries


def query_kernel(head_dim, x_ref, gain_ref, w_ref, q_ref, states, spread):
    queries = head_queries(head_dim, x_ref, gain_ref, w_ref, states)
    for h, one in enumerate(queries):
        spread[pl.ds(h, one.shape[0], stride=len(queries)), :] = one
    if q_ref is not None:
        q_ref[...] = spread[...].astype(BF16)


def halves_kernel(head_dim, low, me_ref, *refs):
    pieces, refs = refs[:low], refs[low:]
    (gain_ref, w_ref), outs, (states, x_ref, spread) = refs[:2], refs[2:2 + low], refs[2 + low:]
    me = me_ref[0]
    for l, piece in enumerate(pieces):
        for h in range(piece.shape[0]):
            x_ref[me ^ (l + h * low)] = piece[h]
    devices, own, _ = x_ref.shape
    for h, one in enumerate(head_queries(head_dim, x_ref, gain_ref, w_ref, states)):
        for i in range(devices):
            spread[i, own * h:own * (h + 1), :] = one[own * i:own * (i + 1), :]
    for l, out in enumerate(outs):
        for g in range(out.shape[0]):
            out[g] = spread[(me % low ^ l) + g * low].astype(BF16)


def cache_kernel(own, kv_heads, me_ref, len_ref, k_ref, v_ref, *refs):
    *blocks, wide = refs
    half = kv_heads // 2
    first = jnp.where(me_ref[0] >= kv_heads, 0, half)
    span = k_ref.shape[1] // kv_heads
    cache = span // own
    line = lax.broadcasted_iota(jnp.int32, (EXTRA, LANES), 0)
    place = lax.broadcasted_iota(jnp.int32, (EXTRA, LANES), 1) + line * LANES
    for step, block in enumerate(blocks, 1):
        at = 0
        for ref in (k_ref, v_ref):
            wide[...] = ref[step].astype(F32)
            for j in range(half):
                block[at:at + span, :] = wide[pl.ds(first + j, span, stride=kv_heads), :].astype(BF16)
                at += span
        valid = jnp.zeros((EXTRA, LANES), F32)
        for r in range(own):
            inside = (place >= r * cache) & (place < r * cache + len_ref[step, :, r:r + 1])
            valid = jnp.where(inside, 1.0, valid)
        block[at:, :] = valid.astype(BF16)


def softmax_times(scores, valid, head_dim, values):
    exps = jnp.where(valid, jnp.exp2(scores * (head_dim ** (-0.5) * LOG2E)), 0.0)
    context = jnp.dot(exps.astype(BF16), values, preferred_element_type=F32)
    return context * (1.0 / jnp.sum(exps, axis=-1, keepdims=True))


def products(queries, keys):
    return lax.dot_general(queries, keys, (((1,), (1,)), ((), ())), preferred_element_type=F32)


def half_attention_kernel(step, own, kv_heads, me_ref, *refs):
    low = len(refs) - 6
    pieces, (k_ref, v_ref, len_ref, pair_ref, c_ref, q_ref) = refs[:low], refs[low:]
    me = me_ref[0]
    mine = jnp.where(me >= low, 1, 0)
    half = kv_heads // 2
    count, head_dim = pieces[0].shape[1:]
    for l, piece in enumerate(pieces):
        for g in range(2):
            q_ref[g, me % low ^ (low - l) % low] = piece[g]
    rows = low * count
    span = k_ref.shape[1] // kv_heads
    cache = span // own
    q = q_ref[mine].reshape(rows, head_dim)
    line = lax.broadcasted_iota(jnp.int32, (rows, 1), 0)
    place = lax.broadcasted_iota(jnp.int32, (1, span * kv_heads), 1)
    of_row = place // (cache * kv_heads)
    length = jnp.zeros(place.shape, jnp.int32)
    for r in range(own):
        length = jnp.where(of_row == r, len_ref[step, :, r:r + 1], length)
    key_of = jnp.where(place // kv_heads % cache < length, of_row * kv_heads + place % kv_heads, -1)
    key_for = line % own * kv_heads + line // (rows // half) + half * mine
    scores = products(q, k_ref[step])
    other = q_ref[1 - mine].reshape(rows, head_dim)
    part = rows // half
    ends = pair_ref[2 * half * span:, :].astype(F32)
    valid = jnp.concatenate([ends[g:g + 1, :] for g in range(span // LANES)], axis=1) > 0.0
    line = lax.broadcasted_iota(jnp.int32, (part, 1), 0)
    place = lax.broadcasted_iota(jnp.int32, (1, span), 1)
    theirs = (line % own == place // cache) & valid
    others = [products(other[part * j:part * (j + 1), :], pair_ref[span * j:span * (j + 1), :]) for j in range(half)]
    own_context = softmax_times(scores, key_of == key_for, head_dim, v_ref[step])
    contexts = [
        softmax_times(others[j], theirs, head_dim, pair_ref[span * (half + j):span * (half + j + 1), :])
        for j in range(half)
    ]
    heads = part // own
    for h in range(rows // own):
        at = slice(head_dim * h, head_dim * (h + 1))
        j, inside = h // heads, h % heads
        one = own_context[own * h:own * (h + 1), :].astype(BF16)
        two = contexts[j][own * inside:own * (inside + 1), :].astype(BF16)
        for i in range(c_ref.shape[0]):
            c_ref[i, mine, :, at] = one
            c_ref[i, 1 - mine, :, at] = two


def first_attention_kernel(own, pick_ref, q_ref, *refs):
    *rest, c_ref, share_ref, lines = refs
    share_ref[...] = jnp.dot(pick_ref[...], q_ref[...], preferred_element_type=F32)
    attention_kernel(0, own, q_ref, *rest, c_ref, lines)


def attention_kernel(step, own, q_ref, k_ref, v_ref, len_ref, order_ref, line_ref, column_ref, c_ref, lines):
    head_dim = q_ref.shape[1]
    heads = line_ref.shape[0]
    span = column_ref.shape[1]
    q = jnp.dot(order_ref[...], q_ref[...], preferred_element_type=F32).astype(BF16)
    group_of, position = column_ref[0:1, :], column_ref[1:2, :]
    same = group_of == line_ref[...]
    ours = [slice(heads * r, heads * (r + 1)) for r in range(own)]
    keys = [slice(span * r, span * (r + 1)) for r in range(own)]
    scores = [
        lax.dot_general(
            q[ours[r], :], k_ref[step, keys[r], :], (((1,), (1,)), ((), ())), preferred_element_type=F32
        )
        for r in range(own)
    ]
    exps = [
        jnp.where(
            same & (position < len_ref[step, :, r:r + 1]), jnp.exp2(scores[r] * (head_dim ** (-0.5) * LOG2E)), 0.0
        )
        for r in range(own)
    ]
    contexts = [
        jnp.dot(exps[r].astype(BF16), v_ref[step, keys[r], :], preferred_element_type=F32) for r in range(own)
    ]
    for r in range(own):
        lines[ours[r], :] = contexts[r] * (1.0 / jnp.sum(exps[r], axis=-1, keepdims=True))
    for h in range(heads):
        piece = lines[pl.ds(h, own, stride=heads), :].astype(BF16)
        for i in range(c_ref.shape[0]):
            c_ref[i, :, head_dim * h:head_dim * (h + 1)] = piece


def attention_tables(own, heads, local_heads, kv_heads, cache_len):
    group = heads // kv_heads
    row, head = np.divmod(np.arange(own * heads), heads)
    sender, place = head // local_heads, row * local_heads + head % local_heads
    devices, count = heads // local_heads, own * local_heads
    order = np.zeros((own * heads, own * heads), np.float32)
    order[np.arange(own * heads), sender * count + place] = 1.0
    first_order = np.zeros((own * heads, devices * (EXTRA + count)), np.float32)
    first_order[np.arange(own * heads), sender * (EXTRA + count) + EXTRA + place] = 1.0
    pick = np.zeros((devices * own, devices * (EXTRA + count)), np.float32)
    for part in range(3):
        for r in range(own):
            pick[np.arange(devices) * own + r, np.arange(devices) * (EXTRA + count) + part * own + r] = 1.0
    line = (np.arange(heads) // group).astype(np.int32)[:, None]
    position, kv = np.divmod(np.arange(cache_len * kv_heads), kv_heads)
    column = np.zeros((8, cache_len * kv_heads), np.int32)
    column[:2] = kv, position
    asis = jnp.asarray(line), jnp.asarray(column)
    return (jnp.asarray(order, BF16), *asis), (jnp.asarray(first_order, BF16), *asis), jnp.asarray(pick, BF16)


def out_kernel(c_ref, w_ref, o_ref, lines):
    devices, own, width = c_ref.shape
    chunk, totals = 512, {}
    for start in range(0, width, chunk):
        at = slice(start, start + chunk)
        for i in range(devices):
            lines[own * i:own * (i + 1), at] = c_ref[i, :, at].astype(F32)
        add_tiles(totals, lines[:, at].astype(BF16), w_ref, at)
    for at, total in totals.items():
        columns = total.astype(BF16)
        for i in range(devices):
            o_ref[i, :, at:at + columns.shape[1]] = columns


def half_out_kernel(c_ref, w_ref, o_ref, lines):
    devices, slots, own, part = c_ref.shape
    low = devices // slots
    chunk, totals = 512, {}
    for start in range(0, slots * part, chunk):
        at = slice(start, start + chunk)
        half, inside = start // part, slice(start % part, start % part + chunk)
        for i in range(devices):
            lines[own * i:own * (i + 1), at] = c_ref[half * low + i % low, i // low, :, inside].astype(F32)
        add_tiles(totals, lines[:, at].astype(BF16), w_ref, at)
    for at, total in totals.items():
        columns = total.astype(BF16)
        for i in range(devices):
            o_ref[i, :, at:at + columns.shape[1]] = columns


def expert_kernel(step, me_ref, a_ref, x_ref, gain_ref, gate_ref, up_ref, down_ref, share_ref, h_ref, m_ref, middle):
    devices, own, _ = h_ref.shape
    part = a_ref.shape[2]
    width = part * devices
    me = me_ref[0]
    gates, ups, squares = {}, {}, jnp.zeros((devices * own, 128), F32)
    for j in range(devices):
        at = slice(part * j, part * (j + 1))
        values = x_ref[:, at] + a_ref[j].astype(F32)
        middle[:, at] = values
        squares = add_squares(squares, values)
        left = (values * gain_ref[:, at].astype(F32)).astype(BF16)
        add_tiles(gates, left, gate_ref, at)
        add_tiles(ups, left, up_ref, at)
    scale = lax.rsqrt(jnp.sum(squares, axis=-1, keepdims=True) / width + EPS)
    lane = lax.broadcasted_iota(jnp.int32, share_ref.shape, 1)
    mine = lane == step * (devices // 2) + me // 2
    share = jnp.sum(jnp.where(mine, share_ref[...], 0.0), axis=1, keepdims=True)
    active = {}
    for at in gates:
        gate, up = gates[at] * scale, ups[at] * scale
        active[at] = (gate / (1.0 + jnp.exp(-gate)) * up * share).astype(BF16)
    chunk = 512
    for start in range(0, width, chunk):
        piece = None
        for at, left in active.items():
            term = jnp.dot(
                left, down_ref[at:at + left.shape[1], start:start + chunk], preferred_element_type=F32
            )
            piece = term if piece is None else piece + term
        for i in range(devices):
            h_ref[i, :, start:start + chunk] = piece[own * i:own * (i + 1), :].astype(BF16)
    pairs = 8 // own
    block = middle[pl.ds(pl.multiple_of((me // pairs) * 8, 8), 8), :]
    kept = block[0:own, :]
    for p in range(1, pairs):
        kept = jnp.where(me % pairs == p, block[own * p:own * (p + 1), :], kept)
    m_ref[...] = kept


def sending_kernel(step, low, me_ref, *refs):
    pieces, (m_ref, middle, rows) = refs[7:7 + low], refs[7 + low:]
    expert_kernel(step, me_ref, *refs[:7], rows, m_ref, middle)
    me = me_ref[0]
    for l, piece in enumerate(pieces):
        for h in range(piece.shape[0]):
            piece[h] = rows[me ^ (l + h * low)]


def partial_kernel(m_ref, *refs):
    pieces, t_ref = refs[:-1], refs[-1]
    for h in range(t_ref.shape[0]):
        total = m_ref[...] if h == 0 else jnp.zeros(m_ref.shape, F32)
        for piece in pieces:
            total = total + piece[h].astype(F32)
        t_ref[h] = total.astype(BF16)


def join_kernel(*refs):
    parts, x_ref = refs[:-1], refs[-1]
    for g in range(len(parts)):
        total = parts[0][g].astype(F32)
        for h in range(1, len(parts)):
            total = total + parts[h][h ^ g].astype(F32)
        x_ref[g] = total.astype(BF16)


def combine_kernel(r_ref, m_ref, o_ref):
    total = m_ref[...]
    for i in range(r_ref.shape[0]):
        total = total + r_ref[i].astype(F32)
    o_ref[...] = total.astype(BF16)


def body(
    hidden_in,
    attn_gain,
    w_query,
    w_out,
    key_cache,
    value_cache,
    lengths,
    ffn_gain,
    w_gate,
    w_up,
    w_down,
    routes,
    gates,
):
    devices = lax.axis_size("expert")
    me = lax.axis_index("expert").astype(jnp.int32).reshape(1)
    own, width = hidden_in.shape[1:]
    rows = own * devices
    cache_len, kv_heads, head_dim = key_cache.shape[3:]
    query_w, out_w = w_query[0], w_out[0]
    part = query_w.shape[1]
    local_heads = part // head_dim
    heads = local_heads * devices
    gate_w, up_w, down_w = w_gate[0, 0], w_up[0, 0], w_down[0, 0]
    hidden = gate_w.shape[1]
    places = own * cache_len * kv_heads
    keys = key_cache.reshape(STEPS, places, head_dim)
    values = value_cache.reshape(STEPS, places, head_dim)
    routes, gates = routes[0].transpose(0, 2, 1), gates[0].transpose(0, 2, 1)
    lengths = lengths.reshape(STEPS, 1, own)
    tables, first_tables, pick = attention_tables(own, heads, local_heads, kv_heads, cache_len)
    low, high = split(devices)
    by_half = high == 2 and devices == 2 * kv_heads
    smem = whole(pltpu.SMEM)
    q_shape = jax.ShapeDtypeStruct((rows * local_heads, head_dim), BF16)
    x_shape = jax.ShapeDtypeStruct((devices, own, width), BF16)
    states_shape = jax.ShapeDtypeStruct((rows, width), F32)
    m_shape = jax.ShapeDtypeStruct((own, width), F32)
    slots = jax.ShapeDtypeStruct((high, own, width), BF16)
    copies = call(
        spread_kernel,
        x_shape,
        (hidden_in[0],),
        [whole()],
        [],
        "spread",
        (0, 2 * rows * width),
    )
    me, copies = lax.optimization_barrier((me, copies))
    if by_half:
        block = jax.ShapeDtypeStruct((2 * places // 2 + EXTRA, head_dim), BF16)
        others = call(
            functools.partial(cache_kernel, own, kv_heads),
            (block,) * (STEPS - 1),
            (me, lengths, keys, values),
            [smem] + [whole()] * 3,
            [pltpu.VMEM((places, head_dim), F32)],
            "caches_of_other_half",
            (places * head_dim, 8 * places * head_dim),
            0,
        )
        others = [shifted(one, low) for one in others]
    for step in range(STEPS):
        spread = pltpu.VMEM((rows * local_heads, head_dim), F32)
        cost = (2 * rows * width * part, 2 * width * part)
        if step == 0:
            own_q, states = call(
                functools.partial(first_kernel, head_dim),
                (jax.ShapeDtypeStruct((devices, EXTRA + own * local_heads, head_dim), BF16), states_shape),
                (swapped(copies), attn_gain, query_w, routes, gates),
                [whole()] * 5,
                [spread],
                "first_query",
                cost,
            )
        else:
            pieces = [state] + [shifted(state, l) for l in range(1, low)]
            if by_half:
                *queries, states = call(
                    functools.partial(halves_kernel, head_dim, low),
                    (jax.ShapeDtypeStruct((2, own * local_heads, head_dim), BF16),) * low + (states_shape,),
                    (me, *pieces, attn_gain, query_w),
                    [smem] + [whole()] * (low + 2),
                    [pltpu.VMEM((devices, own, width), BF16), pltpu.VMEM((devices, own * local_heads, head_dim), F32)],
                    "queries_by_half",
                    cost,
                    0,
                )
                queries = [queries[0]] + [shifted(queries[l], l) for l in range(low - 1, 0, -1)]
            else:
                own_q, states = call(
                    functools.partial(order_kernel, head_dim, low),
                    (q_shape, states_shape),
                    (me, *pieces, attn_gain, query_w),
                    [smem] + [whole()] * (low + 2),
                    [pltpu.VMEM((devices, own, width), BF16), spread],
                    "order_query",
                    cost,
                )
        if step and by_half:
            context = call(
                functools.partial(half_attention_kernel, step, own, kv_heads),
                jax.ShapeDtypeStruct((devices, 2, own, heads * head_dim // 2), BF16),
                (me, *queries, keys, values, lengths, others[step - 1]),
                [smem] + [whole()] * (low + 4),
                [pltpu.VMEM((2, low, own * local_heads, head_dim), BF16)],
                "half_attention",
                cost,
            )
        else:
            c_shape = jax.ShapeDtypeStruct((devices, own, heads * head_dim), BF16)
            by_row = [pltpu.VMEM((own * heads, head_dim), F32)]
            cost = (4 * own * heads * places * head_dim, 4 * places * head_dim)
            queries = swapped(own_q.reshape(devices, -1, head_dim)).reshape(-1, head_dim)
            if step == 0:
                context, shares = call(
                    functools.partial(first_attention_kernel, own),
                    (c_shape, jax.ShapeDtypeStruct((rows, LANES), F32)),
                    (pick, queries, keys, values, lengths, *first_tables),
                    [whole()] * 8,
                    by_row,
                    "first_attention",
                    cost,
                )
            else:
                context = call(
                    functools.partial(attention_kernel, step, own),
                    c_shape,
                    (queries, keys, values, lengths, *tables),
                    [whole()] * 7,
                    by_row,
                    "attention",
                    cost,
                )
        contexts = swapped(context)
        columns = call(
            half_out_kernel if step and by_half else out_kernel,
            jax.ShapeDtypeStruct((devices, rows, part), BF16),
            (contexts, out_w),
            [whole()] * 2,
            [pltpu.VMEM((rows, heads * head_dim), F32)],
            "attention_out",
            (2 * rows * width * part, 2 * width * part),
        )
        attended = swapped(columns)
        operands = (me, attended, states, ffn_gain, gate_w, up_w, down_w, shares)
        specs = [smem] + [whole()] * 7
        scratch = [pltpu.VMEM((rows, width), F32)]
        cost = (6 * rows * width * hidden, 6 * width * hidden)
        if step + 1 == STEPS:
            half_out, middle = call(
                functools.partial(expert_kernel, step), (x_shape, m_shape), operands, specs, scratch, "experts", cost
            )
            state = call(
                combine_kernel,
                jax.ShapeDtypeStruct((own, width), BF16),
                (swapped(half_out), middle),
                [whole()] * 2,
                [],
                "combine",
                (rows * width, 4 * rows * width),
            )
        else:
            *pieces, middle = call(
                functools.partial(sending_kernel, step, low),
                (slots,) * low + (m_shape,),
                operands,
                specs,
                scratch + [pltpu.VMEM((devices, own, width), BF16)],
                "experts_sending",
                cost,
            )
            pieces = [pieces[0]] + [shifted(pieces[l], l) for l in range(low - 1, 0, -1)]
            part_sums = call(
                partial_kernel, slots, (middle, *pieces), [whole()] * (low + 1), [], "partial",
                (rows * width, 4 * rows * width),
            )
            parts = [shifted(part_sums, h * low, 1) for h in range(high)]
            state = call(
                join_kernel, slots, tuple(parts), [whole()] * high, [], "join", (rows * width, 4 * rows * width), 0
            )
    return state[None]


def solution(mesh):
    return jax.shard_map(
        body,
        mesh=mesh,
        in_specs=(
            P("section", "expert", None),
            P("section", None),
            P("section", None, "expert"),
            P("section", None, "expert"),
            P("section", None, "expert", None, None, None),
            P("section", None, "expert", None, None, None),
            P("section", None, "expert"),
            P("section", None),
            P("section", "expert", None, None),
            P("section", "expert", None, None),
            P("section", "expert", None, None),
            P("section", None, "expert", None),
            P("section", None, "expert", None),
        ),
        out_specs=P("section", "expert", None),
        check_vma=False,
    )
```
